256 devices in a mesh: tm: 32 (over x, z_lo, core), space: 8 (over z_hi, y).
Axes of the slice: x: 4, y: 4, z: 8 (z_hi: 2, z_lo: 4; z = z_hi * 4 + z_lo), core: 2. Of those that a mesh axis runs over, the one named last changes fastest.
Arguments:
- slice_starts: float32 [32, 3, 128, 32, 128], P('tm', None, 'space'), may hold values from -6 to 6
- coriolis: float32 [32], replicated, may hold values from 0.05 to 0.2
- stratification: float32 [128, 32, 128], P('space'), may hold values from 0.25 to 1
- inverse_blocks: float32 [3, 128, 128], replicated, may hold values from 0 to 0.51153846
Outputs:
- new_starts: float32 [32, 3, 128, 32, 128], P('tm', None, 'space')
The draws below stay inside these ranges and needn't reach their ends.
All inputs are finite; a program needn't handle non-finite values.
Results may differ from the reference program's by a relative error of at most 0.00011.
Values sent between devices are 32-bit elements; how exact they have to be, the bound alone decides.
No kernel may reach another device: no remote copies, remote signals or barrier semaphores. Data moves between devices by JAX's collectives and lax.ppermute only.
A program may use at most 64 MiB of HBM per device.

```python
import math
import jax
import jax.numpy as jnp
from jax import lax

NY = 32
NZ = 128
STEPS = 8
SLICES = 32
NX = 128


def draw_inverse_blocks(key, part):
    key = jax.random.fold_in(key, 7)
    levels = jnp.arange(NZ, dtype=jnp.float32)
    distance = jnp.abs(levels[:, None] - levels[None, :])
    reach = NZ / 4.0
    spread_part = jnp.exp(-distance / reach) * (0.6 / (2.0 * reach + 1.0))
    identity_part = jnp.where(distance < 0.5, 0.4, 0.0)
    base = identity_part + spread_part
    factor = jax.random.uniform(key, (3, NZ, NZ), jnp.float32, 0.85, 1.15)
    return (base[None] * factor).astype(jnp.float32)


def steps_of(own_key, shape, pieces, low, largest):
    factor_of, own = 1.0, jax.random.fold_in(own_key, 6)
    for dim, shards_of in pieces:
        steps = jnp.exp(jax.random.uniform(jax.random.fold_in(own, dim), (shards_of,), jnp.float32, low / len(pieces), largest / len(pieces)))
        factor_of = factor_of * jnp.repeat(steps, shape[dim] // shards_of).reshape([-1 if axis == dim else 1 for axis in range(len(shape))])
    return factor_of


def gaussian(stream_key, extent, deviation, bound, pieces=(), kind=jnp.bfloat16):
    factor_of = steps_of(stream_key, extent, pieces, -0.22, 0.18) if pieces else 1.0
    result = jax.random.normal(stream_key, extent, jnp.float32) * deviation * factor_of
    return jnp.minimum(jnp.maximum(result, -bound), bound).astype(kind)


def setup_inputs(seed: int = 0) -> dict:
    streams_of = jax.random.split(jax.random.key(seed), 5)
    slice_starts = gaussian(streams_of[0], (SLICES, 3, NX, NY, NZ), 1.0, 6.0, ((0, 32), (2, 8)), jnp.float32)
    coriolis = jnp.clip(jnp.exp(jax.random.uniform(streams_of[1], (NY,), jnp.float32, math.log(0.05), math.log(0.2))), 0.05, 0.2)
    stratification = jnp.clip(jnp.exp(math.log(1.0) - 1.3862944 * jax.random.uniform(streams_of[2], (NX, NY, NZ), jnp.float32) ** steps_of(streams_of[2], (NX, NY, NZ), ((0, 8),), -0.2, 0.2)), 0.25, 1.0)
    inverse_blocks = draw_inverse_blocks(jax.random.fold_in(streams_of[4], 71), 0)
    return dict(slice_starts=slice_starts, coriolis=coriolis, stratification=stratification, inverse_blocks=inverse_blocks)


TIME_STEP = 0.5
VISCOSITY = 0.1
DIFFUSIVITY = 0.3
COARSE_STEP = 4.0
COARSE_SPACING = 4.0


def along_x(field):
    return (field[2:] - field[:-2]) * 0.5


def along_y(field):
    return (jnp.roll(field, -1, axis=1) - jnp.roll(field, 1, axis=1)) * 0.5


def lateral_laplacian(field):
    middle = field[1:-1]
    return field[2:] + field[:-2] + jnp.roll(middle, -1, axis=1) + jnp.roll(middle, 1, axis=1) - 4.0 * middle


def vertical_second(field):
    padded = jnp.concatenate([field[..., :1], field, field[..., -1:]], axis=-1)
    return padded[..., 2:] + padded[..., :-2] - 2.0 * field


def fine_core(padded, coriolis, stratification):
    zonal, meridional, buoyancy = padded[0], padded[1], padded[2]
    spin = coriolis[None, :, None]
    zonal_mid = zonal[1:-1]
    meridional_mid = meridional[1:-1]
    zonal_new = zonal_mid + TIME_STEP * (spin * meridional_mid - along_x(buoyancy) + VISCOSITY * lateral_laplacian(zonal) + DIFFUSIVITY * vertical_second(zonal_mid))
    meridional_new = meridional_mid + TIME_STEP * (-spin * zonal_new - along_y(buoyancy[1:-1]) + VISCOSITY * lateral_laplacian(meridional) + DIFFUSIVITY * vertical_second(meridional_mid))
    buoyancy_mid = buoyancy[2:-2]
    buoyancy_new = buoyancy_mid + TIME_STEP * (-stratification * (along_x(zonal_new) + along_y(meridional_new[1:-1])) + VISCOSITY * lateral_laplacian(buoyancy[1:-1]) + DIFFUSIVITY * vertical_second(buoyancy_mid))
    return jnp.stack([zonal_new[1:-1], meridional_new[1:-1], buoyancy_new])


def coarse_core(padded, spin_coarse, strat_coarse, inverse_blocks):
    zonal, meridional, buoyancy = padded[0], padded[1], padded[2]
    spin = spin_coarse[None, :, None]
    ratio = COARSE_STEP / COARSE_SPACING
    zonal_half = zonal[1:-1] + COARSE_STEP * spin * meridional[1:-1] - ratio * along_x(buoyancy)
    meridional_half = meridional[1:-1] - COARSE_STEP * spin * zonal_half - ratio * along_y(buoyancy[1:-1])
    buoyancy_half = buoyancy[2:-2] - ratio * strat_coarse * (along_x(zonal_half) + along_y(meridional_half[1:-1]))
    explicit = jnp.stack([zonal_half[1:-1], meridional_half[1:-1], buoyancy_half])
    return jnp.einsum("kxyj,kij->kxyi", explicit, inverse_blocks, precision=lax.Precision.HIGHEST)


def restrict(state):
    kinds, across, along, levels = state.shape
    return state.reshape(kinds, across // 4, 4, along // 4, 4, levels).mean(axis=(2, 4))


def prolong(state):
    kinds, across, along, levels = state.shape
    expanded = jnp.broadcast_to(state[:, :, None, :, None, :], (kinds, across, 4, along, 4, levels))
    return expanded.reshape(kinds, across * 4, along * 4, levels)


def wrap_pad(state):
    return jnp.concatenate([state[:, -2:], state, state[:, :2]], axis=1)


def reference(slice_starts, coriolis, stratification, inverse_blocks):
    spin_coarse = coriolis.reshape(-1, 4).mean(axis=1)
    strat_coarse = restrict(stratification[None])[0]

    def coarse_map(state):
        return coarse_core(wrap_pad(state), spin_coarse, strat_coarse, inverse_blocks)

    def increment(start):
        fine = start
        for step in range(STEPS):
            fine = fine_core(wrap_pad(fine), coriolis, stratification)
        return fine - prolong(coarse_map(restrict(start)))

    increments = lax.map(increment, slice_starts)

    def chain(coarse, delta):
        image = coarse_map(coarse)
        ends = prolong(image) + delta
        return image + restrict(delta), ends

    final_coarse, ends = lax.scan(chain, restrict(slice_starts[0]), increments)
    return jnp.roll(ends, 1, axis=0)
```

```python
import jax
import jax.numpy as jnp
from jax import lax
from jax.experimental import pallas as pl
from jax.experimental.pallas import tpu as pltpu
from jax.sharding import Mesh
from jax.sharding import PartitionSpec as P

AXES = ("x", "zl", "c", "zh", "y")
SIZES = (4, 4, 2, 2, 4)
TM = ("x", "zl", "c")
SPACE = ("zh", "y")
PLANE = ("zl", "zh", "y")

VMEM = pl.BlockSpec(memory_space=pltpu.VMEM)
SMEM = pl.BlockSpec(memory_space=pltpu.SMEM)
PARAMS = pltpu.CompilerParams(vmem_limit_bytes=40 * 1024 * 1024)

HALO = 8
WIDE = 16 + 2 * HALO


def ring(size, by):
    return [(i, (i + by) % size) for i in range(size)]


def y_next(q):
    return pltpu.roll(q, q.shape[0] - 1, 0)


def y_prev(q):
    return pltpu.roll(q, 1, 0)


def fine_steps(bufs, strat, half_spin, lane_weight):
    def spread(q):
        diff = (pltpu.roll(q, 127, 1) - q) * lane_weight
        return diff - pltpu.roll(diff, 1, 1)

    for step in range(4):
        src, dst = bufs[step % 2], bufs[(step + 1) % 2]
        reach = 2 * (3 - step)
        first = HALO - reach
        count = 16 + 2 * reach

        def zonal(x, src=src):
            u = src[0, x]
            sides = src[0, x + 1] + src[0, x - 1] + (y_next(u) + y_prev(u))
            push = src[2, x + 1] - src[2, x - 1]
            return (
                (0.8 * u + spread(u))
                + (half_spin[...] * src[1, x] - 0.25 * push)
                + 0.05 * sides
            )

        def chunk(i, carry, src=src, dst=dst, first=first, zonal=zonal):
            before, here = carry
            for k in range(4):
                x = first + 4 * i + k
                after = zonal(x + 1)
                dst[0, x] = here
                v = src[1, x]
                b = src[2, x]
                b_next, b_prev = y_next(b), y_prev(b)
                v_new = (
                    (0.8 * v + spread(v))
                    - (half_spin[...] * here + 0.25 * (b_next - b_prev))
                    + 0.05 * (src[1, x + 1] + src[1, x - 1] + (y_next(v) + y_prev(v)))
                )
                dst[1, x] = v_new
                flow = (after - before) + (y_next(v_new) - y_prev(v_new))
                dst[2, x] = (
                    (0.8 * b + spread(b))
                    - strat[x] * flow
                    + 0.05 * (src[2, x + 1] + src[2, x - 1] + (b_next + b_prev))
                )
                before, here = here, after
            return before, here

        lax.fori_loop(0, count // 4, chunk, (zonal(first - 1), zonal(first)))


def lane_weights():
    lane = lax.broadcasted_iota(jnp.int32, (32, 128), 1)
    return jnp.where(lane < 127, 0.15, 0.0).astype(jnp.float32)


def fill_strat(strat, left, own, right):
    for x in range(6):
        strat[HALO - 6 + x] = 0.25 * left[x]
        strat[HALO + 16 + x] = 0.25 * right[x]
    for x in range(16):
        strat[HALO + x] = 0.25 * own[x]


def first_half_kernel(spin, left, start, right, own_strat, low, high, one, two, strat):
    for k in range(3):
        for x in range(8):
            one[k, x] = left[8 * k + x]
            one[k, 24 + x] = right[8 * k + x]
        for x in range(16):
            one[k, 8 + x] = start[k, x]
    fill_strat(strat, left.at[pl.ds(24, 6)], own_strat, right.at[pl.ds(24, 6)])
    fine_steps((one, two), strat, spin, lane_weights())
    for k in range(3):
        for x in range(8):
            low[k, x] = one[k, 8 + x]
            high[k, x] = one[k, 16 + x]


def second_half_kernel(
    spin, left, low, high, right, left_first, right_first, own_strat, next_mean, strat_tile,
    detail, payload, one, two, strat, rows,
):
    for k in range(3):
        for x in range(8):
            one[k, x] = left[k, x]
            one[k, 8 + x] = low[k, x]
            one[k, 16 + x] = high[k, x]
            one[k, 24 + x] = right[k, x]
    fill_strat(strat, left_first.at[pl.ds(24, 6)], own_strat, right_first.at[pl.ds(24, 6)])
    fine_steps((one, two), strat, spin, lane_weights())
    for k in range(3):
        for cell in range(4):
            x = HALO + 4 * cell
            slot = (4 * k + cell) % 2
            rows[slot] = (one[k, x] + one[k, x + 1]) + (one[k, x + 2] + one[k, x + 3])
            parts = [rows[slot, pl.ds(j, 8, stride=4), :] for j in range(4)]
            mean = ((parts[0] + parts[1]) + (parts[2] + parts[3])) * 0.0625
            payload[4 * k + cell] = mean - next_mean[k, cell]
            for j in range(4):
                rows[2 + slot, pl.ds(j, 8, stride=4), :] = mean
            for j in range(4):
                detail[k, 4 * cell + j] = one[k, x + j] - rows[2 + slot]
    payload[12] = strat_tile[...]


def coarse_step(state, halves, blocks, spin, strat, added=None):
    zonal, meridional = {}, {}

    def half_zonal(x):
        x = x % 32
        if x not in zonal:
            push = state[2, (x + 1) % 32] - state[2, (x - 1) % 32]
            zonal[x] = state[0, x] + spin * state[1, x] - 0.5 * push
        return zonal[x]

    def half_meridional(x):
        b = state[2, x]
        return state[1, x] - spin * half_zonal(x) - 0.5 * (y_next(b) - y_prev(b))

    def keep(k, pair, value):
        top = value.astype(jnp.bfloat16)
        rest = (value - top.astype(jnp.float32)).astype(jnp.bfloat16)
        halves[k, pl.ds(16 * pair, 16), pl.ds(0, 128)] = top
        halves[k, pl.ds(16 * pair, 16), pl.ds(128, 128)] = rest

    for pair in range(16):
        columns = [[], [], []]
        for x in (2 * pair, 2 * pair + 1):
            u = half_zonal(x)
            v = half_meridional(x)
            flow = (half_zonal(x + 1) - half_zonal(x - 1)) + (y_next(v) - y_prev(v))
            columns[0].append(u)
            columns[1].append(v)
            columns[2].append(state[2, x] - strat[x] * flow)
        for k in range(3):
            keep(k, pair, jnp.concatenate(columns[k], axis=0))
    for k in range(3):
        wide = jnp.dot(halves[k], blocks[k], preferred_element_type=jnp.float32)
        image = (wide[:, :128] + wide[:, 128:]).reshape(32, 8, 128)
        for x in range(32):
            tile = image[x]
            state[k, x] = tile if added is None else tile + added(k, x)


def chosen(mine, other, core, turn):
    run = turn // 2
    is_mine = jnp.full((8, 128), turn % 2 - core, jnp.int32) == 0

    def tile(k, x):
        place, row = 8 * run + x // 4, 4 * k + x % 4
        return jnp.where(is_mine, mine[place, row], other[place, row])

    return tile


def plane_kernel(where, spin, blocks, mine, other, end, part, strat, state, halves):
    core = where[0]
    for x in range(32):
        strat[x] = 0.5 * mine[8 * (x % 4) + x // 4, 12]
    start = chosen(mine, other, core, 0)
    for k in range(3):
        for x in range(32):
            state[k, x] = start(k, x)

    def turn(i, carry):
        coarse_step(state, halves, blocks, spin[...], strat, chosen(mine, other, core, i))
        return carry

    lax.fori_loop(1, 8, turn, 0)
    for k in range(3):
        for x in range(32):
            end[k, x] = state[k, x]
        part[k] = state[k, pl.ds(16 * core, 16)]


def final_kernel(
    where, spin, blocks, mine, other, strat, end, here, there, detail, mean, out,
    ends, state, halves, rows,
):
    core, row, turns, block = where[0], where[1], where[2], where[3]
    groups = jnp.where((row == 0) & (turns == 0), 4, row)
    for k in range(3):
        for x in range(32):
            ends[0, k, x] = end[k, x]
    for j in range(3):
        for k in range(3):
            ends[j + 1, k, pl.ds(16 * core, 16)] = here[j, k]
            ends[j + 1, k, pl.ds(16 * (1 - core), 16)] = there[j, k]

    scale = jnp.where(groups > 0, 1.0, 0.0).astype(jnp.float32)
    first = row % 4
    for k in range(3):
        for x in range(32):
            state[k, x] = ends[first, k, x] * scale

    def group(g, carry):
        def plain(i, inner):
            coarse_step(state, halves, blocks, spin[...], strat)
            return inner

        lax.fori_loop(0, 8, plain, 0)
        place = (row - g + 4) % 4
        for k in range(3):
            for x in range(32):
                state[k, x] = state[k, x] + ends[place, k, x]
        return carry

    lax.fori_loop(1, groups, group, 0)

    def turn(i, carry):
        coarse_step(state, halves, blocks, spin[...], strat, chosen(mine, other, core, i))
        return carry

    lax.fori_loop(0, turns, turn, 0)

    for k in range(3):
        for cell in range(4):
            slot = (4 * k + cell) % 2
            value = state[k, 4 * block + cell] + mean[k, cell]
            for j in range(4):
                rows[slot, pl.ds(j, 8, stride=4), :] = value
            for j in range(4):
                out[k, 4 * cell + j] = detail[k, 4 * cell + j] + rows[slot]


def call(kernel, outs, scratch, scalars=0):
    f32 = jnp.float32

    def run(*args):
        return pl.pallas_call(
            kernel,
            out_shape=[jax.ShapeDtypeStruct(shape, f32) for shape in outs],
            in_specs=[SMEM] * scalars + [VMEM] * (len(args) - scalars),
            out_specs=[VMEM] * len(outs),
            scratch_shapes=[pltpu.VMEM(shape, kind) for shape, kind in scratch],
            compiler_params=PARAMS,
        )(*args)

    return run


def restrict(state):
    kinds, across, along, levels = state.shape
    return state.reshape(kinds, across // 4, 4, along // 4, 4, levels).mean(axis=(2, 4))


def per_device(slice_starts, coriolis, stratification, inverse_blocks):
    f32, bf16 = jnp.float32, jnp.bfloat16
    start = slice_starts[0]
    fine_scratch = [((3, WIDE, 32, 128), f32)] * 2 + [((WIDE, 32, 128), f32)]
    chain_scratch = [((3, 32, 8, 128), f32), ((3, 256, 256), bf16)]

    head = jnp.concatenate([start[:, :8].reshape(24, 32, 128), stratification[:6]])
    tail = jnp.concatenate([start[:, 8:].reshape(24, 32, 128), stratification[10:]])
    left = lax.ppermute(tail, SPACE, ring(8, 1))
    right = lax.ppermute(head, SPACE, ring(8, -1))
    mean = restrict(start)
    next_mean = lax.ppermute(mean, TM, ring(32, -1))

    run, core = lax.axis_index("zl"), lax.axis_index("c")
    where = jnp.stack(
        [core, lax.axis_index("x"), 2 * run + core, lax.axis_index(SPACE)]
    ).astype(jnp.int32)
    half_spin = jnp.broadcast_to(0.5 * coriolis[:, None], (32, 128))
    coarse_spin = jnp.broadcast_to(4.0 * coriolis.reshape(8, 4).mean(axis=1)[:, None], (8, 128))
    strat_tile = lax.dynamic_index_in_dim(restrict(stratification[None])[0], run, 0, keepdims=False)
    turned = jnp.swapaxes(inverse_blocks, 1, 2)
    top = lax.reduce_precision(turned, exponent_bits=8, mantissa_bits=7)
    wide = jnp.concatenate([top, turned - top], axis=2).astype(bf16)
    blocks = jnp.concatenate([wide, wide], axis=1)

    low, high = call(first_half_kernel, [(3, 8, 32, 128)] * 2, fine_scratch)(
        half_spin, left, start, right, stratification
    )
    left_again = lax.ppermute(high, SPACE, ring(8, 1))
    right_again = lax.ppermute(low, SPACE, ring(8, -1))
    detail, payload = call(
        second_half_kernel,
        [(3, 16, 32, 128), (13, 8, 128)],
        fine_scratch + [((4, 32, 128), f32)],
    )(
        half_spin, left_again, low, high, right_again, left, right, stratification,
        next_mean, strat_tile,
    )

    mine = lax.all_to_all(jnp.broadcast_to(payload[None], (32, 13, 8, 128)), PLANE, 0, 0)
    other = lax.ppermute(mine, "c", ring(2, 1))
    detail = lax.ppermute(detail, TM, ring(32, 1))
    end, part, strat = call(
        plane_kernel, [(3, 32, 8, 128), (3, 16, 8, 128), (32, 8, 128)], chain_scratch, 1
    )(where, coarse_spin, blocks, mine, other)
    here = jnp.stack([lax.ppermute(part, "x", ring(4, by)) for by in (1, 2, 3)])
    there = lax.ppermute(here, "c", ring(2, 1))
    (out,) = call(
        final_kernel,
        [(3, 16, 32, 128)],
        [((4, 3, 32, 8, 128), f32)] + chain_scratch + [((2, 32, 128), f32)],
        1,
    )(where, coarse_spin, blocks, mine, other, strat, end, here, there, detail, mean)
    return out[None]


def solution(mesh):
    inner = Mesh(mesh.devices.reshape(SIZES), AXES)
    in_specs = (P(TM, None, SPACE, None, None), P(), P(SPACE, None, None), P())
    out_specs = P(TM, None, SPACE, None, None)
    return jax.shard_map(
        per_device, mesh=inner, in_specs=in_specs, out_specs=out_specs, check_vma=False
    )
```

```python
import jax
import jax.numpy as jnp
from jax import lax
from jax.experimental import pallas as pl
from jax.experimental.pallas import tpu as pltpu
from jax.sharding import Mesh
from jax.sharding import PartitionSpec as P

AXES = ("x", "zl", "c", "zh", "y")
SIZES = (4, 4, 2, 2, 4)
TM = ("x", "zl", "c")
SPACE = ("zh", "y")

VMEM = pl.BlockSpec(memory_space=pltpu.VMEM)
SMEM = pl.BlockSpec(memory_space=pltpu.SMEM)
PARAMS = pltpu.CompilerParams(vmem_limit_bytes=40 * 1024 * 1024)

HALO = 8
WIDE = 16 + 2 * HALO


def ring(size, by):
    return [(i, (i + by) % size) for i in range(size)]


def y_next(q):
    return pltpu.roll(q, q.shape[0] - 1, 0)


def y_prev(q):
    return pltpu.roll(q, 1, 0)


def fine_steps(bufs, strat, half_spin, lane_weight):
    def spread(q):
        diff = (pltpu.roll(q, 127, 1) - q) * lane_weight
        return diff - pltpu.roll(diff, 1, 1)

    for step in range(4):
        src, dst = bufs[step % 2], bufs[(step + 1) % 2]
        reach = 2 * (3 - step)
        first = HALO - reach
        count = 16 + 2 * reach

        def zonal(x, src=src):
            u = src[0, x]
            sides = src[0, x + 1] + src[0, x - 1] + (y_next(u) + y_prev(u))
            push = src[2, x + 1] - src[2, x - 1]
            return (
                (0.8 * u + spread(u))
                + (half_spin[...] * src[1, x] - 0.25 * push)
                + 0.05 * sides
            )

        def chunk(i, carry, src=src, dst=dst, first=first, zonal=zonal):
            before, here = carry
            for k in range(4):
                x = first + 4 * i + k
                after = zonal(x + 1)
                dst[0, x] = here
                v = src[1, x]
                b = src[2, x]
                b_next, b_prev = y_next(b), y_prev(b)
                v_new = (
                    (0.8 * v + spread(v))
                    - (half_spin[...] * here + 0.25 * (b_next - b_prev))
                    + 0.05 * (src[1, x + 1] + src[1, x - 1] + (y_next(v) + y_prev(v)))
                )
                dst[1, x] = v_new
                flow = (after - before) + (y_next(v_new) - y_prev(v_new))
                dst[2, x] = (
                    (0.8 * b + spread(b))
                    - strat[x] * flow
                    + 0.05 * (src[2, x + 1] + src[2, x - 1] + (b_next + b_prev))
                )
                before, here = here, after
            return before, here

        lax.fori_loop(0, count // 4, chunk, (zonal(first - 1), zonal(first)))


def lane_weights():
    lane = lax.broadcasted_iota(jnp.int32, (32, 128), 1)
    return jnp.where(lane < 127, 0.15, 0.0).astype(jnp.float32)


def fill_strat(strat, left, own, right):
    for x in range(6):
        strat[HALO - 6 + x] = 0.25 * left[x]
        strat[HALO + 16 + x] = 0.25 * right[x]
    for x in range(16):
        strat[HALO + x] = 0.25 * own[x]


def first_half_kernel(spin, left, start, right, own_strat, low, high, one, two, strat):
    for k in range(3):
        for x in range(8):
            one[k, x] = left[8 * k + x]
            one[k, 24 + x] = right[8 * k + x]
        for x in range(16):
            one[k, 8 + x] = start[k, x]
    fill_strat(strat, left.at[pl.ds(24, 6)], own_strat, right.at[pl.ds(24, 6)])
    fine_steps((one, two), strat, spin, lane_weights())
    for k in range(3):
        for x in range(8):
            low[k, x] = one[k, 8 + x]
            high[k, x] = one[k, 16 + x]


def second_half_kernel(
    spin, left, low, high, right, left_first, right_first, own_strat, next_mean,
    detail, payload, one, two, strat, rows,
):
    for k in range(3):
        for x in range(8):
            one[k, x] = left[k, x]
            one[k, 8 + x] = low[k, x]
            one[k, 16 + x] = high[k, x]
            one[k, 24 + x] = right[k, x]
    fill_strat(strat, left_first.at[pl.ds(24, 6)], own_strat, right_first.at[pl.ds(24, 6)])
    fine_steps((one, two), strat, spin, lane_weights())
    for k in range(3):
        for cell in range(4):
            x = HALO + 4 * cell
            slot = (4 * k + cell) % 2
            rows[slot] = (one[k, x] + one[k, x + 1]) + (one[k, x + 2] + one[k, x + 3])
            parts = [rows[slot, pl.ds(j, 8, stride=4), :] for j in range(4)]
            mean = ((parts[0] + parts[1]) + (parts[2] + parts[3])) * 0.0625
            payload[4 * k + cell] = mean - next_mean[k, cell]
            for j in range(4):
                rows[2 + slot, pl.ds(j, 8, stride=4), :] = mean
            for j in range(4):
                detail[k, 4 * cell + j] = one[k, x + j] - rows[2 + slot]


def coarse_step(state, halves, blocks, spin, strat):
    zonal, meridional = {}, {}

    def half_zonal(x):
        x = x % 32
        if x not in zonal:
            push = state[2, (x + 1) % 32] - state[2, (x - 1) % 32]
            zonal[x] = state[0, x] + spin * state[1, x] - 0.5 * push
        return zonal[x]

    def half_meridional(x):
        b = state[2, x]
        return state[1, x] - spin * half_zonal(x) - 0.5 * (y_next(b) - y_prev(b))

    def keep(k, pair, value):
        top = value.astype(jnp.bfloat16)
        rest = (value - top.astype(jnp.float32)).astype(jnp.bfloat16)
        halves[k, pl.ds(16 * pair, 16), pl.ds(0, 128)] = top
        halves[k, pl.ds(16 * pair, 16), pl.ds(128, 128)] = rest

    for pair in range(16):
        columns = [[], [], []]
        for x in (2 * pair, 2 * pair + 1):
            u = half_zonal(x)
            v = half_meridional(x)
            flow = (half_zonal(x + 1) - half_zonal(x - 1)) + (y_next(v) - y_prev(v))
            columns[0].append(u)
            columns[1].append(v)
            columns[2].append(state[2, x] - strat[x] * flow)
        for k in range(3):
            keep(k, pair, jnp.concatenate(columns[k], axis=0))
    for k in range(3):
        wide = jnp.dot(halves[k], blocks[k], preferred_element_type=jnp.float32)
        image = (wide[:, :128] + wide[:, 128:]).reshape(32, 8, 128)
        for x in range(32):
            state[k, x] = image[x]


def table(where, increments, mine, other):
    for j in range(4):
        run = (where[0] - j + 4) % 4
        for n in range(12):
            increments[2 * run + where[1], n] = mine[j][n]
            increments[2 * run + 1 - where[1], n] = other[j][n]


def add_block(state, increments, turn, block):
    for k in range(3):
        for cell in range(4):
            place = 4 * block + cell
            state[k, place] = state[k, place] + increments[turn, 4 * k + cell]


def clear(state):
    for k in range(3):
        for x in range(32):
            state[k, x] = jnp.zeros((8, 128), jnp.float32)


def plane_kernel(where, spin, blocks, strat_mine, strat_other, *refs):
    mine, other, (end, part, strat, state, halves, increments) = refs[:4], refs[4:8], refs[8:]
    core, zh, y = where[1], where[3], where[4]
    for j in range(4):
        column = (y - j + 4) % 4
        for cell in range(4):
            strat[4 * (4 * zh + column) + cell] = 0.5 * strat_mine[j, cell]
            strat[4 * (4 * (1 - zh) + column) + cell] = 0.5 * strat_other[j, cell]
    table(where, increments, mine, other)
    clear(state)
    block = 4 * zh + y
    add_block(state, increments, 0, block)

    def turn(i, carry):
        coarse_step(state, halves, blocks, spin[...], strat)
        add_block(state, increments, i, block)
        return carry

    lax.fori_loop(1, 8, turn, 0)
    for k in range(3):
        for x in range(32):
            end[k, x] = state[k, x]
        part[k] = state[k, pl.ds(16 * core, 16)]


def chain_kernel(where, spin, blocks, strat, end, *refs):
    mine, other, here, there = refs[:4], refs[4:8], refs[8:11], refs[11:14]
    parts, (ends, state, halves, increments) = refs[14:18], refs[18:]
    run, core, row, zh, y = where[0], where[1], where[2], where[3], where[4]
    turns = 2 * run + core
    groups = jnp.where((row == 0) & (turns == 0), 4, row)
    table(where, increments, mine, other)
    for k in range(3):
        for x in range(32):
            ends[0, k, x] = end[k, x]
    for j in range(3):
        for k in range(3):
            ends[j + 1, k, pl.ds(16 * core, 16)] = here[j][k]
            ends[j + 1, k, pl.ds(16 * (1 - core), 16)] = there[j][k]

    scale = jnp.where(groups > 0, 1.0, 0.0).astype(jnp.float32)
    for k in range(3):
        for x in range(32):
            state[k, x] = ends[row, k, x] * scale

    def group(g, carry):
        def plain(i, inner):
            coarse_step(state, halves, blocks, spin[...], strat)
            return inner

        lax.fori_loop(0, 8, plain, 0)
        place = (row - g + 4) % 4
        for k in range(3):
            for x in range(32):
                state[k, x] = state[k, x] + ends[place, k, x]
        return carry

    lax.fori_loop(1, groups, group, 0)
    block = 4 * zh + y

    def turn(i, carry):
        coarse_step(state, halves, blocks, spin[...], strat)
        add_block(state, increments, i, block)
        return carry

    lax.fori_loop(0, turns, turn, 0)

    for j in range(4):
        column = (y + j) % 4
        for half in range(2):
            side = zh if half == 0 else 1 - zh
            for k in range(3):
                for cell in range(4):
                    parts[j][half, 4 * k + cell] = state[k, 4 * (4 * side + column) + cell]


def final_kernel(kept, sent, detail, mean, out, rows):
    for k in range(3):
        for cell in range(4):
            n = 4 * k + cell
            slot = n % 2
            value = kept[n] + sent[n] + mean[k, cell]
            for j in range(4):
                rows[slot, pl.ds(j, 8, stride=4), :] = value
            for j in range(4):
                out[k, 4 * cell + j] = detail[k, 4 * cell + j] + rows[slot]


def call(kernel, outs, scratch, scalars=0):
    f32 = jnp.float32

    def run(*args):
        return pl.pallas_call(
            kernel,
            out_shape=[jax.ShapeDtypeStruct(shape, f32) for shape in outs],
            in_specs=[SMEM] * scalars + [VMEM] * (len(args) - scalars),
            out_specs=[VMEM] * len(outs),
            scratch_shapes=[pltpu.VMEM(shape, kind) for shape, kind in scratch],
            compiler_params=PARAMS,
        )(*args)

    return run


def restrict(state):
    kinds, across, along, levels = state.shape
    return state.reshape(kinds, across // 4, 4, along // 4, 4, levels).mean(axis=(2, 4))


def per_device(slice_starts, coriolis, stratification, inverse_blocks):
    f32, bf16 = jnp.float32, jnp.bfloat16
    start = slice_starts[0]
    fine_scratch = [((3, WIDE, 32, 128), f32)] * 2 + [((WIDE, 32, 128), f32)]
    chain_scratch = [((3, 32, 8, 128), f32), ((3, 256, 256), bf16), ((8, 12, 8, 128), f32)]

    head = jnp.concatenate([start[:, :8].reshape(24, 32, 128), stratification[:6]])
    tail = jnp.concatenate([start[:, 8:].reshape(24, 32, 128), stratification[10:]])
    left = lax.ppermute(tail, SPACE, ring(8, 1))
    right = lax.ppermute(head, SPACE, ring(8, -1))
    mean = restrict(start)
    next_mean = lax.ppermute(mean, TM, ring(32, -1))

    where = jnp.stack([lax.axis_index(name) for name in ("zl", "c", "x", "zh", "y")]).astype(jnp.int32)
    half_spin = jnp.broadcast_to(0.5 * coriolis[:, None], (32, 128))
    coarse_spin = jnp.broadcast_to(4.0 * coriolis.reshape(8, 4).mean(axis=1)[:, None], (8, 128))
    turned = jnp.swapaxes(inverse_blocks, 1, 2)
    top = lax.reduce_precision(turned, exponent_bits=8, mantissa_bits=7)
    wide = jnp.concatenate([top, turned - top], axis=2).astype(bf16)
    blocks = jnp.concatenate([wide, wide], axis=1)
    own_strat = restrict(stratification[None])[0]
    strat_mine = jnp.stack(
        [own_strat] + [lax.ppermute(own_strat, "y", ring(4, by)) for by in (1, 2, 3)]
    )
    strat_other = lax.ppermute(strat_mine, "zh", ring(2, 1))

    low, high = call(first_half_kernel, [(3, 8, 32, 128)] * 2, fine_scratch)(
        half_spin, left, start, right, stratification
    )
    left_again = lax.ppermute(high, SPACE, ring(8, 1))
    right_again = lax.ppermute(low, SPACE, ring(8, -1))
    detail, increment = call(
        second_half_kernel,
        [(3, 16, 32, 128), (12, 8, 128)],
        fine_scratch + [((4, 32, 128), f32)],
    )(
        half_spin, left_again, low, high, right_again, left, right, stratification, next_mean
    )

    mine = [increment] + [lax.ppermute(increment, "zl", ring(4, by)) for by in (1, 2, 3)]
    other = [lax.ppermute(part, "c", ring(2, 1)) for part in mine]
    detail = lax.ppermute(detail, TM, ring(32, 1))
    end, part, strat = call(
        plane_kernel, [(3, 32, 8, 128), (3, 16, 8, 128), (32, 8, 128)], chain_scratch, 1
    )(where, coarse_spin, blocks, strat_mine, strat_other, *mine, *other)
    here = [lax.ppermute(part, "x", ring(4, by)) for by in (1, 2, 3)]
    there = [lax.ppermute(part, "c", ring(2, 1)) for part in here]
    parts = call(
        chain_kernel,
        [(2, 12, 8, 128)] * 4,
        [((4, 3, 32, 8, 128), f32)] + chain_scratch,
        1,
    )(where, coarse_spin, blocks, strat, end, *mine, *other, *here, *there)
    total = parts[0]
    for by in (1, 2, 3):
        total = total + lax.ppermute(parts[by], "y", ring(4, by))
    sent = lax.ppermute(total[1], "zh", ring(2, 1))
    (out,) = call(final_kernel, [(3, 16, 32, 128)], [((2, 32, 128), f32)])(
        total[0], sent, detail, mean
    )
    return out[None]


def solution(mesh):
    inner = Mesh(mesh.devices.reshape(SIZES), AXES)
    in_specs = (P(TM, None, SPACE, None, None), P(), P(SPACE, None, None), P())
    out_specs = P(TM, None, SPACE, None, None)
    return jax.shard_map(
        per_device, mesh=inner, in_specs=in_specs, out_specs=out_specs, check_vma=False
    )
```

```python
import itertools

import jax
import jax.numpy as jnp
from jax import lax
from jax.experimental import pallas as pl
from jax.experimental.pallas import tpu as pltpu
from jax.sharding import Mesh
from jax.sharding import PartitionSpec as P

AXES = ("x", "zl", "c", "zh", "y")
SIZES = (4, 4, 2, 2, 4)
TM = ("x", "zl", "c")
SPACE = ("zh", "y")

VMEM = pl.BlockSpec(memory_space=pltpu.VMEM)
SMEM = pl.BlockSpec(memory_space=pltpu.SMEM)
PARAMS = pltpu.CompilerParams(vmem_limit_bytes=40 * 1024 * 1024)

HALO = 8
WIDE = 16 + 2 * HALO


def ring(size, by):
    return [(i, (i + by) % size) for i in range(size)]


def y_next(q):
    return pltpu.roll(q, q.shape[0] - 1, 0)


def y_prev(q):
    return pltpu.roll(q, 1, 0)


def fine_steps(bufs, strat, half_spin, lane_weight):
    def spread(q):
        diff = (pltpu.roll(q, 127, 1) - q) * lane_weight
        return diff - pltpu.roll(diff, 1, 1)

    for step in range(4):
        src, dst = bufs[step % 2], bufs[(step + 1) % 2]
        reach = 2 * (3 - step)
        first = HALO - reach
        count = 16 + 2 * reach

        def zonal(x, src=src):
            u = src[0, x]
            sides = src[0, x + 1] + src[0, x - 1] + (y_next(u) + y_prev(u))
            push = src[2, x + 1] - src[2, x - 1]
            return (
                (0.8 * u + spread(u))
                + (half_spin[...] * src[1, x] - 0.25 * push)
                + 0.05 * sides
            )

        def chunk(i, carry, src=src, dst=dst, first=first, zonal=zonal):
            before, here = carry
            for k in range(4):
                x = first + 4 * i + k
                after = zonal(x + 1)
                dst[0, x] = here
                v = src[1, x]
                b = src[2, x]
                b_next, b_prev = y_next(b), y_prev(b)
                v_new = (
                    (0.8 * v + spread(v))
                    - (half_spin[...] * here + 0.25 * (b_next - b_prev))
                    + 0.05 * (src[1, x + 1] + src[1, x - 1] + (y_next(v) + y_prev(v)))
                )
                dst[1, x] = v_new
                flow = (after - before) + (y_next(v_new) - y_prev(v_new))
                dst[2, x] = (
                    (0.8 * b + spread(b))
                    - strat[x] * flow
                    + 0.05 * (src[2, x + 1] + src[2, x - 1] + (b_next + b_prev))
                )
                before, here = here, after
            return before, here

        lax.fori_loop(0, count // 4, chunk, (zonal(first - 1), zonal(first)))


def lane_weights():
    lane = lax.broadcasted_iota(jnp.int32, (32, 128), 1)
    return jnp.where(lane < 127, 0.15, 0.0).astype(jnp.float32)


def fill_strat(strat, left, own, right):
    for x in range(6):
        strat[HALO - 6 + x] = 0.25 * left[x]
        strat[HALO + 16 + x] = 0.25 * right[x]
    for x in range(16):
        strat[HALO + x] = 0.25 * own[x]


def fill_state(buf, left, own, right):
    for k in range(3):
        for x in range(16):
            buf[k, HALO + x] = own[k, x]
    for x in range(8):
        buf[0, x] = left[x]
        buf[2, x] = left[15 + x]
        buf[0, 24 + x] = right[x]
        buf[2, 24 + x] = right[15 + x]
    for x in range(7):
        buf[1, 1 + x] = left[8 + x]
        buf[1, 24 + x] = right[8 + x]


def first_half_kernel(
    spin, y, c0, c1, c2, c3, left_strat, right_strat, own_strat, start, left, right,
    middle, low, high, columns, one, two, strat,
):
    fill_state(one, left, start, right)
    fill_strat(strat, left_strat, own_strat, right_strat)
    for j, cells in enumerate((c0, c1, c2, c3)):
        columns[(y[0] - j + 4) % 4] = cells[...]
    fine_steps((one, two), strat, spin, lane_weights())
    for k in range(3):
        for x in range(16):
            middle[k, x] = one[k, HALO + x]
    for x in range(8):
        low[x] = one[0, 8 + x]
        low[15 + x] = one[2, 8 + x]
        high[x] = one[0, 16 + x]
        high[15 + x] = one[2, 16 + x]
    for x in range(7):
        low[8 + x] = one[1, 8 + x]
        high[8 + x] = one[1, 17 + x]


def second_half_kernel(
    spin, zh, near, far, next_mean, left_strat, right_strat, own_strat, middle, left, right,
    detail, increment, coarse_strat, one, two, strat, rows,
):
    fill_state(one, left, middle, right)
    fill_strat(strat, left_strat, own_strat, right_strat)
    for column in range(4):
        for cell in range(4):
            coarse_strat[16 * zh[0] + 4 * column + cell] = 0.5 * near[column, cell]
            coarse_strat[16 * (1 - zh[0]) + 4 * column + cell] = 0.5 * far[column, cell]
    fine_steps((one, two), strat, spin, lane_weights())
    for k in range(3):
        for cell in range(4):
            x = HALO + 4 * cell
            slot = (4 * k + cell) % 2
            rows[slot] = (one[k, x] + one[k, x + 1]) + (one[k, x + 2] + one[k, x + 3])
            parts = [rows[slot, pl.ds(j, 8, stride=4), :] for j in range(4)]
            mean = ((parts[0] + parts[1]) + (parts[2] + parts[3])) * 0.0625
            increment[4 * k + cell] = mean - next_mean[k, cell]
            for j in range(4):
                rows[2 + slot, pl.ds(j, 8, stride=4), :] = mean
            for j in range(4):
                detail[k, 4 * cell + j] = one[k, x + j] - rows[2 + slot]


def coarse_step(state, halves, blocks, spin, strat):
    zonal, meridional = {}, {}

    def half_zonal(x):
        x = x % 32
        if x not in zonal:
            push = state[2, (x + 1) % 32] - state[2, (x - 1) % 32]
            zonal[x] = state[0, x] + spin * state[1, x] - 0.5 * push
        return zonal[x]

    def half_meridional(x):
        b = state[2, x]
        return state[1, x] - spin * half_zonal(x) - 0.5 * (y_next(b) - y_prev(b))

    def keep(k, pair, value):
        top = value.astype(jnp.bfloat16)
        rest = (value - top.astype(jnp.float32)).astype(jnp.bfloat16)
        halves[k, pl.ds(16 * pair, 16), pl.ds(0, 128)] = top
        halves[k, pl.ds(16 * pair, 16), pl.ds(128, 128)] = rest

    for pair in range(16):
        columns = [[], [], []]
        for x in (2 * pair, 2 * pair + 1):
            u = half_zonal(x)
            v = half_meridional(x)
            flow = (half_zonal(x + 1) - half_zonal(x - 1)) + (y_next(v) - y_prev(v))
            columns[0].append(u)
            columns[1].append(v)
            columns[2].append(state[2, x] - strat[x] * flow)
        for k in range(3):
            keep(k, pair, jnp.concatenate(columns[k], axis=0))
    for k in range(3):
        wide = jnp.dot(halves[k], blocks[k], preferred_element_type=jnp.float32)
        image = (wide[:, :128] + wide[:, 128:]).reshape(32, 8, 128)
        for x in range(32):
            state[k, x] = image[x]


def table(where, increments, mine, other):
    for j in range(4):
        run = (where[0] - j + 4) % 4
        for n in range(12):
            increments[2 * run + where[1], n] = mine[j][n]
            increments[2 * run + 1 - where[1], n] = other[j][n]


def add_block(state, increments, turn, block):
    for k in range(3):
        for cell in range(4):
            place = 4 * block + cell
            state[k, place] = state[k, place] + increments[turn, 4 * k + cell]


def clear(state):
    for k in range(3):
        for x in range(32):
            state[k, x] = jnp.zeros((8, 128), jnp.float32)


def steps(count, state, halves, blocks, spin, strat):
    def step(i, carry):
        coarse_step(state, halves, blocks, spin[...], strat)
        return carry

    lax.fori_loop(0, count, step, 0)


def plane_kernel(where, spin, blocks, strat, *refs):
    mine, other, (state, part, halves, increments) = refs[:4], refs[4:8], refs[8:]
    core, zh, y = where[1], where[3], where[4]
    table(where, increments, mine, other)
    clear(state)
    block = 4 * zh + y
    add_block(state, increments, 0, block)

    def turn(i, carry):
        coarse_step(state, halves, blocks, spin[...], strat)
        add_block(state, increments, i, block)
        return carry

    lax.fori_loop(1, 8, turn, 0)
    for k in range(3):
        part[k] = state[k, pl.ds(16 * core, 16)]


def power_kernel(where, spin, blocks, strat, before, *refs):
    state, part, halves = refs[-3:]
    for k in range(3):
        for x in range(32):
            state[k, x] = before[k, x]
    steps(8, state, halves, blocks, spin, strat)
    for k in range(3):
        part[k] = state[k, pl.ds(16 * where[1], 16)]


def chain_kernel(where, spin, blocks, strat, last, *refs):
    mine, other, here, there = refs[:4], refs[4:8], refs[10:7:-1], refs[13:10:-1]
    parts, (state, halves, increments) = refs[14:18], refs[18:]
    run, core, row, zh, y = where[0], where[1], where[2], where[3], where[4]
    turns = 2 * run + core
    closing = (row == 0) & (turns == 0)
    table(where, increments, mine, other)
    clear(state)

    @pl.when(closing)
    def _():
        for k in range(3):
            for x in range(32):
                state[k, x] = last[k, x]
        steps(8, state, halves, blocks, spin, strat)

    for j in range(3):

        @pl.when(closing | (row > j))
        def _(j=j):
            for k in range(3):
                for x in range(16):
                    near, far = 16 * core + x, 16 * (1 - core) + x
                    state[k, near] = state[k, near] + here[j][k, x]
                    state[k, far] = state[k, far] + there[j][k, x]

    block = 4 * zh + y

    def turn(i, carry):
        coarse_step(state, halves, blocks, spin[...], strat)
        add_block(state, increments, i, block)
        return carry

    lax.fori_loop(0, turns, turn, 0)

    for j in range(4):
        column = (y + j) % 4
        for half in range(2):
            side = zh if half == 0 else 1 - zh
            for k in range(3):
                for cell in range(4):
                    parts[j][half, 4 * k + cell] = state[k, 4 * (4 * side + column) + cell]


def final_kernel(kept, sent, detail, mean, out, rows):
    for k in range(3):
        for cell in range(4):
            n = 4 * k + cell
            slot = n % 2
            value = kept[n] + sent[n] + mean[k, cell]
            for j in range(4):
                rows[slot, pl.ds(j, 8, stride=4), :] = value
            for j in range(4):
                out[k, 4 * cell + j] = detail[k, 4 * cell + j] + rows[slot]


def call(kernel, outs, scratch, cost=0):
    f32 = jnp.float32

    def run(*args):
        return pl.pallas_call(
            kernel,
            out_shape=[jax.ShapeDtypeStruct(shape, f32) for shape in outs],
            in_specs=[SMEM if arg.dtype == jnp.int32 else VMEM for arg in args],
            cost_estimate=pl.CostEstimate(flops=cost, bytes_accessed=cost // 256, transcendentals=0),
            out_specs=[VMEM] * len(outs),
            scratch_shapes=[pltpu.VMEM(shape, kind) for shape, kind in scratch],
            compiler_params=PARAMS,
        )(*args)

    return run


def restrict(state):
    kinds, across, along, levels = state.shape
    return state.reshape(kinds, across // 4, 4, along // 4, 4, levels).mean(axis=(2, 4))


def strat_sources(by):
    pairs = []
    for x, zl, c, zh, y in itertools.product(*map(range, SIZES)):
        from_zh, from_y = divmod((4 * zh + y + by) % 8, 4)
        from_zl = zl if from_zh == zh else 3 - zl
        source = (((x * 4 + from_zl) * 2 + c) * 2 + from_zh) * 4 + from_y
        pairs.append((source, (((x * 4 + zl) * 2 + c) * 2 + zh) * 4 + y))
    return pairs


def per_device(slice_starts, coriolis, stratification, inverse_blocks):
    f32, bf16 = jnp.float32, jnp.bfloat16
    start = slice_starts[0]
    fine_scratch = [((3, WIDE, 32, 128), f32)] * 2 + [((WIDE, 32, 128), f32)]
    halves, state = ((3, 256, 256), bf16), ((3, 32, 8, 128), f32)
    increments = ((8, 12, 8, 128), f32)

    head = jnp.concatenate([start[0, :8], start[1, :7], start[2, :8]])
    tail = jnp.concatenate([start[0, 8:], start[1, 9:], start[2, 8:]])
    left = lax.ppermute(tail, SPACE, ring(8, 1))
    right = lax.ppermute(head, SPACE, ring(8, -1))
    left_strat = lax.ppermute(stratification[10:], AXES, strat_sources(-1))
    right_strat = lax.ppermute(stratification[:6], AXES, strat_sources(1))
    mean = restrict(start)
    next_mean = lax.ppermute(mean, TM, ring(32, -1))
    own_strat = restrict(stratification[None])[0]
    strat_parts = [own_strat] + [lax.ppermute(own_strat, "y", ring(4, by)) for by in (1, 2, 3)]

    spots = [lax.axis_index(name).astype(jnp.int32) for name in ("zl", "c", "x", "zh", "y")]
    where = jnp.stack(spots)
    half_spin = jnp.broadcast_to(0.5 * coriolis[:, None], (32, 128))
    coarse_spin = jnp.broadcast_to(4.0 * coriolis.reshape(8, 4).mean(axis=1)[:, None], (8, 128))
    turned = jnp.swapaxes(inverse_blocks, 1, 2)
    top = lax.reduce_precision(turned, exponent_bits=8, mantissa_bits=7)
    wide = jnp.concatenate([top, turned - top], axis=2).astype(bf16)
    blocks = jnp.concatenate([wide, wide], axis=1)

    middle, low, high, near = call(
        first_half_kernel,
        [(3, 16, 32, 128), (23, 32, 128), (23, 32, 128), (4, 4, 8, 128)],
        fine_scratch,
    )(
        half_spin, spots[4][None], *strat_parts, left_strat, right_strat, stratification,
        start, left, right,
    )
    left_again = lax.ppermute(high, SPACE, ring(8, 1))
    right_again = lax.ppermute(low, SPACE, ring(8, -1))
    far = lax.ppermute(near, "zh", ring(2, 1))
    detail, increment, strat = call(
        second_half_kernel,
        [(3, 16, 32, 128), (12, 8, 128), (32, 8, 128)],
        fine_scratch + [((4, 32, 128), f32)],
    )(
        half_spin, spots[3][None], near, far, next_mean, left_strat, right_strat,
        stratification, middle, left_again, right_again,
    )

    mine = [increment] + [lax.ppermute(increment, "zl", ring(4, by)) for by in (1, 2, 3)]
    other = [lax.ppermute(part, "c", ring(2, 1)) for part in mine]
    detail = lax.ppermute(detail, TM, ring(32, 1))
    common = (where, coarse_spin, blocks, strat)
    pair = [state[0], (3, 16, 8, 128)]
    end, part = call(plane_kernel, pair, [halves, increments])(*common, *mine, *other)
    here = [lax.ppermute(part, "x", ring(4, 1))]
    for by in (2, 3):
        end, part = call(power_kernel, pair, [halves], 10**9)(*common, end, *here[: by - 2])
        here.append(lax.ppermute(part, "x", ring(4, by)))
    there = [lax.ppermute(part, "c", ring(2, 1)) for part in here]
    parts = call(chain_kernel, [(2, 12, 8, 128)] * 4, [state, halves, increments])(
        *common, end, *mine, *other, *here[::-1], *there[::-1]
    )
    total = parts[0]
    for by in (1, 2, 3):
        total = total + lax.ppermute(parts[by], "y", ring(4, by))
    sent = lax.ppermute(total[1], "zh", ring(2, 1))
    (out,) = call(final_kernel, [(3, 16, 32, 128)], [((2, 32, 128), f32)])(
        total[0], sent, detail, mean
    )
    return out[None]


def solution(mesh):
    inner = Mesh(mesh.devices.reshape(SIZES), AXES)
    in_specs = (P(TM, None, SPACE, None, None), P(), P(SPACE, None, None), P())
    out_specs = P(TM, None, SPACE, None, None)
    return jax.shard_map(
        per_device, mesh=inner, in_specs=in_specs, out_specs=out_specs, check_vma=False
    )
```

```python
import jax
import jax.numpy as jnp
from jax import lax
from jax.experimental import pallas as pl
from jax.experimental.pallas import tpu as pltpu
from jax.sharding import Mesh
from jax.sharding import PartitionSpec as P

AXES = ("x", "zl", "c", "zh", "y")
SIZES = (4, 4, 2, 2, 4)
TM = ("x", "zl", "c")
SPACE = ("zh", "y")

VMEM = pl.BlockSpec(memory_space=pltpu.VMEM)
SMEM = pl.BlockSpec(memory_space=pltpu.SMEM)
PARAMS = pltpu.CompilerParams(vmem_limit_bytes=40 * 1024 * 1024)

STEPS = 8
HALO = 16
WIDE = 16 + 2 * HALO
COST = 10**10
UNROLL = (11, 20, 18, 16, 14, 12, 10, 16)


def ring(size, by):
    return [(i, (i + by) % size) for i in range(size)]


def y_next(q):
    return pltpu.roll(q, q.shape[0] - 1, 0)


def y_prev(q):
    return pltpu.roll(q, 1, 0)


def fine_steps(bufs, strat, half_spin, weights):
    here_weight, up_weight, down_weight = weights

    def vertical(q):
        above, below = pltpu.roll(q, 127, 1), pltpu.roll(q, 1, 1)
        return here_weight[...] * q + (up_weight[...] * above + down_weight[...] * below)

    for step in range(STEPS):
        src, dst = bufs[step % 2], bufs[(step + 1) % 2]
        reach = 2 * (STEPS - 1 - step)
        first = HALO - reach
        count = 16 + 2 * reach
        unroll = UNROLL[step]

        def zonal(x, src=src):
            u = src[0, x]
            sides = src[0, x + 1] + src[0, x - 1] + (y_next(u) + y_prev(u))
            push = src[2, x + 1] - src[2, x - 1]
            return vertical(u) + (half_spin[...] * src[1, x] - 0.25 * push) + 0.05 * sides

        def chunk(i, carry, src=src, dst=dst, first=first, unroll=unroll, zonal=zonal):
            before, here = carry
            for k in range(unroll):
                x = first + unroll * i + k
                after = zonal(x + 1)
                dst[0, x] = here
                v = src[1, x]
                b = src[2, x]
                b_next, b_prev = y_next(b), y_prev(b)
                v_new = (
                    vertical(v)
                    - (half_spin[...] * here + 0.25 * (b_next - b_prev))
                    + 0.05 * (src[1, x + 1] + src[1, x - 1] + (y_next(v) + y_prev(v)))
                )
                dst[1, x] = v_new
                flow = (after - before) + (y_next(v_new) - y_prev(v_new))
                dst[2, x] = (
                    vertical(b)
                    - strat[x] * flow
                    + 0.05 * (src[2, x + 1] + src[2, x - 1] + (b_next + b_prev))
                )
                before, here = here, after
            return before, here

        lax.fori_loop(0, count // unroll, chunk, (zonal(first - 1), zonal(first)))


def block_means(rows, cells):
    rows[...] = (cells[0] + cells[1]) + (cells[2] + cells[3])
    parts = [rows[pl.ds(j, 8, stride=4), :] for j in range(4)]
    return ((parts[0] + parts[1]) + (parts[2] + parts[3])) * 0.0625


def means_kernel(start, strat, mean, own_strat, rows):
    for k in range(3):
        for cell in range(4):
            cells = [start[k, 4 * cell + j] for j in range(4)]
            mean[k, cell] = block_means(rows.at[cell % 2], cells)
    for cell in range(4):
        cells = [strat[4 * cell + j] for j in range(4)]
        own_strat[cell] = block_means(rows.at[cell % 2], cells)


def fine_kernel(
    spin, place, near, far, blocks, next_mean, own, left, right,
    detail, increment, coarse_strat, one, two, strat, rows, weights,
):
    del blocks
    for k in range(3):
        for x in range(16):
            one[k, x] = left[16 * k + x]
            one[k, 16 + x] = own[16 * k + x]
            one[k, 32 + x] = right[16 * k + x]
    for x in range(16):
        strat[x] = 0.25 * left[48 + x]
        strat[16 + x] = 0.25 * own[48 + x]
        strat[32 + x] = 0.25 * right[48 + x]
    zh, y = place[0], place[1]
    for j in range(4):
        column = (y - j + 4) % 4
        for cell in range(4):
            mine, other = 4 * zh + column, 4 * (1 - zh) + column
            coarse_strat[4 * mine + cell] = 0.5 * near[j, cell]
            coarse_strat[4 * other + cell] = 0.5 * far[j, cell]
    lane = lax.broadcasted_iota(jnp.int32, (32, 128), 1)
    up = jnp.where(lane < 127, 0.15, 0.0).astype(jnp.float32)
    down = jnp.where(lane > 0, 0.15, 0.0).astype(jnp.float32)
    weights[0] = 0.8 - up - down
    weights[1] = up
    weights[2] = down
    fine_steps((one, two), strat, spin, [weights.at[n] for n in range(3)])
    for k in range(3):
        for cell in range(4):
            x = HALO + 4 * cell
            slot = (4 * k + cell) % 2
            mean = block_means(rows.at[slot], [one[k, x + j] for j in range(4)])
            increment[4 * k + cell] = mean - next_mean[k, cell]
            for j in range(4):
                rows[2 + slot, pl.ds(j, 8, stride=4), :] = mean
            for j in range(4):
                detail[k, 4 * cell + j] = one[k, x + j] - rows[2 + slot]


def coarse_step(state, halves, blocks, spin, strat):
    zonal, meridional = {}, {}

    def half_zonal(x):
        x = x % 32
        if x not in zonal:
            push = state[2, (x + 1) % 32] - state[2, (x - 1) % 32]
            zonal[x] = state[0, x] + spin * state[1, x] - 0.5 * push
        return zonal[x]

    def half_meridional(x):
        b = state[2, x]
        return state[1, x] - spin * half_zonal(x) - 0.5 * (y_next(b) - y_prev(b))

    def keep(k, pair, value):
        top = value.astype(jnp.bfloat16)
        rest = (value - top.astype(jnp.float32)).astype(jnp.bfloat16)
        halves[k, pl.ds(16 * pair, 16), pl.ds(0, 128)] = top
        halves[k, pl.ds(16 * pair, 16), pl.ds(128, 128)] = rest

    for pair in range(16):
        columns = [[], [], []]
        for x in (2 * pair, 2 * pair + 1):
            u = half_zonal(x)
            v = half_meridional(x)
            flow = (half_zonal(x + 1) - half_zonal(x - 1)) + (y_next(v) - y_prev(v))
            columns[0].append(u)
            columns[1].append(v)
            columns[2].append(state[2, x] - strat[x] * flow)
        for k in range(3):
            keep(k, pair, jnp.concatenate(columns[k], axis=0))
    for k in range(3):
        wide = jnp.dot(halves[k], blocks[k], preferred_element_type=jnp.float32)
        image = (wide[:, :128] + wide[:, 128:]).reshape(32, 8, 128)
        for x in range(32):
            state[k, x] = image[x]


def table(where, increments, mine, other):
    zl = where[0]
    low = zl % 2
    beside = zl + 1 - 2 * low
    for j, run in enumerate((zl, beside, (zl + 2) % 4, (beside + 2) % 4)):
        for n in range(12):
            increments[2 * run + where[1], n] = mine[j][n]
            increments[2 * run + 1 - where[1], n] = other[j][n]


def add_block(state, increments, turn, block):
    for k in range(3):
        for cell in range(4):
            place = 4 * block + cell
            state[k, place] = state[k, place] + increments[turn, 4 * k + cell]


def clear(state):
    for k in range(3):
        for x in range(32):
            state[k, x] = jnp.zeros((8, 128), jnp.float32)


def steps(count, state, halves, blocks, spin, strat):
    def step(i, carry):
        coarse_step(state, halves, blocks, spin[...], strat)
        return carry

    lax.fori_loop(0, count, step, 0)


def plane_kernel(where, spin, blocks, strat, *refs):
    mine, other, (state, part, halves, increments) = refs[:4], refs[4:8], refs[8:]
    core, zh, y = where[1], where[3], where[4]
    table(where, increments, mine, other)
    clear(state)
    block = 4 * zh + y
    add_block(state, increments, 0, block)

    def turn(i, carry):
        coarse_step(state, halves, blocks, spin[...], strat)
        add_block(state, increments, i, block)
        return carry

    lax.fori_loop(1, 8, turn, 0)
    for k in range(3):
        part[k] = state[k, pl.ds(16 * core, 16)]


def power_kernel(where, spin, blocks, strat, before, *refs):
    state, part, halves = refs[-3:]
    for k in range(3):
        for x in range(32):
            state[k, x] = before[k, x]
    steps(8, state, halves, blocks, spin, strat)
    for k in range(3):
        part[k] = state[k, pl.ds(16 * where[1], 16)]


def chain_kernel(where, spin, blocks, strat, last, *refs):
    mine, other, here, there = refs[:4], refs[4:8], refs[10:7:-1], refs[13:10:-1]
    parts, (state, halves, increments) = refs[14:18], refs[18:]
    run, core, row, zh, y = where[0], where[1], where[2], where[3], where[4]
    turns = 2 * run + core
    closing = (row == 0) & (turns == 0)
    table(where, increments, mine, other)
    clear(state)

    @pl.when(closing)
    def _():
        for k in range(3):
            for x in range(32):
                state[k, x] = last[k, x]
        steps(8, state, halves, blocks, spin, strat)

    for j in range(3):

        @pl.when(closing | (row > j))
        def _(j=j):
            for k in range(3):
                for x in range(16):
                    near, far = 16 * core + x, 16 * (1 - core) + x
                    state[k, near] = state[k, near] + here[j][k, x]
                    state[k, far] = state[k, far] + there[j][k, x]

    block = 4 * zh + y

    def turn(i, carry):
        coarse_step(state, halves, blocks, spin[...], strat)
        add_block(state, increments, i, block)
        return carry

    lax.fori_loop(0, turns, turn, 0)

    for j in range(4):
        column = (y + j) % 4
        for half in range(2):
            side = zh if half == 0 else 1 - zh
            for k in range(3):
                for cell in range(4):
                    parts[j][half, 4 * k + cell] = state[k, 4 * (4 * side + column) + cell]


def final_kernel(kept, sent, detail, mean, out, rows):
    for k in range(3):
        for cell in range(4):
            n = 4 * k + cell
            slot = n % 2
            value = kept[n] + sent[n] + mean[k, cell]
            for j in range(4):
                rows[slot, pl.ds(j, 8, stride=4), :] = value
            for j in range(4):
                out[k, 4 * cell + j] = detail[k, 4 * cell + j] + rows[slot]


def call(kernel, outs, scratch, cost=0):
    f32 = jnp.float32

    def run(*args):
        return pl.pallas_call(
            kernel,
            out_shape=[jax.ShapeDtypeStruct(shape, f32) for shape in outs],
            in_specs=[SMEM if arg.dtype == jnp.int32 else VMEM for arg in args],
            cost_estimate=pl.CostEstimate(flops=cost, bytes_accessed=cost // 256, transcendentals=0),
            out_specs=[VMEM] * len(outs),
            scratch_shapes=[pltpu.VMEM(shape, kind) for shape, kind in scratch],
            compiler_params=PARAMS,
        )(*args)

    return run


def swapped(by):
    return [(i, i ^ by) for i in range(4)]


def gathered(part, axis):
    return jnp.stack([part] + [lax.ppermute(part, axis, ring(4, by)) for by in (1, 2, 3)])


def per_device(slice_starts, coriolis, stratification, inverse_blocks):
    f32, bf16 = jnp.float32, jnp.bfloat16
    start = slice_starts[0]
    halves, state = ((3, 256, 256), bf16), ((3, 32, 8, 128), f32)
    increments = ((8, 12, 8, 128), f32)

    own = jnp.concatenate([start.reshape(48, 32, 128), stratification])
    left = lax.ppermute(own, SPACE, ring(8, 1))
    right = lax.ppermute(own, SPACE, ring(8, -1))
    mean, own_strat = call(
        means_kernel, [(3, 4, 8, 128), (4, 8, 128)], [((2, 32, 128), f32)], COST
    )(start, stratification)
    near = gathered(own_strat, "y")
    far = lax.ppermute(near, "zh", ring(2, 1))
    next_mean = lax.ppermute(mean, TM, ring(32, -1))

    spots = [lax.axis_index(name).astype(jnp.int32) for name in ("zl", "c", "x", "zh", "y")]
    where = jnp.stack(spots)
    half_spin = jnp.broadcast_to(0.5 * coriolis[:, None], (32, 128))
    coarse_spin = jnp.broadcast_to(4.0 * coriolis.reshape(8, 4).mean(axis=1)[:, None], (8, 128))
    turned = jnp.swapaxes(inverse_blocks, 1, 2)
    top = lax.reduce_precision(turned, exponent_bits=8, mantissa_bits=7)
    wide = jnp.concatenate([top, turned - top], axis=2).astype(bf16)
    blocks = jnp.concatenate([wide, wide], axis=1)

    detail, increment, strat = call(
        fine_kernel,
        [(3, 16, 32, 128), (12, 8, 128), (32, 8, 128)],
        [((3, WIDE, 32, 128), f32)] * 2
        + [((WIDE, 32, 128), f32), ((4, 32, 128), f32), ((3, 32, 128), f32)],
    )(
        half_spin, where[3:], near, far, blocks, next_mean, own, left, right
    )

    beside = lax.ppermute(increment, "zl", swapped(1))
    mine = [increment, beside]
    mine += [lax.ppermute(part, "zl", swapped(2)) for part in (increment, beside)]
    other = [lax.ppermute(part, "c", ring(2, 1)) for part in mine]
    detail = lax.ppermute(detail, TM, ring(32, 1))
    common = (where, coarse_spin, blocks, strat)
    pair = [state[0], (3, 16, 8, 128)]
    end, part = call(plane_kernel, pair, [halves, increments])(*common, *mine, *other)
    here = [lax.ppermute(part, "x", ring(4, 1))]
    for by in (2, 3):
        end, part = call(power_kernel, pair, [halves], COST)(*common, end, *here[: by - 2])
        here.append(lax.ppermute(part, "x", ring(4, by)))
    there = [lax.ppermute(part, "c", ring(2, 1)) for part in here]
    parts = call(chain_kernel, [(2, 12, 8, 128)] * 4, [state, halves, increments])(
        *common, end, *mine, *other, *here[::-1], *there[::-1]
    )
    total = parts[0]
    for by in (1, 2, 3):
        total = total + lax.ppermute(parts[by], "y", ring(4, by))
    sent = lax.ppermute(total[1], "zh", ring(2, 1))
    (out,) = call(final_kernel, [(3, 16, 32, 128)], [((2, 32, 128), f32)])(
        total[0], sent, detail, mean
    )
    return out[None]


def solution(mesh):
    inner = Mesh(mesh.devices.reshape(SIZES), AXES)
    in_specs = (P(TM, None, SPACE, None, None), P(), P(SPACE, None, None), P())
    out_specs = P(TM, None, SPACE, None, None)
    return jax.shard_map(
        per_device, mesh=inner, in_specs=in_specs, out_specs=out_specs, check_vma=False
    )
```

```python
import jax
import jax.numpy as jnp
from jax import lax
from jax.experimental import pallas as pl
from jax.experimental.pallas import tpu as pltpu
from jax.sharding import Mesh
from jax.sharding import PartitionSpec as P

AXES = ("x", "zl", "c", "zh", "y")
SIZES = (4, 4, 2, 2, 4)
TM = ("x", "zl", "c")
SPACE = ("zh", "y")

VMEM = pl.BlockSpec(memory_space=pltpu.VMEM)
SMEM = pl.BlockSpec(memory_space=pltpu.SMEM)
PARAMS = pltpu.CompilerParams(vmem_limit_bytes=40 * 1024 * 1024)

STEPS = 8
HALO = 16
WIDE = 16 + 2 * HALO
COST = 10**10
DIRECT = 40
UNROLL = (11, 20, 18, 16, 14, 12, 10, 16)


def ring(size, by):
    return [(i, (i + by) % size) for i in range(size)]


def y_next(q):
    return pltpu.roll(q, q.shape[0] - 1, 0)


def y_prev(q):
    return pltpu.roll(q, 1, 0)


def fine_steps(bufs, out, strat, half_spin, weights):
    here_weight, up_weight, down_weight = weights

    def vertical(q):
        above, below = pltpu.roll(q, 127, 1), pltpu.roll(q, 1, 1)
        return here_weight[...] * q + (up_weight[...] * above + down_weight[...] * below)

    for step in range(STEPS):
        src, dst = bufs[step % 2], bufs[(step + 1) % 2]
        reach = 2 * (STEPS - 1 - step)
        first = HALO - reach
        count = 16 + 2 * reach
        back = 0
        if reach == 0:
            dst, back = out, HALO
        unroll = UNROLL[step]

        def zonal(x, src=src):
            u = src[0, x]
            sides = src[0, x + 1] + src[0, x - 1] + (y_next(u) + y_prev(u))
            push = src[2, x + 1] - src[2, x - 1]
            return vertical(u) + (half_spin[...] * src[1, x] - 0.25 * push) + 0.05 * sides

        def chunk(i, carry, src=src, dst=dst, first=first, unroll=unroll, zonal=zonal, back=back):
            before, here = carry
            for k in range(unroll):
                x = first + unroll * i + k
                after = zonal(x + 1)
                dst[0, x - back] = here
                v = src[1, x]
                b = src[2, x]
                b_next, b_prev = y_next(b), y_prev(b)
                v_new = (
                    vertical(v)
                    - (half_spin[...] * here + 0.25 * (b_next - b_prev))
                    + 0.05 * (src[1, x + 1] + src[1, x - 1] + (y_next(v) + y_prev(v)))
                )
                dst[1, x - back] = v_new
                flow = (after - before) + (y_next(v_new) - y_prev(v_new))
                dst[2, x - back] = (
                    vertical(b)
                    - strat[x] * flow
                    + 0.05 * (src[2, x + 1] + src[2, x - 1] + (b_next + b_prev))
                )
                before, here = here, after
            return before, here

        lax.fori_loop(0, count // unroll, chunk, (zonal(first - 1), zonal(first)))


def block_means(rows, cells):
    rows[...] = (cells[0] + cells[1]) + (cells[2] + cells[3])
    parts = [rows[pl.ds(j, 8, stride=4), :] for j in range(4)]
    return ((parts[0] + parts[1]) + (parts[2] + parts[3])) * 0.0625


def means_kernel(start, strat, mean, own_strat, rows):
    for k in range(3):
        for cell in range(4):
            cells = [start[k, 4 * cell + j] for j in range(4)]
            mean[k, cell] = block_means(rows.at[cell % 2], cells)
    for cell in range(4):
        cells = [strat[4 * cell + j] for j in range(4)]
        own_strat[cell] = block_means(rows.at[cell % 2], cells)


def fine_kernel(
    spin, blocks, start, own_strat, left, right, left_near, right_near, left_far, right_far,
    out, one, two, strat, weights,
):
    del blocks
    for k in range(3):
        for x in range(16):
            one[k, 16 + x] = start[k, x]
    for x in range(16):
        strat[16 + x] = 0.25 * own_strat[x]
    for at, direct, near, far in ((0, left, left_near, left_far), (32, right, right_near, right_far)):
        for x in range(DIRECT):
            one[x // 16, at + x % 16] = direct[x]
        for x in range(64 - DIRECT):
            value = near[x] + far[x]
            if DIRECT + x < 48:
                one[2, at + DIRECT + x - 32] = value
            else:
                strat[at + DIRECT + x - 48] = 0.25 * value
    lane = lax.broadcasted_iota(jnp.int32, (32, 128), 1)
    up = jnp.where(lane < 127, 0.15, 0.0).astype(jnp.float32)
    down = jnp.where(lane > 0, 0.15, 0.0).astype(jnp.float32)
    weights[0] = 0.8 - up - down
    weights[1] = up
    weights[2] = down
    fine_steps((one, two), out, strat, spin, [weights.at[n] for n in range(3)])


def split_kernel(place, fine, next_mean, strat_near, strat_far, detail, increment, strat, rows):
    zh, y = place[0], place[1]
    for j in range(4):
        column = (y - j + 4) % 4
        for cell in range(4):
            strat[4 * (4 * zh + column) + cell] = 0.5 * strat_near[j, cell]
            strat[4 * (4 * (1 - zh) + column) + cell] = 0.5 * strat_far[j, cell]
    for k in range(3):
        for cell in range(4):
            slot = (4 * k + cell) % 2
            mean = block_means(rows.at[slot], [fine[k, 4 * cell + j] for j in range(4)])
            increment[4 * k + cell] = mean - next_mean[k, cell]
            for j in range(4):
                rows[2 + slot, pl.ds(j, 8, stride=4), :] = mean
            for j in range(4):
                detail[k, 4 * cell + j] = fine[k, 4 * cell + j] - rows[2 + slot]


def coarse_step(state, halves, blocks, spin, strat):
    zonal, meridional = {}, {}

    def half_zonal(x):
        x = x % 32
        if x not in zonal:
            push = state[2, (x + 1) % 32] - state[2, (x - 1) % 32]
            zonal[x] = state[0, x] + spin * state[1, x] - 0.5 * push
        return zonal[x]

    def half_meridional(x):
        b = state[2, x]
        return state[1, x] - spin * half_zonal(x) - 0.5 * (y_next(b) - y_prev(b))

    def keep(k, pair, value):
        top = value.astype(jnp.bfloat16)
        rest = (value - top.astype(jnp.float32)).astype(jnp.bfloat16)
        halves[k, pl.ds(16 * pair, 16), pl.ds(0, 128)] = top
        halves[k, pl.ds(16 * pair, 16), pl.ds(128, 128)] = rest

    for pair in range(16):
        columns = [[], [], []]
        for x in (2 * pair, 2 * pair + 1):
            u = half_zonal(x)
            v = half_meridional(x)
            flow = (half_zonal(x + 1) - half_zonal(x - 1)) + (y_next(v) - y_prev(v))
            columns[0].append(u)
            columns[1].append(v)
            columns[2].append(state[2, x] - strat[x] * flow)
        for k in range(3):
            keep(k, pair, jnp.concatenate(columns[k], axis=0))
    for k in range(3):
        wide = jnp.dot(halves[k], blocks[k], preferred_element_type=jnp.float32)
        image = (wide[:, :128] + wide[:, 128:]).reshape(32, 8, 128)
        for x in range(32):
            state[k, x] = image[x]


def table(where, increments, mine, other):
    zl = where[0]
    low = zl % 2
    beside = zl + 1 - 2 * low
    for j, run in enumerate((zl, beside, (zl + 2) % 4, (beside + 2) % 4)):
        for n in range(12):
            increments[2 * run + where[1], n] = mine[j][n]
            increments[2 * run + 1 - where[1], n] = other[j][n]


def add_block(state, increments, turn, block):
    for k in range(3):
        for cell in range(4):
            place = 4 * block + cell
            state[k, place] = state[k, place] + increments[turn, 4 * k + cell]


def clear(state):
    for k in range(3):
        for x in range(32):
            state[k, x] = jnp.zeros((8, 128), jnp.float32)


def steps(count, state, halves, blocks, spin, strat):
    def step(i, carry):
        coarse_step(state, halves, blocks, spin[...], strat)
        return carry

    lax.fori_loop(0, count, step, 0)


def plane_kernel(where, spin, blocks, strat, *refs):
    mine, other, (state, part, halves, increments) = refs[:4], refs[4:8], refs[8:]
    core, zh, y = where[1], where[3], where[4]
    table(where, increments, mine, other)
    clear(state)
    block = 4 * zh + y
    add_block(state, increments, 0, block)

    def turn(i, carry):
        coarse_step(state, halves, blocks, spin[...], strat)
        add_block(state, increments, i, block)
        return carry

    lax.fori_loop(1, 8, turn, 0)
    for k in range(3):
        part[k] = state[k, pl.ds(16 * core, 16)]


def power_kernel(where, spin, blocks, strat, before, *refs):
    state, part, halves = refs[-3:]
    for k in range(3):
        for x in range(32):
            state[k, x] = before[k, x]
    steps(8, state, halves, blocks, spin, strat)
    for k in range(3):
        part[k] = state[k, pl.ds(16 * where[1], 16)]


def chain_kernel(where, spin, blocks, strat, last, *refs):
    mine, other, here, there = refs[:4], refs[4:8], refs[10:7:-1], refs[13:10:-1]
    parts, (state, halves, increments) = refs[14:18], refs[18:]
    run, core, row, zh, y = where[0], where[1], where[2], where[3], where[4]
    turns = 2 * run + core
    closing = (row == 0) & (turns == 0)
    table(where, increments, mine, other)
    clear(state)

    @pl.when(closing)
    def _():
        for k in range(3):
            for x in range(32):
                state[k, x] = last[k, x]
        steps(8, state, halves, blocks, spin, strat)

    for j in range(3):

        @pl.when(closing | (row > j))
        def _(j=j):
            for k in range(3):
                for x in range(16):
                    near, far = 16 * core + x, 16 * (1 - core) + x
                    state[k, near] = state[k, near] + here[j][k, x]
                    state[k, far] = state[k, far] + there[j][k, x]

    block = 4 * zh + y

    def turn(i, carry):
        coarse_step(state, halves, blocks, spin[...], strat)
        add_block(state, increments, i, block)
        return carry

    lax.fori_loop(0, turns, turn, 0)

    for j in range(4):
        column = (y + j) % 4
        for half in range(2):
            side = zh if half == 0 else 1 - zh
            for k in range(3):
                for cell in range(4):
                    parts[j][half, 4 * k + cell] = state[k, 4 * (4 * side + column) + cell]


def final_kernel(kept, sent, detail, mean, out, rows):
    for k in range(3):
        for cell in range(4):
            n = 4 * k + cell
            slot = n % 2
            value = kept[n] + sent[n] + mean[k, cell]
            for j in range(4):
                rows[slot, pl.ds(j, 8, stride=4), :] = value
            for j in range(4):
                out[k, 4 * cell + j] = detail[k, 4 * cell + j] + rows[slot]


def call(kernel, outs, scratch, cost=0):
    f32 = jnp.float32

    def run(*args):
        return pl.pallas_call(
            kernel,
            out_shape=[jax.ShapeDtypeStruct(shape, f32) for shape in outs],
            in_specs=[SMEM if arg.dtype == jnp.int32 else VMEM for arg in args],
            cost_estimate=pl.CostEstimate(flops=cost, bytes_accessed=cost // 256, transcendentals=0),
            out_specs=[VMEM] * len(outs),
            scratch_shapes=[pltpu.VMEM(shape, kind) for shape, kind in scratch],
            compiler_params=PARAMS,
        )(*args)

    return run


def swapped(by):
    return [(i, i ^ by) for i in range(4)]


def gathered(part, axis):
    return jnp.stack([part] + [lax.ppermute(part, axis, ring(4, by)) for by in (1, 2, 3)])


def per_device(slice_starts, coriolis, stratification, inverse_blocks):
    f32, bf16 = jnp.float32, jnp.bfloat16
    start = slice_starts[0]
    halves, state = ((3, 256, 256), bf16), ((3, 32, 8, 128), f32)
    increments = ((8, 12, 8, 128), f32)

    layers = start.reshape(48, 32, 128)
    rest = jnp.concatenate([layers[DIRECT:], stratification])
    left_near = lax.ppermute(rest, SPACE, [(s, s + 1) for s in range(8) if s % 4 != 3])
    right_near = lax.ppermute(rest, SPACE, [(s, s - 1) for s in range(8) if s % 4 != 0])
    left = lax.ppermute(layers[:DIRECT], SPACE, ring(8, 1))
    right = lax.ppermute(layers[:DIRECT], SPACE, ring(8, -1))
    left_far = lax.ppermute(right_near, SPACE, [(2, 4), (6, 0)])
    right_far = lax.ppermute(left_near, SPACE, [(1, 7), (5, 3)])
    mean, own_strat = call(
        means_kernel, [(3, 4, 8, 128), (4, 8, 128)], [((2, 32, 128), f32)], COST
    )(start, stratification)
    near = gathered(own_strat, "y")
    far = lax.ppermute(near, "zh", ring(2, 1))
    next_mean = lax.ppermute(mean, TM, ring(32, -1))

    spots = [lax.axis_index(name).astype(jnp.int32) for name in ("zl", "c", "x", "zh", "y")]
    where = jnp.stack(spots)
    half_spin = jnp.broadcast_to(0.5 * coriolis[:, None], (32, 128))
    coarse_spin = jnp.broadcast_to(4.0 * coriolis.reshape(8, 4).mean(axis=1)[:, None], (8, 128))
    turned = jnp.swapaxes(inverse_blocks, 1, 2)
    top = lax.reduce_precision(turned, exponent_bits=8, mantissa_bits=7)
    wide = jnp.concatenate([top, turned - top], axis=2).astype(bf16)
    blocks = jnp.concatenate([wide, wide], axis=1)

    (fine,) = call(
        fine_kernel,
        [(3, 16, 32, 128)],
        [((3, WIDE, 32, 128), f32)] * 2 + [((WIDE, 32, 128), f32), ((3, 32, 128), f32)],
        COST,
    )(
        half_spin, blocks, start, stratification,
        left, right, left_near, right_near, left_far, right_far,
    )
    detail, increment, strat = call(
        split_kernel, [(3, 16, 32, 128), (12, 8, 128), (32, 8, 128)], [((4, 32, 128), f32)]
    )(where[3:], fine, next_mean, near, far)

    beside = lax.ppermute(increment, "zl", swapped(1))
    mine = [increment, beside]
    mine += [lax.ppermute(part, "zl", swapped(2)) for part in (increment, beside)]
    other = [lax.ppermute(part, "c", ring(2, 1)) for part in mine]
    detail = lax.ppermute(detail, TM, ring(32, 1))
    pair = [state[0], (3, 16, 8, 128)]
    common = (where, coarse_spin, blocks, strat)
    end, part = call(plane_kernel, pair, [halves, increments])(*common, *mine, *other)
    here = [lax.ppermute(part, "x", ring(4, 1))]
    for by in (2, 3):
        end, part = call(power_kernel, pair, [halves], COST)(*common, end, *here[: by - 2])
        here.append(lax.ppermute(part, "x", ring(4, by)))
    there = [lax.ppermute(part, "c", ring(2, 1)) for part in here]
    parts = call(chain_kernel, [(2, 12, 8, 128)] * 4, [state, halves, increments])(
        *common, end, *mine, *other, *here[::-1], *there[::-1]
    )
    total = parts[0]
    for by in (1, 2, 3):
        total = total + lax.ppermute(parts[by], "y", ring(4, by))
    sent = lax.ppermute(total[1], "zh", ring(2, 1))
    (out,) = call(final_kernel, [(3, 16, 32, 128)], [((2, 32, 128), f32)])(
        total[0], sent, detail, mean
    )
    return out[None]


def solution(mesh):
    inner = Mesh(mesh.devices.reshape(SIZES), AXES)
    in_specs = (P(TM, None, SPACE, None, None), P(), P(SPACE, None, None), P())
    out_specs = P(TM, None, SPACE, None, None)
    return jax.shard_map(
        per_device, mesh=inner, in_specs=in_specs, out_specs=out_specs, check_vma=False
    )
```

```python
import jax
import jax.numpy as jnp
from jax import lax
from jax.experimental import pallas as pl
from jax.experimental.pallas import tpu as pltpu
from jax.sharding import Mesh
from jax.sharding import PartitionSpec as P

AXES = ("x", "zl", "c", "zh", "y")
SIZES = (4, 4, 2, 2, 4)
TM = ("x", "zl", "c")
SPACE = ("zh", "y")

VMEM = pl.BlockSpec(memory_space=pltpu.VMEM)
SMEM = pl.BlockSpec(memory_space=pltpu.SMEM)
PARAMS = pltpu.CompilerParams(vmem_limit_bytes=40 * 1024 * 1024)

STEPS = 8
HALO = 16
WIDE = 16 + 2 * HALO
COST = 10**10
UNROLL = (11, 20, 18, 16, 14, 12, 10, 16)


def ring(size, by):
    return [(i, (i + by) % size) for i in range(size)]


def y_next(q):
    return pltpu.roll(q, q.shape[0] - 1, 0)


def y_prev(q):
    return pltpu.roll(q, 1, 0)


def fine_steps(bufs, out, strat, half_spin, weights):
    here_weight, up_weight, down_weight = weights

    def vertical(q):
        above, below = pltpu.roll(q, 127, 1), pltpu.roll(q, 1, 1)
        return here_weight[...] * q + (up_weight[...] * above + down_weight[...] * below)

    for step in range(STEPS):
        src, dst = bufs[step % 2], bufs[(step + 1) % 2]
        reach = 2 * (STEPS - 1 - step)
        first = HALO - reach
        count = 16 + 2 * reach
        back = 0
        if reach == 0:
            dst, back = out, HALO
        unroll = UNROLL[step]

        def zonal(x, src=src):
            u = src[0, x]
            sides = src[0, x + 1] + src[0, x - 1] + (y_next(u) + y_prev(u))
            push = src[2, x + 1] - src[2, x - 1]
            return vertical(u) + (half_spin[...] * src[1, x] - 0.25 * push) + 0.05 * sides

        def chunk(i, carry, src=src, dst=dst, first=first, unroll=unroll, zonal=zonal, back=back):
            before, here = carry
            for k in range(unroll):
                x = first + unroll * i + k
                after = zonal(x + 1)
                dst[0, x - back] = here
                v = src[1, x]
                b = src[2, x]
                b_next, b_prev = y_next(b), y_prev(b)
                v_new = (
                    vertical(v)
                    - (half_spin[...] * here + 0.25 * (b_next - b_prev))
                    + 0.05 * (src[1, x + 1] + src[1, x - 1] + (y_next(v) + y_prev(v)))
                )
                dst[1, x - back] = v_new
                flow = (after - before) + (y_next(v_new) - y_prev(v_new))
                dst[2, x - back] = (
                    vertical(b)
                    - strat[x] * flow
                    + 0.05 * (src[2, x + 1] + src[2, x - 1] + (b_next + b_prev))
                )
                before, here = here, after
            return before, here

        lax.fori_loop(0, count // unroll, chunk, (zonal(first - 1), zonal(first)))


def block_means(rows, cells):
    rows[...] = (cells[0] + cells[1]) + (cells[2] + cells[3])
    parts = [rows[pl.ds(j, 8, stride=4), :] for j in range(4)]
    return ((parts[0] + parts[1]) + (parts[2] + parts[3])) * 0.0625


def means_kernel(start, mean, rows):
    for k in range(3):
        for cell in range(4):
            cells = [start[k, 4 * cell + j] for j in range(4)]
            mean[k, cell] = block_means(rows.at[cell % 2], cells)


def strat_means_kernel(left, own, right, means, rows):
    for n, block in enumerate((left, own, right)):
        for cell in range(4):
            cells = [block[4 * cell + j] for j in range(4)]
            means[n, cell] = block_means(rows.at[cell % 2], cells)


def columns_kernel(place, own, partner, columns):
    y = place[1]
    for middle, means in ((y, own), ((y + 2) % 4, partner)):
        for n in range(3):

            @pl.when((middle + n >= 1) & (middle + n <= 4))
            def _(middle=middle, means=means, n=n):
                columns[middle + n - 1] = means[n]


def fine_kernel(
    spin, blocks, own_strat, left_near, right_near, left_far, right_far, start, left, right,
    out, one, two, strat, weights,
):
    del blocks
    for k in range(3):
        for x in range(16):
            one[k, x] = left[k, x]
            one[k, 16 + x] = start[k, x]
            one[k, 32 + x] = right[k, x]
    for x in range(16):
        strat[x] = 0.25 * (left_near[x] + left_far[x])
        strat[16 + x] = 0.25 * own_strat[x]
        strat[32 + x] = 0.25 * (right_near[x] + right_far[x])
    lane = lax.broadcasted_iota(jnp.int32, (32, 128), 1)
    up = jnp.where(lane < 127, 0.15, 0.0).astype(jnp.float32)
    down = jnp.where(lane > 0, 0.15, 0.0).astype(jnp.float32)
    weights[0] = 0.8 - up - down
    weights[1] = up
    weights[2] = down
    fine_steps((one, two), out, strat, spin, [weights.at[n] for n in range(3)])


def split_kernel(place, fine, next_mean, strat_near, strat_far, detail, increment, strat, rows):
    zh = place[0]
    for column in range(4):
        for cell in range(4):
            strat[16 * zh + 4 * column + cell] = 0.5 * strat_near[column, cell]
            strat[16 * (1 - zh) + 4 * column + cell] = 0.5 * strat_far[column, cell]
    for k in range(3):
        for cell in range(4):
            slot = (4 * k + cell) % 2
            mean = block_means(rows.at[slot], [fine[k, 4 * cell + j] for j in range(4)])
            increment[4 * k + cell] = mean - next_mean[k, cell]
            for j in range(4):
                rows[2 + slot, pl.ds(j, 8, stride=4), :] = mean
            for j in range(4):
                detail[k, 4 * cell + j] = fine[k, 4 * cell + j] - rows[2 + slot]


def coarse_step(state, halves, blocks, spin, strat):
    zonal, meridional = {}, {}

    def half_zonal(x):
        x = x % 32
        if x not in zonal:
            push = state[2, (x + 1) % 32] - state[2, (x - 1) % 32]
            zonal[x] = state[0, x] + spin * state[1, x] - 0.5 * push
        return zonal[x]

    def half_meridional(x):
        b = state[2, x]
        return state[1, x] - spin * half_zonal(x) - 0.5 * (y_next(b) - y_prev(b))

    def keep(k, pair, value):
        top = value.astype(jnp.bfloat16)
        rest = (value - top.astype(jnp.float32)).astype(jnp.bfloat16)
        halves[k, pl.ds(16 * pair, 16), pl.ds(0, 128)] = top
        halves[k, pl.ds(16 * pair, 16), pl.ds(128, 128)] = rest

    for pair in range(16):
        columns = [[], [], []]
        for x in (2 * pair, 2 * pair + 1):
            u = half_zonal(x)
            v = half_meridional(x)
            flow = (half_zonal(x + 1) - half_zonal(x - 1)) + (y_next(v) - y_prev(v))
            columns[0].append(u)
            columns[1].append(v)
            columns[2].append(state[2, x] - strat[x] * flow)
        for k in range(3):
            keep(k, pair, jnp.concatenate(columns[k], axis=0))
    for k in range(3):
        wide = jnp.dot(halves[k], blocks[k], preferred_element_type=jnp.float32)
        image = (wide[:, :128] + wide[:, 128:]).reshape(32, 8, 128)
        for x in range(32):
            state[k, x] = image[x]


def table(where, increments, mine, other):
    zl = where[0]
    low = zl % 2
    beside = zl + 1 - 2 * low
    for j, run in enumerate((zl, beside, (zl + 2) % 4, (beside + 2) % 4)):
        for n in range(12):
            increments[2 * run + where[1], n] = mine[j][n]
            increments[2 * run + 1 - where[1], n] = other[j][n]


def add_block(state, increments, turn, block):
    for k in range(3):
        for cell in range(4):
            place = 4 * block + cell
            state[k, place] = state[k, place] + increments[turn, 4 * k + cell]


def clear(state):
    for k in range(3):
        for x in range(32):
            state[k, x] = jnp.zeros((8, 128), jnp.float32)


def steps(count, state, halves, blocks, spin, strat):
    def step(i, carry):
        coarse_step(state, halves, blocks, spin[...], strat)
        return carry

    lax.fori_loop(0, count, step, 0)


def plane_kernel(where, spin, blocks, strat, *refs):
    mine, other, (state, part, halves, increments) = refs[:4], refs[4:8], refs[8:]
    core, zh, y = where[1], where[3], where[4]
    table(where, increments, mine, other)
    clear(state)
    block = 4 * zh + y
    add_block(state, increments, 0, block)

    def turn(i, carry):
        coarse_step(state, halves, blocks, spin[...], strat)
        add_block(state, increments, i, block)
        return carry

    lax.fori_loop(1, 8, turn, 0)
    for k in range(3):
        part[k] = state[k, pl.ds(16 * core, 16)]


def chain_kernel(where, spin, blocks, strat, end, *refs):
    mine, other, here, there = refs[:4], refs[4:8], refs[8:11], refs[11:14]
    parts, (ends, state, halves, increments) = refs[14:18], refs[18:]
    run, core, row, zh, y = where[0], where[1], where[2], where[3], where[4]
    turns = 2 * run + core
    groups = jnp.where((row == 0) & (turns == 0), 4, row)
    table(where, increments, mine, other)
    for k in range(3):
        for x in range(32):
            ends[0, k, x] = end[k, x]
    for j in range(3):
        for k in range(3):
            ends[j + 1, k, pl.ds(16 * core, 16)] = here[j][k]
            ends[j + 1, k, pl.ds(16 * (1 - core), 16)] = there[j][k]
    clear(state)

    def group(g, carry):
        @pl.when(g > 0)
        def _():
            steps(8, state, halves, blocks, spin, strat)

        place = (row - g + 4) % 4
        for k in range(3):
            for x in range(32):
                state[k, x] = state[k, x] + ends[place, k, x]
        return carry

    lax.fori_loop(0, groups, group, 0)
    block = 4 * zh + y

    def turn(i, carry):
        coarse_step(state, halves, blocks, spin[...], strat)
        add_block(state, increments, i, block)
        return carry

    lax.fori_loop(0, turns, turn, 0)

    for j in range(4):
        column = (y + j) % 4
        for half in range(2):
            side = zh if half == 0 else 1 - zh
            for k in range(3):
                for cell in range(4):
                    parts[j][half, 4 * k + cell] = state[k, 4 * (4 * side + column) + cell]


def final_kernel(kept, sent, detail, mean, out, rows):
    for k in range(3):
        for cell in range(4):
            n = 4 * k + cell
            slot = n % 2
            value = kept[n] + sent[n] + mean[k, cell]
            for j in range(4):
                rows[slot, pl.ds(j, 8, stride=4), :] = value
            for j in range(4):
                out[k, 4 * cell + j] = detail[k, 4 * cell + j] + rows[slot]


def call(kernel, outs, scratch, cost=0):
    f32 = jnp.float32

    def run(*args):
        return pl.pallas_call(
            kernel,
            out_shape=[jax.ShapeDtypeStruct(shape, f32) for shape in outs],
            in_specs=[SMEM if arg.dtype == jnp.int32 else VMEM for arg in args],
            cost_estimate=pl.CostEstimate(flops=cost, bytes_accessed=cost // 256, transcendentals=0),
            out_specs=[VMEM] * len(outs),
            scratch_shapes=[pltpu.VMEM(shape, kind) for shape, kind in scratch],
            compiler_params=PARAMS,
        )(*args)

    return run


def swapped(by):
    return [(i, i ^ by) for i in range(4)]


def per_device(slice_starts, coriolis, stratification, inverse_blocks):
    f32, bf16 = jnp.float32, jnp.bfloat16
    start = slice_starts[0]
    halves, state = ((3, 256, 256), bf16), ((3, 32, 8, 128), f32)
    increments = ((8, 12, 8, 128), f32)

    left = lax.ppermute(start, SPACE, ring(8, 1))
    right = lax.ppermute(start, SPACE, ring(8, -1))
    left_near = lax.ppermute(stratification, SPACE, [(s, s + 1) for s in range(8) if s % 4 != 3])
    right_near = lax.ppermute(stratification, SPACE, [(s, s - 1) for s in range(8) if s % 4 != 0])
    left_far = lax.ppermute(right_near, SPACE, [(2, 4), (6, 0)])
    right_far = lax.ppermute(left_near, SPACE, [(1, 7), (5, 3)])
    (mean,) = call(means_kernel, [(3, 4, 8, 128)], [((2, 32, 128), f32)], COST)(start)
    next_mean = lax.ppermute(mean, TM, ring(32, -1))

    spots = [lax.axis_index(name).astype(jnp.int32) for name in ("zl", "c", "x", "zh", "y")]
    where = jnp.stack(spots)
    (three,) = call(strat_means_kernel, [(3, 4, 8, 128)], [((2, 32, 128), f32)])(
        left_near, stratification, right_near
    )
    partner = lax.ppermute(three, "y", swapped(2))
    (near,) = call(columns_kernel, [(4, 4, 8, 128)], [])(where[3:], three, partner)
    far = lax.ppermute(near, "zh", ring(2, 1))
    half_spin = jnp.broadcast_to(0.5 * coriolis[:, None], (32, 128))
    coarse_spin = jnp.broadcast_to(4.0 * coriolis.reshape(8, 4).mean(axis=1)[:, None], (8, 128))
    turned = jnp.swapaxes(inverse_blocks, 1, 2)
    top = lax.reduce_precision(turned, exponent_bits=8, mantissa_bits=7)
    wide = jnp.concatenate([top, turned - top], axis=2).astype(bf16)
    blocks = jnp.concatenate([wide, wide], axis=1)

    (fine,) = call(
        fine_kernel,
        [(3, 16, 32, 128)],
        [((3, WIDE, 32, 128), f32)] * 2 + [((WIDE, 32, 128), f32), ((3, 32, 128), f32)],
        COST,
    )(
        half_spin, blocks, stratification,
        left_near, right_near, left_far, right_far, start, left, right,
    )
    detail, increment, strat = call(
        split_kernel, [(3, 16, 32, 128), (12, 8, 128), (32, 8, 128)], [((4, 32, 128), f32)]
    )(where[3:], fine, next_mean, near, far)

    beside = lax.ppermute(increment, "zl", swapped(1))
    mine = [increment, beside]
    mine += [lax.ppermute(part, "zl", swapped(2)) for part in (increment, beside)]
    other = [lax.ppermute(part, "c", ring(2, 1)) for part in mine]
    detail = lax.ppermute(detail, TM, ring(32, 1))
    pair = [state[0], (3, 16, 8, 128)]
    common = (where, coarse_spin, blocks, strat)
    end, part = call(plane_kernel, pair, [halves, increments])(*common, *mine, *other)
    here = [lax.ppermute(part, "x", ring(4, by)) for by in (1, 2, 3)]
    there = [lax.ppermute(part, "c", ring(2, 1)) for part in here]
    parts = call(
        chain_kernel, [(2, 12, 8, 128)] * 4, [((4, 3, 32, 8, 128), f32), state, halves, increments]
    )(*common, end, *mine, *other, *here, *there)
    total = parts[0]
    for by in (1, 2, 3):
        total = total + lax.ppermute(parts[by], "y", ring(4, by))
    sent = lax.ppermute(total[1], "zh", ring(2, 1))
    (out,) = call(final_kernel, [(3, 16, 32, 128)], [((2, 32, 128), f32)])(
        total[0], sent, detail, mean
    )
    return out[None]


def solution(mesh):
    inner = Mesh(mesh.devices.reshape(SIZES), AXES)
    in_specs = (P(TM, None, SPACE, None, None), P(), P(SPACE, None, None), P())
    out_specs = P(TM, None, SPACE, None, None)
    return jax.shard_map(
        per_device, mesh=inner, in_specs=in_specs, out_specs=out_specs, check_vma=False
    )
```

```python
import jax
import jax.numpy as jnp
from jax import lax
from jax.experimental import pallas as pl
from jax.experimental.pallas import tpu as pltpu
from jax.sharding import Mesh
from jax.sharding import PartitionSpec as P

AXES = ("x", "zl", "c", "zh", "y")
SIZES = (4, 4, 2, 2, 4)
TM = ("x", "zl", "c")
SPACE = ("zh", "y")

VMEM = pl.BlockSpec(memory_space=pltpu.VMEM)
SMEM = pl.BlockSpec(memory_space=pltpu.SMEM)
PARAMS = pltpu.CompilerParams(vmem_limit_bytes=40 * 1024 * 1024)

STEPS = 8
HALO = 16
WIDE = 16 + 2 * HALO
COST = 10**10
DIRECT = 36
UNROLL = (11, 20, 18, 16, 14, 12, 10, 16)


def ring(size, by):
    return [(i, (i + by) % size) for i in range(size)]


def y_next(q):
    return pltpu.roll(q, q.shape[0] - 1, 0)


def y_prev(q):
    return pltpu.roll(q, 1, 0)


def fine_steps(bufs, out, strat, half_spin, weights):
    here_weight, up_weight, down_weight = weights

    def vertical(q):
        above, below = pltpu.roll(q, 127, 1), pltpu.roll(q, 1, 1)
        return here_weight[...] * q + (up_weight[...] * above + down_weight[...] * below)

    for step in range(STEPS):
        src, dst = bufs[step % 2], bufs[(step + 1) % 2]
        reach = 2 * (STEPS - 1 - step)
        first = HALO - reach
        count = 16 + 2 * reach
        back = 0
        if reach == 0:
            dst, back = out, HALO
        unroll = UNROLL[step]

        def zonal(x, src=src):
            u = src[0, x]
            sides = src[0, x + 1] + src[0, x - 1] + (y_next(u) + y_prev(u))
            push = src[2, x + 1] - src[2, x - 1]
            return vertical(u) + (half_spin[...] * src[1, x] - 0.25 * push) + 0.05 * sides

        def chunk(i, carry, src=src, dst=dst, first=first, unroll=unroll, zonal=zonal, back=back):
            before, here = carry
            for k in range(unroll):
                x = first + unroll * i + k
                after = zonal(x + 1)
                dst[0, x - back] = here
                v = src[1, x]
                b = src[2, x]
                b_next, b_prev = y_next(b), y_prev(b)
                v_new = (
                    vertical(v)
                    - (half_spin[...] * here + 0.25 * (b_next - b_prev))
                    + 0.05 * (src[1, x + 1] + src[1, x - 1] + (y_next(v) + y_prev(v)))
                )
                dst[1, x - back] = v_new
                flow = (after - before) + (y_next(v_new) - y_prev(v_new))
                dst[2, x - back] = (
                    vertical(b)
                    - strat[x] * flow
                    + 0.05 * (src[2, x + 1] + src[2, x - 1] + (b_next + b_prev))
                )
                before, here = here, after
            return before, here

        lax.fori_loop(0, count // unroll, chunk, (zonal(first - 1), zonal(first)))


def block_means(rows, cells):
    rows[...] = (cells[0] + cells[1]) + (cells[2] + cells[3])
    parts = [rows[pl.ds(j, 8, stride=4), :] for j in range(4)]
    return ((parts[0] + parts[1]) + (parts[2] + parts[3])) * 0.0625


def means_kernel(start, mean, rows):
    for k in range(3):
        for cell in range(4):
            cells = [start[k, 4 * cell + j] for j in range(4)]
            mean[k, cell] = block_means(rows.at[cell % 2], cells)


def pack_kernel(layers, strat, direct, rest, sems):
    copies = [
        pltpu.make_async_copy(layers.at[pl.ds(DIRECT, 48 - DIRECT)], rest.at[pl.ds(0, 48 - DIRECT)], sems.at[0]),
        pltpu.make_async_copy(strat, rest.at[pl.ds(48 - DIRECT, 16)], sems.at[1]),
        pltpu.make_async_copy(layers.at[pl.ds(0, DIRECT)], direct, sems.at[2]),
    ]
    for copy in copies:
        copy.start()
    for copy in copies:
        copy.wait()


def strat_means_kernel(left, own, right, means, rows):
    for n, (block, at) in enumerate(((left, 48 - DIRECT), (own, 0), (right, 48 - DIRECT))):
        for cell in range(4):
            cells = [block[at + 4 * cell + j] for j in range(4)]
            means[n, cell] = block_means(rows.at[cell % 2], cells)


def columns_kernel(place, own, partner, columns):
    y = place[1]
    for middle, means in ((y, own), ((y + 2) % 4, partner)):
        for n in range(3):

            @pl.when((middle + n >= 1) & (middle + n <= 4))
            def _(middle=middle, means=means, n=n):
                columns[middle + n - 1] = means[n]


def fine_kernel(
    spin, blocks, own_strat, left_near, right_near, left_far, right_far, start, left, right,
    out, one, two, strat, weights,
):
    del blocks
    for k in range(3):
        for x in range(16):
            one[k, 16 + x] = start[k, x]
    for x in range(16):
        strat[16 + x] = 0.25 * own_strat[x]
    for at, direct, near, far in ((0, left, left_near, left_far), (32, right, right_near, right_far)):
        for n in range(DIRECT):
            one[n // 16, at + n % 16] = direct[n]
        for n in range(64 - DIRECT):
            value = near[n] + far[n]
            if DIRECT + n < 48:
                one[2, at + DIRECT + n - 32] = value
            else:
                strat[at + DIRECT + n - 48] = 0.25 * value
    lane = lax.broadcasted_iota(jnp.int32, (32, 128), 1)
    up = jnp.where(lane < 127, 0.15, 0.0).astype(jnp.float32)
    down = jnp.where(lane > 0, 0.15, 0.0).astype(jnp.float32)
    weights[0] = 0.8 - up - down
    weights[1] = up
    weights[2] = down
    fine_steps((one, two), out, strat, spin, [weights.at[n] for n in range(3)])


def split_kernel(place, fine, next_mean, strat_near, strat_far, detail, increment, strat, rows):
    zh = place[0]
    for column in range(4):
        for cell in range(4):
            strat[16 * zh + 4 * column + cell] = 0.5 * strat_near[column, cell]
            strat[16 * (1 - zh) + 4 * column + cell] = 0.5 * strat_far[column, cell]
    for k in range(3):
        for cell in range(4):
            slot = (4 * k + cell) % 2
            mean = block_means(rows.at[slot], [fine[k, 4 * cell + j] for j in range(4)])
            increment[4 * k + cell] = mean - next_mean[k, cell]
            for j in range(4):
                rows[2 + slot, pl.ds(j, 8, stride=4), :] = mean
            for j in range(4):
                detail[k, 4 * cell + j] = fine[k, 4 * cell + j] - rows[2 + slot]


def coarse_step(state, halves, blocks, spin, strat):
    zonal, meridional = {}, {}

    def half_zonal(x):
        x = x % 32
        if x not in zonal:
            push = state[2, (x + 1) % 32] - state[2, (x - 1) % 32]
            zonal[x] = state[0, x] + spin * state[1, x] - 0.5 * push
        return zonal[x]

    def half_meridional(x):
        b = state[2, x]
        return state[1, x] - spin * half_zonal(x) - 0.5 * (y_next(b) - y_prev(b))

    def keep(k, pair, value):
        top = value.astype(jnp.bfloat16)
        rest = (value - top.astype(jnp.float32)).astype(jnp.bfloat16)
        halves[k, pl.ds(16 * pair, 16), pl.ds(0, 128)] = top
        halves[k, pl.ds(16 * pair, 16), pl.ds(128, 128)] = rest

    for pair in range(16):
        columns = [[], [], []]
        for x in (2 * pair, 2 * pair + 1):
            u = half_zonal(x)
            v = half_meridional(x)
            flow = (half_zonal(x + 1) - half_zonal(x - 1)) + (y_next(v) - y_prev(v))
            columns[0].append(u)
            columns[1].append(v)
            columns[2].append(state[2, x] - strat[x] * flow)
        for k in range(3):
            keep(k, pair, jnp.concatenate(columns[k], axis=0))
    for k in range(3):
        wide = jnp.dot(halves[k], blocks[k], preferred_element_type=jnp.float32)
        image = (wide[:, :128] + wide[:, 128:]).reshape(32, 8, 128)
        for x in range(32):
            state[k, x] = image[x]


def table(where, increments, mine, other):
    zl = where[0]
    low = zl % 2
    beside = zl + 1 - 2 * low
    for j, run in enumerate((zl, beside, (zl + 2) % 4, (beside + 2) % 4)):
        for n in range(12):
            increments[2 * run + where[1], n] = mine[j][n]
            increments[2 * run + 1 - where[1], n] = other[j][n]


def add_block(state, increments, turn, block):
    for k in range(3):
        for cell in range(4):
            place = 4 * block + cell
            state[k, place] = state[k, place] + increments[turn, 4 * k + cell]


def clear(state):
    for k in range(3):
        for x in range(32):
            state[k, x] = jnp.zeros((8, 128), jnp.float32)


def steps(count, state, halves, blocks, spin, strat):
    def step(i, carry):
        coarse_step(state, halves, blocks, spin[...], strat)
        return carry

    lax.fori_loop(0, count, step, 0)


def plane_kernel(where, spin, blocks, strat, *refs):
    mine, other, (state, part, halves, increments) = refs[:4], refs[4:8], refs[8:]
    core, zh, y = where[1], where[3], where[4]
    table(where, increments, mine, other)
    clear(state)
    block = 4 * zh + y
    add_block(state, increments, 0, block)

    def turn(i, carry):
        coarse_step(state, halves, blocks, spin[...], strat)
        add_block(state, increments, i, block)
        return carry

    lax.fori_loop(1, 8, turn, 0)
    for k in range(3):
        part[k] = state[k, pl.ds(16 * core, 16)]


def chain_kernel(where, spin, blocks, strat, end, *refs):
    mine, other, here, there = refs[:4], refs[4:8], refs[8:11], refs[11:14]
    parts, (ends, state, halves, increments) = refs[14:18], refs[18:]
    run, core, row, zh, y = where[0], where[1], where[2], where[3], where[4]
    turns = 2 * run + core
    groups = jnp.where((row == 0) & (turns == 0), 4, row)
    table(where, increments, mine, other)
    for k in range(3):
        for x in range(32):
            ends[0, k, x] = end[k, x]
    for j in range(3):
        for k in range(3):
            ends[j + 1, k, pl.ds(16 * core, 16)] = here[j][k]
            ends[j + 1, k, pl.ds(16 * (1 - core), 16)] = there[j][k]
    clear(state)

    def group(g, carry):
        @pl.when(g > 0)
        def _():
            steps(8, state, halves, blocks, spin, strat)

        place = (row - g + 4) % 4
        for k in range(3):
            for x in range(32):
                state[k, x] = state[k, x] + ends[place, k, x]
        return carry

    lax.fori_loop(0, groups, group, 0)
    block = 4 * zh + y

    def turn(i, carry):
        coarse_step(state, halves, blocks, spin[...], strat)
        add_block(state, increments, i, block)
        return carry

    lax.fori_loop(0, turns, turn, 0)

    for j in range(4):
        column = (y + j) % 4
        for half in range(2):
            side = zh if half == 0 else 1 - zh
            for k in range(3):
                for cell in range(4):
                    parts[j][half, 4 * k + cell] = state[k, 4 * (4 * side + column) + cell]


def final_kernel(kept, sent, detail, mean, out, rows):
    for k in range(3):
        for cell in range(4):
            n = 4 * k + cell
            slot = n % 2
            value = kept[n] + sent[n] + mean[k, cell]
            for j in range(4):
                rows[slot, pl.ds(j, 8, stride=4), :] = value
            for j in range(4):
                out[k, 4 * cell + j] = detail[k, 4 * cell + j] + rows[slot]


def call(kernel, outs, scratch, cost=0):
    f32 = jnp.float32

    def run(*args):
        return pl.pallas_call(
            kernel,
            out_shape=[jax.ShapeDtypeStruct(shape, f32) for shape in outs],
            in_specs=[SMEM if arg.dtype == jnp.int32 else VMEM for arg in args],
            cost_estimate=pl.CostEstimate(flops=cost, bytes_accessed=cost // 256, transcendentals=0),
            out_specs=[VMEM] * len(outs),
            scratch_shapes=[pltpu.VMEM(shape, kind) for shape, kind in scratch],
            compiler_params=PARAMS,
        )(*args)

    return run


def swapped(by):
    return [(i, i ^ by) for i in range(4)]


def plane_pairs(by):
    return [
        (4 * x + zl, (4 * (x + by) + zl) % 16)
        for x in range(4)
        for zl in range(4)
        if x + by < 4 or (x + by == 4 and zl == 0)
    ]


def per_device(slice_starts, coriolis, stratification, inverse_blocks):
    f32, bf16 = jnp.float32, jnp.bfloat16
    start = slice_starts[0]
    halves, state = ((3, 256, 256), bf16), ((3, 32, 8, 128), f32)
    increments = ((8, 12, 8, 128), f32)

    anywhere = pl.BlockSpec(memory_space=pl.ANY)
    direct, rest = pl.pallas_call(
        pack_kernel,
        out_shape=[jax.ShapeDtypeStruct((n, 32, 128), f32) for n in (DIRECT, 64 - DIRECT)],
        in_specs=[anywhere] * 2,
        out_specs=[anywhere] * 2,
        scratch_shapes=[pltpu.SemaphoreType.DMA((3,))],
        compiler_params=pltpu.CompilerParams(vmem_limit_bytes=60 * 1024 * 1024),
    )(start.reshape(48, 32, 128), stratification)
    left_near = lax.ppermute(rest, SPACE, [(s, s + 1) for s in range(8) if s % 4 != 3])
    right_near = lax.ppermute(rest, SPACE, [(s, s - 1) for s in range(8) if s % 4 != 0])
    left = lax.ppermute(direct, SPACE, ring(8, 1))
    right = lax.ppermute(direct, SPACE, ring(8, -1))
    left_far = lax.ppermute(right_near, SPACE, [(2, 4), (6, 0)])
    right_far = lax.ppermute(left_near, SPACE, [(1, 7), (5, 3)])
    (mean,) = call(means_kernel, [(3, 4, 8, 128)], [((2, 32, 128), f32)], COST)(start)
    next_mean = lax.ppermute(mean, TM, ring(32, -1))

    spots = [lax.axis_index(name).astype(jnp.int32) for name in ("zl", "c", "x", "zh", "y")]
    where = jnp.stack(spots)
    (three,) = call(strat_means_kernel, [(3, 4, 8, 128)], [((2, 32, 128), f32)])(
        left_near, stratification, right_near
    )
    partner = lax.ppermute(three, "y", swapped(2))
    (near,) = call(columns_kernel, [(4, 4, 8, 128)], [])(where[3:], three, partner)
    far = lax.ppermute(near, "zh", ring(2, 1))
    half_spin = jnp.broadcast_to(0.5 * coriolis[:, None], (32, 128))
    coarse_spin = jnp.broadcast_to(4.0 * coriolis.reshape(8, 4).mean(axis=1)[:, None], (8, 128))
    turned = jnp.swapaxes(inverse_blocks, 1, 2)
    top = lax.reduce_precision(turned, exponent_bits=8, mantissa_bits=7)
    wide = jnp.concatenate([top, turned - top], axis=2).astype(bf16)
    blocks = jnp.concatenate([wide, wide], axis=1)

    (fine,) = call(
        fine_kernel,
        [(3, 16, 32, 128)],
        [((3, WIDE, 32, 128), f32)] * 2 + [((WIDE, 32, 128), f32), ((3, 32, 128), f32)],
        COST,
    )(
        half_spin, blocks, stratification,
        left_near, right_near, left_far, right_far, start, left, right,
    )
    detail, increment, strat = call(
        split_kernel, [(3, 16, 32, 128), (12, 8, 128), (32, 8, 128)], [((4, 32, 128), f32)]
    )(where[3:], fine, next_mean, near, far)

    beside = lax.ppermute(increment, "zl", swapped(1))
    mine = [increment, beside]
    mine += [lax.ppermute(part, "zl", swapped(2)) for part in (increment, beside)]
    other = [lax.ppermute(part, "c", ring(2, 1)) for part in mine]
    detail = lax.ppermute(detail, TM, ring(32, 1))
    pair = [state[0], (3, 16, 8, 128)]
    common = (where, coarse_spin, blocks, strat)
    end, part = call(plane_kernel, pair, [halves, increments])(*common, *mine, *other)
    here = [lax.ppermute(part, ("x", "zl"), plane_pairs(by)) for by in (1, 2, 3)]
    there = [lax.ppermute(part, "c", ring(2, 1)) for part in here]
    parts = call(
        chain_kernel, [(2, 12, 8, 128)] * 4, [((4, 3, 32, 8, 128), f32), state, halves, increments]
    )(*common, end, *mine, *other, *here, *there)
    total = parts[0]
    for by in (1, 2, 3):
        total = total + lax.ppermute(parts[by], "y", ring(4, by))
    sent = lax.ppermute(total[1], "zh", ring(2, 1))
    (out,) = call(final_kernel, [(3, 16, 32, 128)], [((2, 32, 128), f32)])(
        total[0], sent, detail, mean
    )
    return out[None]


def solution(mesh):
    inner = Mesh(mesh.devices.reshape(SIZES), AXES)
    in_specs = (P(TM, None, SPACE, None, None), P(), P(SPACE, None, None), P())
    out_specs = P(TM, None, SPACE, None, None)
    return jax.shard_map(
        per_device, mesh=inner, in_specs=in_specs, out_specs=out_specs, check_vma=False
    )
```

```python
import jax
import jax.numpy as jnp
from jax import lax
from jax.experimental import pallas as pl
from jax.experimental.pallas import tpu as pltpu
from jax.sharding import Mesh
from jax.sharding import PartitionSpec as P

AXES = ("x", "zl", "c", "zh", "y")
SIZES = (4, 4, 2, 2, 4)
TM = ("x", "zl", "c")
SPACE = ("zh", "y")

VMEM = pl.BlockSpec(memory_space=pltpu.VMEM)
SMEM = pl.BlockSpec(memory_space=pltpu.SMEM)
PARAMS = pltpu.CompilerParams(vmem_limit_bytes=40 * 1024 * 1024)

STEPS = 8
HALO = 16
WIDE = 16 + 2 * HALO
COST = 10**10
UNROLL = (11, 20, 18, 16, 14, 12, 10, 16)


def ring(size, by):
    return [(i, (i + by) % size) for i in range(size)]


def y_next(q):
    return pltpu.roll(q, q.shape[0] - 1, 0)


def y_prev(q):
    return pltpu.roll(q, 1, 0)


def fine_steps(bufs, out, strat, half_spin, weights):
    here_weight, up_weight, down_weight = weights

    def vertical(q):
        above, below = pltpu.roll(q, 127, 1), pltpu.roll(q, 1, 1)
        return here_weight[...] * q + (up_weight[...] * above + down_weight[...] * below)

    for step in range(STEPS):
        src, dst = bufs[step % 2], bufs[(step + 1) % 2]
        reach = 2 * (STEPS - 1 - step)
        first = HALO - reach
        count = 16 + 2 * reach
        back = 0
        if reach == 0:
            dst, back = out, HALO
        unroll = UNROLL[step]

        def zonal(x, src=src):
            u = src[0, x]
            sides = src[0, x + 1] + src[0, x - 1] + (y_next(u) + y_prev(u))
            push = src[2, x + 1] - src[2, x - 1]
            return vertical(u) + (half_spin[...] * src[1, x] - 0.25 * push) + 0.05 * sides

        def chunk(i, carry, src=src, dst=dst, first=first, unroll=unroll, zonal=zonal, back=back):
            before, here = carry
            for k in range(unroll):
                x = first + unroll * i + k
                after = zonal(x + 1)
                dst[0, x - back] = here
                v = src[1, x]
                b = src[2, x]
                b_next, b_prev = y_next(b), y_prev(b)
                v_new = (
                    vertical(v)
                    - (half_spin[...] * here + 0.25 * (b_next - b_prev))
                    + 0.05 * (src[1, x + 1] + src[1, x - 1] + (y_next(v) + y_prev(v)))
                )
                dst[1, x - back] = v_new
                flow = (after - before) + (y_next(v_new) - y_prev(v_new))
                dst[2, x - back] = (
                    vertical(b)
                    - strat[x] * flow
                    + 0.05 * (src[2, x + 1] + src[2, x - 1] + (b_next + b_prev))
                )
                before, here = here, after
            return before, here

        lax.fori_loop(0, count // unroll, chunk, (zonal(first - 1), zonal(first)))


def block_means(rows, cells):
    rows[...] = (cells[0] + cells[1]) + (cells[2] + cells[3])
    parts = [rows[pl.ds(j, 8, stride=4), :] for j in range(4)]
    return ((parts[0] + parts[1]) + (parts[2] + parts[3])) * 0.0625


def means_kernel(start, mean, rows):
    for k in range(3):
        for cell in range(4):
            cells = [start[k, 4 * cell + j] for j in range(4)]
            mean[k, cell] = block_means(rows.at[cell % 2], cells)


def strat_means_kernel(even, own, odd, means, rows):
    for n, block in enumerate((even, own, odd)):
        for cell in range(4):
            cells = [block[4 * cell + j] for j in range(4)]
            means[n, cell] = block_means(rows.at[cell % 2], cells)


def columns_kernel(place, own, partner, columns):
    y = place[1]
    for column, means in ((y, own), ((y + 2) % 4, partner)):
        columns[column + 1 - 2 * (column % 2)] = means[0]
        columns[column] = means[1]

        @pl.when((column == 1) | (column == 2))
        def _(column=column, means=means):
            columns[3 - column] = means[2]


def fine_kernel(
    spin, blocks, place, own_strat, even_strat, odd_strat, hopped_strat, start, odd, even,
    out, one, two, strat, weights,
):
    del blocks
    at_odd = 32 * (place[1] % 2)
    at_even = 32 - at_odd
    for k in range(3):
        for x in range(16):
            one[k, 16 + x] = start[k, x]
            one[k, at_even + x] = even[k, x]
            one[k, at_odd + x] = odd[k, x]
    for x in range(16):
        strat[16 + x] = 0.25 * own_strat[x]
        strat[at_even + x] = 0.25 * even_strat[x]
        strat[at_odd + x] = 0.25 * (odd_strat[x] + hopped_strat[x])
    lane = lax.broadcasted_iota(jnp.int32, (32, 128), 1)
    up = jnp.where(lane < 127, 0.15, 0.0).astype(jnp.float32)
    down = jnp.where(lane > 0, 0.15, 0.0).astype(jnp.float32)
    weights[0] = 0.8 - up - down
    weights[1] = up
    weights[2] = down
    fine_steps((one, two), out, strat, spin, [weights.at[n] for n in range(3)])


def split_kernel(place, fine, next_mean, strat_near, strat_far, detail, increment, strat, rows):
    zh = place[0]
    for column in range(4):
        for cell in range(4):
            strat[16 * zh + 4 * column + cell] = 0.5 * strat_near[column, cell]
            strat[16 * (1 - zh) + 4 * column + cell] = 0.5 * strat_far[column, cell]
    for k in range(3):
        for cell in range(4):
            slot = (4 * k + cell) % 2
            mean = block_means(rows.at[slot], [fine[k, 4 * cell + j] for j in range(4)])
            increment[4 * k + cell] = mean - next_mean[k, cell]
            for j in range(4):
                rows[2 + slot, pl.ds(j, 8, stride=4), :] = mean
            for j in range(4):
                detail[k, 4 * cell + j] = fine[k, 4 * cell + j] - rows[2 + slot]


def coarse_step(state, halves, blocks, spin, strat):
    zonal, meridional = {}, {}

    def half_zonal(x):
        x = x % 32
        if x not in zonal:
            push = state[2, (x + 1) % 32] - state[2, (x - 1) % 32]
            zonal[x] = state[0, x] + spin * state[1, x] - 0.5 * push
        return zonal[x]

    def half_meridional(x):
        b = state[2, x]
        return state[1, x] - spin * half_zonal(x) - 0.5 * (y_next(b) - y_prev(b))

    def keep(k, pair, value):
        top = value.astype(jnp.bfloat16)
        rest = (value - top.astype(jnp.float32)).astype(jnp.bfloat16)
        halves[k, pl.ds(16 * pair, 16), pl.ds(0, 128)] = top
        halves[k, pl.ds(16 * pair, 16), pl.ds(128, 128)] = rest

    for pair in range(16):
        columns = [[], [], []]
        for x in (2 * pair, 2 * pair + 1):
            u = half_zonal(x)
            v = half_meridional(x)
            flow = (half_zonal(x + 1) - half_zonal(x - 1)) + (y_next(v) - y_prev(v))
            columns[0].append(u)
            columns[1].append(v)
            columns[2].append(state[2, x] - strat[x] * flow)
        for k in range(3):
            keep(k, pair, jnp.concatenate(columns[k], axis=0))
    for k in range(3):
        wide = jnp.dot(halves[k], blocks[k], preferred_element_type=jnp.float32)
        image = (wide[:, :128] + wide[:, 128:]).reshape(32, 8, 128)
        for x in range(32):
            state[k, x] = image[x]


def table(where, increments, mine, other):
    zl = where[0]
    low = zl % 2
    beside = zl + 1 - 2 * low
    for j, run in enumerate((zl, beside, (zl + 2) % 4, (beside + 2) % 4)):
        for n in range(12):
            increments[2 * run + where[1], n] = mine[j][n]
            increments[2 * run + 1 - where[1], n] = other[j][n]


def add_block(state, increments, turn, block):
    for k in range(3):
        for cell in range(4):
            place = 4 * block + cell
            state[k, place] = state[k, place] + increments[turn, 4 * k + cell]


def clear(state):
    for k in range(3):
        for x in range(32):
            state[k, x] = jnp.zeros((8, 128), jnp.float32)


def steps(count, state, halves, blocks, spin, strat):
    def step(i, carry):
        coarse_step(state, halves, blocks, spin[...], strat)
        return carry

    lax.fori_loop(0, count, step, 0)


def plane_kernel(where, spin, blocks, strat, *refs):
    mine, other, (state, part, halves, increments) = refs[:4], refs[4:8], refs[8:]
    core, zh, y = where[1], where[3], where[4]
    table(where, increments, mine, other)
    clear(state)
    block = 4 * zh + y
    add_block(state, increments, 0, block)

    def turn(i, carry):
        coarse_step(state, halves, blocks, spin[...], strat)
        add_block(state, increments, i, block)
        return carry

    lax.fori_loop(1, 8, turn, 0)
    for k in range(3):
        part[k] = state[k, pl.ds(16 * core, 16)]


def chain_kernel(where, spin, blocks, strat, end, *refs):
    mine, other, here, there = refs[:4], refs[4:8], refs[8:11], refs[11:14]
    parts, (ends, state, halves, increments) = refs[14:18], refs[18:]
    run, core, row, zh, y = where[0], where[1], where[2], where[3], where[4]
    turns = 2 * run + core
    groups = jnp.where((row == 0) & (turns == 0), 4, row)
    table(where, increments, mine, other)
    for k in range(3):
        for x in range(32):
            ends[row, k, x] = end[k, x]
    for j in range(3):
        plane = row ^ (j + 1)
        for k in range(3):
            ends[plane, k, pl.ds(16 * core, 16)] = here[j][k]
            ends[plane, k, pl.ds(16 * (1 - core), 16)] = there[j][k]
    clear(state)

    def group(g, carry):
        @pl.when(g > 0)
        def _():
            steps(8, state, halves, blocks, spin, strat)

        for k in range(3):
            for x in range(32):
                state[k, x] = state[k, x] + ends[g, k, x]
        return carry

    lax.fori_loop(0, groups, group, 0)
    block = 4 * zh + y

    def turn(i, carry):
        coarse_step(state, halves, blocks, spin[...], strat)
        add_block(state, increments, i, block)
        return carry

    lax.fori_loop(0, turns, turn, 0)

    for j in range(4):
        column = y ^ j
        for half in range(2):
            side = zh if half == 0 else 1 - zh
            for k in range(3):
                for cell in range(4):
                    parts[j][half, 4 * k + cell] = state[k, 4 * (4 * side + column) + cell]


def final_kernel(kept, sent, detail, mean, out, rows):
    for k in range(3):
        for cell in range(4):
            n = 4 * k + cell
            slot = n % 2
            value = kept[n] + sent[n] + mean[k, cell]
            for j in range(4):
                rows[slot, pl.ds(j, 8, stride=4), :] = value
            for j in range(4):
                out[k, 4 * cell + j] = detail[k, 4 * cell + j] + rows[slot]


def call(kernel, outs, scratch, cost=0):
    f32 = jnp.float32

    def run(*args):
        return pl.pallas_call(
            kernel,
            out_shape=[jax.ShapeDtypeStruct(shape, f32) for shape in outs],
            in_specs=[SMEM if arg.dtype == jnp.int32 else VMEM for arg in args],
            cost_estimate=pl.CostEstimate(flops=cost, bytes_accessed=cost // 256, transcendentals=0),
            out_specs=[VMEM] * len(outs),
            scratch_shapes=[pltpu.VMEM(shape, kind) for shape, kind in scratch],
            compiler_params=PARAMS,
        )(*args)

    return run


def swapped(by):
    return [(i, i ^ by) for i in range(4)]


def per_device(slice_starts, coriolis, stratification, inverse_blocks):
    f32, bf16 = jnp.float32, jnp.bfloat16
    start = slice_starts[0]
    halves, state = ((3, 256, 256), bf16), ((3, 32, 8, 128), f32)
    increments = ((8, 12, 8, 128), f32)

    even_edges = [(s, s ^ 1) for s in range(8)]
    odd_edges = [(s, (s + 1 if s % 2 else s - 1) % 8) for s in range(8)]
    odd = lax.ppermute(start, SPACE, odd_edges)
    even = lax.ppermute(start, SPACE, even_edges)
    even_strat = lax.ppermute(stratification, SPACE, even_edges)
    odd_strat = lax.ppermute(stratification, SPACE, [(1, 2), (2, 1), (5, 6), (6, 5)])
    relayed = lax.ppermute(even_strat, SPACE, [(1, 5), (5, 1), (2, 6), (6, 2)])
    hopped_strat = lax.ppermute(relayed, SPACE, [(1, 3), (5, 7), (2, 0), (6, 4)])
    (mean,) = call(means_kernel, [(3, 4, 8, 128)], [((2, 32, 128), f32)], COST)(start)
    next_mean = lax.ppermute(mean, TM, ring(32, -1))

    spots = [lax.axis_index(name).astype(jnp.int32) for name in ("zl", "c", "x", "zh", "y")]
    where = jnp.stack(spots)
    (three,) = call(strat_means_kernel, [(3, 4, 8, 128)], [((2, 32, 128), f32)])(
        even_strat, stratification, odd_strat
    )
    partner = lax.ppermute(three, "y", swapped(2))
    (near,) = call(columns_kernel, [(4, 4, 8, 128)], [])(where[3:], three, partner)
    far = lax.ppermute(near, "zh", ring(2, 1))
    half_spin = jnp.broadcast_to(0.5 * coriolis[:, None], (32, 128))
    coarse_spin = jnp.broadcast_to(4.0 * coriolis.reshape(8, 4).mean(axis=1)[:, None], (8, 128))
    turned = jnp.swapaxes(inverse_blocks, 1, 2)
    top = lax.reduce_precision(turned, exponent_bits=8, mantissa_bits=7)
    wide = jnp.concatenate([top, turned - top], axis=2).astype(bf16)
    blocks = jnp.concatenate([wide, wide], axis=1)

    (fine,) = call(
        fine_kernel,
        [(3, 16, 32, 128)],
        [((3, WIDE, 32, 128), f32)] * 2 + [((WIDE, 32, 128), f32), ((3, 32, 128), f32)],
        COST,
    )(
        half_spin, blocks, where[3:], stratification, even_strat, odd_strat, hopped_strat,
        start, odd, even,
    )
    detail, increment, strat = call(
        split_kernel, [(3, 16, 32, 128), (12, 8, 128), (32, 8, 128)], [((4, 32, 128), f32)]
    )(where[3:], fine, next_mean, near, far)

    beside = lax.ppermute(increment, "zl", swapped(1))
    mine = [increment, beside]
    mine += [lax.ppermute(part, "zl", swapped(2)) for part in (increment, beside)]
    other = [lax.ppermute(part, "c", ring(2, 1)) for part in mine]
    detail = lax.ppermute(detail, TM, ring(32, 1))
    pair = [state[0], (3, 16, 8, 128)]
    common = (where, coarse_spin, blocks, strat)
    end, part = call(plane_kernel, pair, [halves, increments])(*common, *mine, *other)
    here = [lax.ppermute(part, "x", swapped(by)) for by in (1, 2, 3)]
    there = [lax.ppermute(part, "c", ring(2, 1)) for part in here]
    parts = call(
        chain_kernel, [(2, 12, 8, 128)] * 4, [((4, 3, 32, 8, 128), f32), state, halves, increments]
    )(*common, end, *mine, *other, *here, *there)
    total = parts[0]
    for by in (1, 2, 3):
        total = total + lax.ppermute(parts[by], "y", swapped(by))
    sent = lax.ppermute(total[1], "zh", ring(2, 1))
    (out,) = call(final_kernel, [(3, 16, 32, 128)], [((2, 32, 128), f32)])(
        total[0], sent, detail, mean
    )
    return out[None]


def solution(mesh):
    inner = Mesh(mesh.devices.reshape(SIZES), AXES)
    in_specs = (P(TM, None, SPACE, None, None), P(), P(SPACE, None, None), P())
    out_specs = P(TM, None, SPACE, None, None)
    return jax.shard_map(
        per_device, mesh=inner, in_specs=in_specs, out_specs=out_specs, check_vma=False
    )
```

```python
import jax
import jax.numpy as jnp
from jax import lax
from jax.experimental import pallas as pl
from jax.experimental.pallas import tpu as pltpu
from jax.sharding import Mesh
from jax.sharding import PartitionSpec as P

AXES = ("x", "zl", "c", "zh", "y")
SIZES = (4, 4, 2, 2, 4)
TM = ("x", "zl", "c")
SPACE = ("zh", "y")

VMEM = pl.BlockSpec(memory_space=pltpu.VMEM)
SMEM = pl.BlockSpec(memory_space=pltpu.SMEM)
PARAMS = pltpu.CompilerParams(vmem_limit_bytes=40 * 1024 * 1024)

STEPS = 8
HALO = 16
WIDE = 16 + 2 * HALO
COST = 10**10
UNROLL = (11, 20, 18, 16, 14, 12, 10, 16)


def ring(size, by):
    return [(i, (i + by) % size) for i in range(size)]


def y_next(q):
    return pltpu.roll(q, q.shape[0] - 1, 0)


def y_prev(q):
    return pltpu.roll(q, 1, 0)


def fine_steps(bufs, out, strat, half_spin, weights):
    here_weight, up_weight, down_weight = weights

    def vertical(q):
        above, below = pltpu.roll(q, 127, 1), pltpu.roll(q, 1, 1)
        return here_weight[...] * q + (up_weight[...] * above + down_weight[...] * below)

    for step in range(STEPS):
        src, dst = bufs[step % 2], bufs[(step + 1) % 2]
        reach = 2 * (STEPS - 1 - step)
        first = HALO - reach
        count = 16 + 2 * reach
        back = 0
        if reach == 0:
            dst, back = out, HALO
        unroll = UNROLL[step]

        def zonal(x, src=src):
            u = src[0, x]
            sides = src[0, x + 1] + src[0, x - 1] + (y_next(u) + y_prev(u))
            push = src[2, x + 1] - src[2, x - 1]
            return vertical(u) + (half_spin[...] * src[1, x] - 0.25 * push) + 0.05 * sides

        def chunk(i, carry, src=src, dst=dst, first=first, unroll=unroll, zonal=zonal, back=back):
            before, here = carry
            for k in range(unroll):
                x = first + unroll * i + k
                after = zonal(x + 1)
                dst[0, x - back] = here
                v = src[1, x]
                b = src[2, x]
                b_next, b_prev = y_next(b), y_prev(b)
                v_new = (
                    vertical(v)
                    - (half_spin[...] * here + 0.25 * (b_next - b_prev))
                    + 0.05 * (src[1, x + 1] + src[1, x - 1] + (y_next(v) + y_prev(v)))
                )
                dst[1, x - back] = v_new
                flow = (after - before) + (y_next(v_new) - y_prev(v_new))
                dst[2, x - back] = (
                    vertical(b)
                    - strat[x] * flow
                    + 0.05 * (src[2, x + 1] + src[2, x - 1] + (b_next + b_prev))
                )
                before, here = here, after
            return before, here

        lax.fori_loop(0, count // unroll, chunk, (zonal(first - 1), zonal(first)))


def block_means(rows, cells):
    rows[...] = (cells[0] + cells[1]) + (cells[2] + cells[3])
    parts = [rows[pl.ds(j, 8, stride=4), :] for j in range(4)]
    return ((parts[0] + parts[1]) + (parts[2] + parts[3])) * 0.0625


def means_kernel(start, mean, rows):
    for k in range(3):
        for cell in range(4):
            cells = [start[k, 4 * cell + j] for j in range(4)]
            mean[k, cell] = block_means(rows.at[cell % 2], cells)


def strat_means_kernel(even, own, means, rows):
    for n, block in enumerate((own, even)):
        for cell in range(4):
            cells = [block[4 * cell + j] for j in range(4)]
            means[n, cell] = block_means(rows.at[cell % 2], cells)


def columns_kernel(place, own, across, forwarded, columns):
    y = place[1]
    beside = y + 1 - 2 * (y % 2)
    columns[y] = own[0]
    columns[beside] = own[1]
    inner = (y == 1) | (y == 2)
    near = jnp.where(y < 2, 2, 1)
    far = jnp.where(y < 2, 3, 0)

    @pl.when(inner)
    def _():
        columns[near] = across[0]
        columns[far] = across[1]

    @pl.when(jnp.logical_not(inner))
    def _():
        columns[near] = forwarded[0]
        columns[far] = forwarded[1]


def fine_kernel(
    spin, blocks, place, own_strat, even_strat, odd_strat, hopped_strat, start, odd, even,
    out, one, two, strat, weights,
):
    del blocks
    at_odd = 32 * (place[1] % 2)
    at_even = 32 - at_odd
    for k in range(3):
        for x in range(16):
            one[k, 16 + x] = start[k, x]
            one[k, at_even + x] = even[k, x]
            one[k, at_odd + x] = odd[k, x]
    for x in range(16):
        strat[16 + x] = 0.25 * own_strat[x]
        strat[at_even + x] = 0.25 * even_strat[x]
        strat[at_odd + x] = 0.25 * (odd_strat[x] + hopped_strat[x])
    lane = lax.broadcasted_iota(jnp.int32, (32, 128), 1)
    up = jnp.where(lane < 127, 0.15, 0.0).astype(jnp.float32)
    down = jnp.where(lane > 0, 0.15, 0.0).astype(jnp.float32)
    weights[0] = 0.8 - up - down
    weights[1] = up
    weights[2] = down
    fine_steps((one, two), out, strat, spin, [weights.at[n] for n in range(3)])


def split_kernel(place, fine, next_mean, strat_near, strat_far, detail, increment, strat, rows):
    zh = place[0]
    for column in range(4):
        for cell in range(4):
            strat[16 * zh + 4 * column + cell] = 0.5 * strat_near[column, cell]
            strat[16 * (1 - zh) + 4 * column + cell] = 0.5 * strat_far[column, cell]
    for k in range(3):
        for cell in range(4):
            slot = (4 * k + cell) % 2
            mean = block_means(rows.at[slot], [fine[k, 4 * cell + j] for j in range(4)])
            increment[4 * k + cell] = mean - next_mean[k, cell]
            for j in range(4):
                rows[2 + slot, pl.ds(j, 8, stride=4), :] = mean
            for j in range(4):
                detail[k, 4 * cell + j] = fine[k, 4 * cell + j] - rows[2 + slot]


def coarse_step(state, halves, blocks, spin, strat):
    zonal, meridional = {}, {}

    def half_zonal(x):
        x = x % 32
        if x not in zonal:
            push = state[2, (x + 1) % 32] - state[2, (x - 1) % 32]
            zonal[x] = state[0, x] + spin * state[1, x] - 0.5 * push
        return zonal[x]

    def half_meridional(x):
        b = state[2, x]
        return state[1, x] - spin * half_zonal(x) - 0.5 * (y_next(b) - y_prev(b))

    def keep(k, pair, value):
        top = value.astype(jnp.bfloat16)
        rest = (value - top.astype(jnp.float32)).astype(jnp.bfloat16)
        halves[k, pl.ds(16 * pair, 16), pl.ds(0, 128)] = top
        halves[k, pl.ds(16 * pair, 16), pl.ds(128, 128)] = rest

    for pair in range(16):
        columns = [[], [], []]
        for x in (2 * pair, 2 * pair + 1):
            u = half_zonal(x)
            v = half_meridional(x)
            flow = (half_zonal(x + 1) - half_zonal(x - 1)) + (y_next(v) - y_prev(v))
            columns[0].append(u)
            columns[1].append(v)
            columns[2].append(state[2, x] - strat[x] * flow)
        for k in range(3):
            keep(k, pair, jnp.concatenate(columns[k], axis=0))
    for k in range(3):
        wide = jnp.dot(halves[k], blocks[k], preferred_element_type=jnp.float32)
        image = (wide[:, :128] + wide[:, 128:]).reshape(32, 8, 128)
        for x in range(32):
            state[k, x] = image[x]


def table(where, increments, mine, other):
    zl = where[0]
    low = zl % 2
    beside = zl + 1 - 2 * low
    for j, run in enumerate((zl, beside, (zl + 2) % 4, (beside + 2) % 4)):
        for n in range(12):
            increments[2 * run + where[1], n] = mine[j][n]
            increments[2 * run + 1 - where[1], n] = other[j][n]


def add_block(state, increments, turn, block):
    for k in range(3):
        for cell in range(4):
            place = 4 * block + cell
            state[k, place] = state[k, place] + increments[turn, 4 * k + cell]


def clear(state):
    for k in range(3):
        for x in range(32):
            state[k, x] = jnp.zeros((8, 128), jnp.float32)


def steps(count, state, halves, blocks, spin, strat):
    def step(i, carry):
        coarse_step(state, halves, blocks, spin[...], strat)
        return carry

    lax.fori_loop(0, count, step, 0)


def plane_kernel(where, spin, blocks, strat, *refs):
    mine, other, (state, part, halves, increments) = refs[:4], refs[4:8], refs[8:]
    core, zh, y = where[1], where[3], where[4]
    table(where, increments, mine, other)
    clear(state)
    block = 4 * zh + y
    add_block(state, increments, 0, block)

    def turn(i, carry):
        coarse_step(state, halves, blocks, spin[...], strat)
        add_block(state, increments, i, block)
        return carry

    lax.fori_loop(1, 8, turn, 0)
    for k in range(3):
        part[k] = state[k, pl.ds(16 * core, 16)]


def chain_kernel(where, spin, blocks, strat, end, *refs):
    mine, other, here, there = refs[:4], refs[4:8], refs[8:11], refs[11:14]
    parts, (ends, state, halves, increments) = refs[14:18], refs[18:]
    run, core, row, zh, y = where[0], where[1], where[2], where[3], where[4]
    turns = 2 * run + core
    groups = jnp.where((row == 0) & (turns == 0), 4, row)
    table(where, increments, mine, other)
    for k in range(3):
        for x in range(32):
            ends[row, k, x] = end[k, x]
    for j in range(3):
        plane = (row + 3 - j) % 4
        for k in range(3):
            ends[plane, k, pl.ds(16 * core, 16)] = here[j][k]
            ends[plane, k, pl.ds(16 * (1 - core), 16)] = there[j][k]
    clear(state)

    def group(g, carry):
        @pl.when(g > 0)
        def _():
            steps(8, state, halves, blocks, spin, strat)

        for k in range(3):
            for x in range(32):
                state[k, x] = state[k, x] + ends[g, k, x]
        return carry

    lax.fori_loop(0, groups, group, 0)
    block = 4 * zh + y

    def turn(i, carry):
        coarse_step(state, halves, blocks, spin[...], strat)
        add_block(state, increments, i, block)
        return carry

    lax.fori_loop(0, turns, turn, 0)

    for j in range(4):
        column = y ^ j
        for half in range(2):
            side = zh if half == 0 else 1 - zh
            for k in range(3):
                for cell in range(4):
                    parts[j][half, 4 * k + cell] = state[k, 4 * (4 * side + column) + cell]


def final_kernel(kept, sent, detail, mean, out, rows):
    for k in range(3):
        for cell in range(4):
            n = 4 * k + cell
            slot = n % 2
            value = kept[n] + sent[n] + mean[k, cell]
            for j in range(4):
                rows[slot, pl.ds(j, 8, stride=4), :] = value
            for j in range(4):
                out[k, 4 * cell + j] = detail[k, 4 * cell + j] + rows[slot]


def call(kernel, outs, scratch, cost=0):
    f32 = jnp.float32

    def run(*args):
        return pl.pallas_call(
            kernel,
            out_shape=[jax.ShapeDtypeStruct(shape, f32) for shape in outs],
            in_specs=[SMEM if arg.dtype == jnp.int32 else VMEM for arg in args],
            cost_estimate=pl.CostEstimate(flops=cost, bytes_accessed=cost // 256, transcendentals=0),
            out_specs=[VMEM] * len(outs),
            scratch_shapes=[pltpu.VMEM(shape, kind) for shape, kind in scratch],
            compiler_params=PARAMS,
        )(*args)

    return run


def swapped(by):
    return [(i, i ^ by) for i in range(4)]


def per_device(slice_starts, coriolis, stratification, inverse_blocks):
    f32, bf16 = jnp.float32, jnp.bfloat16
    start = slice_starts[0]
    halves, state = ((3, 256, 256), bf16), ((3, 32, 8, 128), f32)
    increments = ((8, 12, 8, 128), f32)

    even_edges = [(s, s ^ 1) for s in range(8)]
    odd_edges = [(s, (s + 1 if s % 2 else s - 1) % 8) for s in range(8)]
    odd = lax.ppermute(start, SPACE, odd_edges)
    even = lax.ppermute(start, SPACE, even_edges)
    even_strat = lax.ppermute(stratification, SPACE, even_edges)
    odd_strat = lax.ppermute(stratification, SPACE, [(1, 2), (2, 1), (5, 6), (6, 5)])
    relayed = lax.ppermute(even_strat, SPACE, [(1, 5), (5, 1), (2, 6), (6, 2)])
    hopped_strat = lax.ppermute(relayed, SPACE, [(1, 3), (5, 7), (2, 0), (6, 4)])
    (mean,) = call(means_kernel, [(3, 4, 8, 128)], [((2, 32, 128), f32)], COST)(start)
    next_mean = lax.ppermute(mean, TM, ring(32, -1))

    spots = [lax.axis_index(name).astype(jnp.int32) for name in ("zl", "c", "x", "zh", "y")]
    where = jnp.stack(spots)
    (pair_means,) = call(strat_means_kernel, [(2, 4, 8, 128)], [((2, 32, 128), f32)])(
        even_strat, stratification
    )
    across = lax.ppermute(pair_means, "y", [(1, 2), (2, 1)])
    forwarded = lax.ppermute(across, "y", swapped(1))
    (near,) = call(columns_kernel, [(4, 4, 8, 128)], [])(
        where[3:], pair_means, across, forwarded
    )
    far = lax.ppermute(near, "zh", ring(2, 1))
    half_spin = jnp.broadcast_to(0.5 * coriolis[:, None], (32, 128))
    coarse_spin = jnp.broadcast_to(4.0 * coriolis.reshape(8, 4).mean(axis=1)[:, None], (8, 128))
    turned = jnp.swapaxes(inverse_blocks, 1, 2)
    top = lax.reduce_precision(turned, exponent_bits=8, mantissa_bits=7)
    wide = jnp.concatenate([top, turned - top], axis=2).astype(bf16)
    blocks = jnp.concatenate([wide, wide], axis=1)

    (fine,) = call(
        fine_kernel,
        [(3, 16, 32, 128)],
        [((3, WIDE, 32, 128), f32)] * 2 + [((WIDE, 32, 128), f32), ((3, 32, 128), f32)],
        COST,
    )(
        half_spin, blocks, where[3:], stratification, even_strat, odd_strat, hopped_strat,
        start, odd, even,
    )
    detail, increment, strat = call(
        split_kernel, [(3, 16, 32, 128), (12, 8, 128), (32, 8, 128)], [((4, 32, 128), f32)]
    )(where[3:], fine, next_mean, near, far)

    beside = lax.ppermute(increment, "zl", swapped(1))
    mine = [increment, beside]
    mine += [lax.ppermute(part, "zl", swapped(2)) for part in (increment, beside)]
    other = [lax.ppermute(part, "c", ring(2, 1)) for part in mine]
    detail = lax.ppermute(detail, TM, ring(32, 1))
    pair = [state[0], (3, 16, 8, 128)]
    common = (where, coarse_spin, blocks, strat)
    end, part = call(plane_kernel, pair, [halves, increments])(*common, *mine, *other)
    here = [lax.ppermute(part, "x", ring(4, by)) for by in (1, 2, 3)]
    there = [lax.ppermute(part, "c", ring(2, 1)) for part in here]
    parts = call(
        chain_kernel, [(2, 12, 8, 128)] * 4, [((4, 3, 32, 8, 128), f32), state, halves, increments]
    )(*common, end, *mine, *other, *here, *there)
    total = parts[0]
    for by in (1, 2, 3):
        total = total + lax.ppermute(parts[by], "y", swapped(by))
    sent = lax.ppermute(total[1], "zh", ring(2, 1))
    (out,) = call(final_kernel, [(3, 16, 32, 128)], [((2, 32, 128), f32)])(
        total[0], sent, detail, mean
    )
    return out[None]


def solution(mesh):
    inner = Mesh(mesh.devices.reshape(SIZES), AXES)
    in_specs = (P(TM, None, SPACE, None, None), P(), P(SPACE, None, None), P())
    out_specs = P(TM, None, SPACE, None, None)
    return jax.shard_map(
        per_device, mesh=inner, in_specs=in_specs, out_specs=out_specs, check_vma=False
    )
```

```python
import jax
import jax.numpy as jnp
from jax import lax
from jax.experimental import pallas as pl
from jax.experimental.pallas import tpu as pltpu
from jax.sharding import Mesh
from jax.sharding import PartitionSpec as P

AXES = ("x", "zl", "c", "zh", "y")
SIZES = (4, 4, 2, 2, 4)
TM = ("x", "zl", "c")
SPACE = ("zh", "y")

VMEM = pl.BlockSpec(memory_space=pltpu.VMEM)
SMEM = pl.BlockSpec(memory_space=pltpu.SMEM)
PARAMS = pltpu.CompilerParams(vmem_limit_bytes=40 * 1024 * 1024)

STEPS = 8
COST = 10**10
EVEN_UNROLL = (14, 12, 20, 16, 12, 8, 4)


def ring(size, by):
    return [(i, (i + by) % size) for i in range(size)]


def y_next(q):
    return pltpu.roll(q, q.shape[0] - 1, 0)


def y_prev(q):
    return pltpu.roll(q, 1, 0)


def fine_step(src, dst, strat, half_spin, weights, sign, first, count, unroll, place=None):
    here_weight, up_weight, down_weight = weights
    quarter = 0.25 * sign
    place = place or (lambda x: x)

    def vertical(q):
        above, below = pltpu.roll(q, 127, 1), pltpu.roll(q, 1, 1)
        return here_weight[...] * q + (up_weight[...] * above + down_weight[...] * below)

    def zonal(x):
        u = src[0, x]
        sides = src[0, x + 1] + src[0, x - 1] + (y_next(u) + y_prev(u))
        push = src[2, x + 1] - src[2, x - 1]
        return vertical(u) + (half_spin[...] * src[1, x] - quarter * push) + 0.05 * sides

    def chunk(i, carry):
        before, here = carry
        for k in range(unroll):
            x = first + unroll * i + k
            after = zonal(x + 1)
            dst[0, place(x)] = here
            v = src[1, x]
            b = src[2, x]
            b_next, b_prev = y_next(b), y_prev(b)
            v_new = (
                vertical(v)
                - (half_spin[...] * here + 0.25 * (b_next - b_prev))
                + 0.05 * (src[1, x + 1] + src[1, x - 1] + (y_next(v) + y_prev(v)))
            )
            dst[1, place(x)] = v_new
            flow = sign * (after - before) + (y_next(v_new) - y_prev(v_new))
            dst[2, place(x)] = (
                vertical(b)
                - strat[x] * flow
                + 0.05 * (src[2, x + 1] + src[2, x - 1] + (b_next + b_prev))
            )
            before, here = here, after
        return before, here

    lax.fori_loop(0, count // unroll, chunk, (zonal(first - 1), zonal(first)))


def fill_weights(weights):
    lane = lax.broadcasted_iota(jnp.int32, (32, 128), 1)
    up = jnp.where(lane < 127, 0.15, 0.0).astype(jnp.float32)
    down = jnp.where(lane > 0, 0.15, 0.0).astype(jnp.float32)
    weights[0] = 0.8 - up - down
    weights[1] = up
    weights[2] = down
    return [weights.at[n] for n in range(3)]


def turned_round(place):
    reverse = place[1] % 2

    def cell(i):
        return i * (1 - 2 * reverse) + 15 * reverse

    return cell, (1 - 2 * reverse).astype(jnp.float32)


def even_side_kernel(
    spin, blocks, place, own_strat, even_strat, start, even, edges, one, two, strat, weights
):
    del blocks
    cell, sign = turned_round(place)
    for x in range(16):
        strat[cell(x)] = 0.25 * own_strat[x]
        strat[16 + cell(x)] = 0.25 * even_strat[x]
        for k in range(3):
            one[k, cell(x)] = start[k, x]
            one[k, 16 + cell(x)] = even[k, x]
    listed = fill_weights(weights)
    bufs = (one, two)
    for level in range(STEPS):
        src = bufs[level % 2]
        for k in range(3):
            for x in range(4):
                edges[level, k, x] = src[k, 2 * level + x]
        if level < STEPS - 1:
            fine_step(
                src, bufs[(level + 1) % 2], strat, spin, listed, sign,
                2 * level + 2, 28 - 4 * level, EVEN_UNROLL[level],
            )


def odd_side_kernel(
    spin, place, own_strat, odd_strat, hopped_strat, edges, odd, out, one, two, strat, weights
):
    cell, sign = turned_round(place)
    for x in range(16):
        strat[cell(x)] = 0.25 * (odd_strat[x] + hopped_strat[x])
        strat[16 + cell(x)] = 0.25 * own_strat[x]
        for k in range(3):
            one[k, cell(x)] = odd[k, x]
    listed = fill_weights(weights)
    bufs = (one, two)
    for level in range(STEPS):
        src, dst, where = bufs[level % 2], bufs[(level + 1) % 2], None
        if level == STEPS - 1:
            dst, where = out, lambda x: cell(x - 16)
        for k in range(3):
            for x in range(4):
                src[k, 16 + 2 * level + x] = edges[level, k, x]
        fine_step(src, dst, strat, spin, listed, sign, 2 * level + 2, 16, 16, where)


def block_means(rows, cells):
    rows[...] = (cells[0] + cells[1]) + (cells[2] + cells[3])
    parts = [rows[pl.ds(j, 8, stride=4), :] for j in range(4)]
    return ((parts[0] + parts[1]) + (parts[2] + parts[3])) * 0.0625


def means_kernel(start, mean, rows):
    for k in range(3):
        for cell in range(4):
            cells = [start[k, 4 * cell + j] for j in range(4)]
            mean[k, cell] = block_means(rows.at[cell % 2], cells)


def strat_means_kernel(even, own, means, rows):
    for n, block in enumerate((own, even)):
        for cell in range(4):
            cells = [block[4 * cell + j] for j in range(4)]
            means[n, cell] = block_means(rows.at[cell % 2], cells)


def columns_kernel(place, own, across, forwarded, columns):
    y = place[1]
    beside = y + 1 - 2 * (y % 2)
    columns[y] = own[0]
    columns[beside] = own[1]
    inner = (y == 1) | (y == 2)
    near = jnp.where(y < 2, 2, 1)
    far = jnp.where(y < 2, 3, 0)

    @pl.when(inner)
    def _():
        columns[near] = across[0]
        columns[far] = across[1]

    @pl.when(jnp.logical_not(inner))
    def _():
        columns[near] = forwarded[0]
        columns[far] = forwarded[1]


def split_kernel(place, fine, next_mean, strat_near, strat_far, detail, increment, strat, rows):
    zh = place[0]
    for column in range(4):
        for cell in range(4):
            strat[16 * zh + 4 * column + cell] = 0.5 * strat_near[column, cell]
            strat[16 * (1 - zh) + 4 * column + cell] = 0.5 * strat_far[column, cell]
    for k in range(3):
        for cell in range(4):
            slot = (4 * k + cell) % 2
            mean = block_means(rows.at[slot], [fine[k, 4 * cell + j] for j in range(4)])
            increment[4 * k + cell] = mean - next_mean[k, cell]
            for j in range(4):
                rows[2 + slot, pl.ds(j, 8, stride=4), :] = mean
            for j in range(4):
                detail[k, 4 * cell + j] = fine[k, 4 * cell + j] - rows[2 + slot]


def coarse_step(state, halves, blocks, spin, strat):
    zonal, meridional = {}, {}

    def half_zonal(x):
        x = x % 32
        if x not in zonal:
            push = state[2, (x + 1) % 32] - state[2, (x - 1) % 32]
            zonal[x] = state[0, x] + spin * state[1, x] - 0.5 * push
        return zonal[x]

    def half_meridional(x):
        b = state[2, x]
        return state[1, x] - spin * half_zonal(x) - 0.5 * (y_next(b) - y_prev(b))

    def keep(k, pair, value):
        top = value.astype(jnp.bfloat16)
        rest = (value - top.astype(jnp.float32)).astype(jnp.bfloat16)
        halves[k, pl.ds(16 * pair, 16), pl.ds(0, 128)] = top
        halves[k, pl.ds(16 * pair, 16), pl.ds(128, 128)] = rest

    for pair in range(16):
        columns = [[], [], []]
        for x in (2 * pair, 2 * pair + 1):
            u = half_zonal(x)
            v = half_meridional(x)
            flow = (half_zonal(x + 1) - half_zonal(x - 1)) + (y_next(v) - y_prev(v))
            columns[0].append(u)
            columns[1].append(v)
            columns[2].append(state[2, x] - strat[x] * flow)
        for k in range(3):
            keep(k, pair, jnp.concatenate(columns[k], axis=0))
    for k in range(3):
        wide = jnp.dot(halves[k], blocks[k], preferred_element_type=jnp.float32)
        image = (wide[:, :128] + wide[:, 128:]).reshape(32, 8, 128)
        for x in range(32):
            state[k, x] = image[x]


def table(where, increments, mine, other):
    zl = where[0]
    low = zl % 2
    beside = zl + 1 - 2 * low
    for j, run in enumerate((zl, beside, (zl + 2) % 4, (beside + 2) % 4)):
        for n in range(12):
            increments[2 * run + where[1], n] = mine[j][n]
            increments[2 * run + 1 - where[1], n] = other[j][n]


def add_block(state, increments, turn, block):
    for k in range(3):
        for cell in range(4):
            place = 4 * block + cell
            state[k, place] = state[k, place] + increments[turn, 4 * k + cell]


def clear(state):
    for k in range(3):
        for x in range(32):
            state[k, x] = jnp.zeros((8, 128), jnp.float32)


def steps(count, state, halves, blocks, spin, strat):
    def step(i, carry):
        coarse_step(state, halves, blocks, spin[...], strat)
        return carry

    lax.fori_loop(0, count, step, 0)


def plane_kernel(where, spin, blocks, strat, *refs):
    mine, other, (state, part, halves, increments) = refs[:4], refs[4:8], refs[8:]
    core, zh, y = where[1], where[3], where[4]
    table(where, increments, mine, other)
    clear(state)
    block = 4 * zh + y
    add_block(state, increments, 0, block)

    def turn(i, carry):
        coarse_step(state, halves, blocks, spin[...], strat)
        add_block(state, increments, i, block)
        return carry

    lax.fori_loop(1, 8, turn, 0)
    for k in range(3):
        part[k] = state[k, pl.ds(16 * core, 16)]


def chain_kernel(where, spin, blocks, strat, end, *refs):
    mine, other, here, there = refs[:4], refs[4:8], refs[8:11], refs[11:14]
    parts, (ends, state, halves, increments) = refs[14:18], refs[18:]
    run, core, row, zh, y = where[0], where[1], where[2], where[3], where[4]
    turns = 2 * run + core
    groups = jnp.where((row == 0) & (turns == 0), 4, row)
    table(where, increments, mine, other)
    for k in range(3):
        for x in range(32):
            ends[row, k, x] = end[k, x]
    for j in range(3):
        plane = (row + 3 - j) % 4
        for k in range(3):
            ends[plane, k, pl.ds(16 * core, 16)] = here[j][k]
            ends[plane, k, pl.ds(16 * (1 - core), 16)] = there[j][k]
    clear(state)

    def group(g, carry):
        @pl.when(g > 0)
        def _():
            steps(8, state, halves, blocks, spin, strat)

        for k in range(3):
            for x in range(32):
                state[k, x] = state[k, x] + ends[g, k, x]
        return carry

    lax.fori_loop(0, groups, group, 0)
    block = 4 * zh + y

    def turn(i, carry):
        coarse_step(state, halves, blocks, spin[...], strat)
        add_block(state, increments, i, block)
        return carry

    lax.fori_loop(0, turns, turn, 0)

    for j in range(4):
        column = y ^ j
        for half in range(2):
            side = zh if half == 0 else 1 - zh
            for k in range(3):
                for cell in range(4):
                    parts[j][half, 4 * k + cell] = state[k, 4 * (4 * side + column) + cell]


def final_kernel(kept, sent, detail, mean, out, rows):
    for k in range(3):
        for cell in range(4):
            n = 4 * k + cell
            slot = n % 2
            value = kept[n] + sent[n] + mean[k, cell]
            for j in range(4):
                rows[slot, pl.ds(j, 8, stride=4), :] = value
            for j in range(4):
                out[k, 4 * cell + j] = detail[k, 4 * cell + j] + rows[slot]


def call(kernel, outs, scratch, cost=0):
    f32 = jnp.float32

    def run(*args):
        return pl.pallas_call(
            kernel,
            out_shape=[jax.ShapeDtypeStruct(shape, f32) for shape in outs],
            in_specs=[SMEM if arg.dtype == jnp.int32 else VMEM for arg in args],
            cost_estimate=pl.CostEstimate(flops=cost, bytes_accessed=cost // 256, transcendentals=0),
            out_specs=[VMEM] * len(outs),
            scratch_shapes=[pltpu.VMEM(shape, kind) for shape, kind in scratch],
            compiler_params=PARAMS,
        )(*args)

    return run


def swapped(by):
    return [(i, i ^ by) for i in range(4)]


def per_device(slice_starts, coriolis, stratification, inverse_blocks):
    f32, bf16 = jnp.float32, jnp.bfloat16
    start = slice_starts[0]
    halves, state = ((3, 256, 256), bf16), ((3, 32, 8, 128), f32)
    increments = ((8, 12, 8, 128), f32)

    even_edges = [(s, s ^ 1) for s in range(8)]
    odd_edges = [(s, (s + 1 if s % 2 else s - 1) % 8) for s in range(8)]
    odd = lax.ppermute(start, SPACE, odd_edges)
    even = lax.ppermute(start, SPACE, even_edges)
    even_strat = lax.ppermute(stratification, SPACE, even_edges)
    odd_strat = lax.ppermute(stratification, SPACE, [(1, 2), (2, 1), (5, 6), (6, 5)])
    relayed = lax.ppermute(even_strat, SPACE, [(1, 5), (5, 1), (2, 6), (6, 2)])
    hopped_strat = lax.ppermute(relayed, SPACE, [(1, 3), (5, 7), (2, 0), (6, 4)])
    (mean,) = call(means_kernel, [(3, 4, 8, 128)], [((2, 32, 128), f32)], COST)(start)
    next_mean = lax.ppermute(mean, TM, ring(32, -1))

    spots = [lax.axis_index(name).astype(jnp.int32) for name in ("zl", "c", "x", "zh", "y")]
    where = jnp.stack(spots)
    (pair_means,) = call(strat_means_kernel, [(2, 4, 8, 128)], [((2, 32, 128), f32)])(
        even_strat, stratification
    )
    across = lax.ppermute(pair_means, "y", [(1, 2), (2, 1)])
    forwarded = lax.ppermute(across, "y", swapped(1))
    (near,) = call(columns_kernel, [(4, 4, 8, 128)], [])(
        where[3:], pair_means, across, forwarded
    )
    far = lax.ppermute(near, "zh", ring(2, 1))
    half_spin = jnp.broadcast_to(0.5 * coriolis[:, None], (32, 128))
    coarse_spin = jnp.broadcast_to(4.0 * coriolis.reshape(8, 4).mean(axis=1)[:, None], (8, 128))
    turned = jnp.swapaxes(inverse_blocks, 1, 2)
    top = lax.reduce_precision(turned, exponent_bits=8, mantissa_bits=7)
    wide = jnp.concatenate([top, turned - top], axis=2).astype(bf16)
    blocks = jnp.concatenate([wide, wide], axis=1)

    levels = ((3, 32, 32, 128), f32)
    (edges,) = call(
        even_side_kernel,
        [(STEPS, 3, 4, 32, 128)],
        [levels, levels, ((32, 32, 128), f32), ((3, 32, 128), f32)],

    )(half_spin, blocks, where[3:], stratification, even_strat, start, even)
    levels = ((3, 36, 32, 128), f32)
    (fine,) = call(
        odd_side_kernel,
        [(3, 16, 32, 128)],
        [levels, levels, ((32, 32, 128), f32), ((3, 32, 128), f32)],
        COST,
    )(half_spin, where[3:], stratification, odd_strat, hopped_strat, edges, odd)
    detail, increment, strat = call(
        split_kernel, [(3, 16, 32, 128), (12, 8, 128), (32, 8, 128)], [((4, 32, 128), f32)]
    )(where[3:], fine, next_mean, near, far)

    beside = lax.ppermute(increment, "zl", swapped(1))
    mine = [increment, beside]
    mine += [lax.ppermute(part, "zl", swapped(2)) for part in (increment, beside)]
    other = [lax.ppermute(part, "c", ring(2, 1)) for part in mine]
    detail = lax.ppermute(detail, TM, ring(32, 1))
    pair = [state[0], (3, 16, 8, 128)]
    common = (where, coarse_spin, blocks, strat)
    end, part = call(plane_kernel, pair, [halves, increments])(*common, *mine, *other)
    here = [lax.ppermute(part, "x", ring(4, by)) for by in (1, 2, 3)]
    there = [lax.ppermute(part, "c", ring(2, 1)) for part in here]
    parts = call(
        chain_kernel, [(2, 12, 8, 128)] * 4, [((4, 3, 32, 8, 128), f32), state, halves, increments]
    )(*common, end, *mine, *other, *here, *there)
    total = parts[0]
    for by in (1, 2, 3):
        total = total + lax.ppermute(parts[by], "y", swapped(by))
    sent = lax.ppermute(total[1], "zh", ring(2, 1))
    (out,) = call(final_kernel, [(3, 16, 32, 128)], [((2, 32, 128), f32)])(
        total[0], sent, detail, mean
    )
    return out[None]


def solution(mesh):
    inner = Mesh(mesh.devices.reshape(SIZES), AXES)
    in_specs = (P(TM, None, SPACE, None, None), P(), P(SPACE, None, None), P())
    out_specs = P(TM, None, SPACE, None, None)
    return jax.shard_map(
        per_device, mesh=inner, in_specs=in_specs, out_specs=out_specs, check_vma=False
    )
```

```python
import jax
import jax.numpy as jnp
from jax import lax
from jax.experimental import pallas as pl
from jax.experimental.pallas import tpu as pltpu
from jax.sharding import Mesh
from jax.sharding import PartitionSpec as P

AXES = ("x", "zl", "c", "zh", "y")
SIZES = (4, 4, 2, 2, 4)
TM = ("x", "zl", "c")
SPACE = ("zh", "y")

VMEM = pl.BlockSpec(memory_space=pltpu.VMEM)
SMEM = pl.BlockSpec(memory_space=pltpu.SMEM)
PARAMS = pltpu.CompilerParams(vmem_limit_bytes=40 * 1024 * 1024)

STEPS = 8
COST = 10**10
EVEN_UNROLL = (14, 12, 20, 16, 12, 8, 4)


def ring(size, by):
    return [(i, (i + by) % size) for i in range(size)]


def y_next(q):
    return pltpu.roll(q, q.shape[0] - 1, 0)


def y_prev(q):
    return pltpu.roll(q, 1, 0)


def fine_step(src, dst, strat, half_spin, weights, sign, first, count, unroll, place=None):
    here_weight, up_weight, down_weight = weights
    quarter = 0.25 * sign
    place = place or (lambda x: x)

    def vertical(q):
        above, below = pltpu.roll(q, 127, 1), pltpu.roll(q, 1, 1)
        return here_weight[...] * q + (up_weight[...] * above + down_weight[...] * below)

    def zonal(x):
        u = src[0, x]
        sides = src[0, x + 1] + src[0, x - 1] + (y_next(u) + y_prev(u))
        push = src[2, x + 1] - src[2, x - 1]
        return vertical(u) + (half_spin[...] * src[1, x] - quarter * push) + 0.05 * sides

    def chunk(i, carry):
        before, here = carry
        for k in range(unroll):
            x = first + unroll * i + k
            after = zonal(x + 1)
            dst[0, place(x)] = here
            v = src[1, x]
            b = src[2, x]
            b_next, b_prev = y_next(b), y_prev(b)
            v_new = (
                vertical(v)
                - (half_spin[...] * here + 0.25 * (b_next - b_prev))
                + 0.05 * (src[1, x + 1] + src[1, x - 1] + (y_next(v) + y_prev(v)))
            )
            dst[1, place(x)] = v_new
            flow = sign * (after - before) + (y_next(v_new) - y_prev(v_new))
            dst[2, place(x)] = (
                vertical(b)
                - strat[x] * flow
                + 0.05 * (src[2, x + 1] + src[2, x - 1] + (b_next + b_prev))
            )
            before, here = here, after
        return before, here

    lax.fori_loop(0, count // unroll, chunk, (zonal(first - 1), zonal(first)))


def fill_weights(weights):
    lane = lax.broadcasted_iota(jnp.int32, (32, 128), 1)
    up = jnp.where(lane < 127, 0.15, 0.0).astype(jnp.float32)
    down = jnp.where(lane > 0, 0.15, 0.0).astype(jnp.float32)
    weights[0] = 0.8 - up - down
    weights[1] = up
    weights[2] = down
    return [weights.at[n] for n in range(3)]


def turned_round(place):
    reverse = place[1] % 2

    def cell(i):
        return i * (1 - 2 * reverse) + 15 * reverse

    return cell, (1 - 2 * reverse).astype(jnp.float32)


def even_side_kernel(
    spin, blocks, place, own_strat, even_strat, start, even, edges, one, two, strat, weights
):
    del blocks
    cell, sign = turned_round(place)
    for x in range(16):
        strat[cell(x)] = 0.25 * own_strat[x]
        strat[16 + cell(x)] = 0.25 * even_strat[x]
        for k in range(3):
            one[k, cell(x)] = start[k, x]
            one[k, 16 + cell(x)] = even[k, x]
    listed = fill_weights(weights)
    bufs = (one, two)
    for level in range(STEPS):
        src = bufs[level % 2]
        for k in range(3):
            for x in range(4):
                edges[level, k, x] = src[k, 2 * level + x]
        if level < STEPS - 1:
            fine_step(
                src, bufs[(level + 1) % 2], strat, spin, listed, sign,
                2 * level + 2, 28 - 4 * level, EVEN_UNROLL[level],
            )


def odd_side_kernel(
    spin, place, own_strat, odd_strat, hopped_strat, edges, odd, out, one, two, strat, weights
):
    cell, sign = turned_round(place)
    for x in range(16):
        strat[cell(x)] = 0.25 * (odd_strat[x] + hopped_strat[x])
        strat[16 + cell(x)] = 0.25 * own_strat[x]
        for k in range(3):
            one[k, cell(x)] = odd[k, x]
    listed = fill_weights(weights)
    bufs = (one, two)
    for level in range(STEPS):
        src, dst, where = bufs[level % 2], bufs[(level + 1) % 2], None
        if level == STEPS - 1:
            dst, where = out, lambda x: cell(x - 16)
        for k in range(3):
            for x in range(4):
                src[k, 16 + 2 * level + x] = edges[level, k, x]
        fine_step(src, dst, strat, spin, listed, sign, 2 * level + 2, 16, 16, where)


def block_means(rows, cells):
    rows[...] = (cells[0] + cells[1]) + (cells[2] + cells[3])
    parts = [rows[pl.ds(j, 8, stride=4), :] for j in range(4)]
    return ((parts[0] + parts[1]) + (parts[2] + parts[3])) * 0.0625


def means_kernel(start, mean, rows):
    for k in range(3):
        for cell in range(4):
            cells = [start[k, 4 * cell + j] for j in range(4)]
            mean[k, cell] = block_means(rows.at[cell % 2], cells)


def strat_means_kernel(even, own, means, rows):
    for n, block in enumerate((own, even)):
        for cell in range(4):
            cells = [block[4 * cell + j] for j in range(4)]
            means[n, cell] = block_means(rows.at[cell % 2], cells)


def columns_kernel(place, own, across, forwarded, columns):
    y = place[1]
    beside = y + 1 - 2 * (y % 2)
    columns[y] = own[0]
    columns[beside] = own[1]
    inner = (y == 1) | (y == 2)
    near = jnp.where(y < 2, 2, 1)
    far = jnp.where(y < 2, 3, 0)

    @pl.when(inner)
    def _():
        columns[near] = across[0]
        columns[far] = across[1]

    @pl.when(jnp.logical_not(inner))
    def _():
        columns[near] = forwarded[0]
        columns[far] = forwarded[1]


def split_kernel(place, fine, next_mean, strat_near, strat_far, detail, increment, strat, rows):
    zh = place[0]
    for column in range(4):
        for cell in range(4):
            strat[16 * zh + 4 * column + cell] = 0.5 * strat_near[column, cell]
            strat[16 * (1 - zh) + 4 * column + cell] = 0.5 * strat_far[column, cell]
    for k in range(3):
        for cell in range(4):
            slot = (4 * k + cell) % 2
            mean = block_means(rows.at[slot], [fine[k, 4 * cell + j] for j in range(4)])
            increment[4 * k + cell] = mean - next_mean[k, cell]
            for j in range(4):
                rows[2 + slot, pl.ds(j, 8, stride=4), :] = mean
            for j in range(4):
                detail[k, 4 * cell + j] = fine[k, 4 * cell + j] - rows[2 + slot]


def coarse_step(state, halves, blocks, spin, strat):
    zonal, meridional = {}, {}

    def half_zonal(x):
        x = x % 32
        if x not in zonal:
            push = state[2, (x + 1) % 32] - state[2, (x - 1) % 32]
            zonal[x] = state[0, x] + spin * state[1, x] - 0.5 * push
        return zonal[x]

    def half_meridional(x):
        b = state[2, x]
        return state[1, x] - spin * half_zonal(x) - 0.5 * (y_next(b) - y_prev(b))

    def keep(k, pair, value):
        top = value.astype(jnp.bfloat16)
        rest = (value - top.astype(jnp.float32)).astype(jnp.bfloat16)
        halves[k, pl.ds(16 * pair, 16), pl.ds(0, 128)] = top
        halves[k, pl.ds(16 * pair, 16), pl.ds(128, 128)] = rest

    for pair in range(16):
        columns = [[], [], []]
        for x in (2 * pair, 2 * pair + 1):
            u = half_zonal(x)
            v = half_meridional(x)
            flow = (half_zonal(x + 1) - half_zonal(x - 1)) + (y_next(v) - y_prev(v))
            columns[0].append(u)
            columns[1].append(v)
            columns[2].append(state[2, x] - strat[x] * flow)
        for k in range(3):
            keep(k, pair, jnp.concatenate(columns[k], axis=0))
    for k in range(3):
        wide = jnp.dot(halves[k], blocks[k], preferred_element_type=jnp.float32)
        image = (wide[:, :128] + wide[:, 128:]).reshape(32, 8, 128)
        for x in range(32):
            state[k, x] = image[x]


def table(where, increments, mine, other):
    zl = where[0]
    low = zl % 2
    beside = zl + 1 - 2 * low
    for j, run in enumerate((zl, beside, (zl + 2) % 4, (beside + 2) % 4)):
        for n in range(12):
            increments[2 * run + where[1], n] = mine[j][n]
            increments[2 * run + 1 - where[1], n] = other[j][n]


def add_block(state, increments, turn, block):
    for k in range(3):
        for cell in range(4):
            place = 4 * block + cell
            state[k, place] = state[k, place] + increments[turn, 4 * k + cell]


def clear(state):
    for k in range(3):
        for x in range(32):
            state[k, x] = jnp.zeros((8, 128), jnp.float32)


def steps(count, state, halves, blocks, spin, strat):
    def step(i, carry):
        coarse_step(state, halves, blocks, spin[...], strat)
        return carry

    lax.fori_loop(0, count, step, 0)


def plane_kernel(where, spin, blocks, strat, *refs):
    mine, other, (state, part, halves, increments) = refs[:4], refs[4:8], refs[8:]
    core, zh, y = where[1], where[3], where[4]
    table(where, increments, mine, other)
    clear(state)
    block = 4 * zh + y
    add_block(state, increments, 0, block)

    def turn(i, carry):
        coarse_step(state, halves, blocks, spin[...], strat)
        add_block(state, increments, i, block)
        return carry

    lax.fori_loop(1, 8, turn, 0)
    for k in range(3):
        part[k] = state[k, pl.ds(16 * core, 16)]


def add_end(state, core, here, there):
    for k in range(3):
        for x in range(16):
            near, far = 16 * core + x, 16 * (1 - core) + x
            state[k, near] = state[k, near] + here[k, x]
            state[k, far] = state[k, far] + there[k, x]


def early_kernel(where, spin, blocks, strat, end, here, there, state, halves):
    run, core, row = where[0], where[1], where[2]
    closing = (row == 0) & (2 * run + core == 0)
    clear(state)

    @pl.when(closing)
    def _():
        for k in range(3):
            for x in range(32):
                state[k, x] = end[k, x]
        steps(8, state, halves, blocks, spin, strat)

    @pl.when(closing | (row == 3))
    def _():
        add_end(state, core, here, there)
        steps(8, state, halves, blocks, spin, strat)


def chain_kernel(where, spin, blocks, strat, early, *refs):
    mine, other, (here_two, there_two, here_one, there_one) = refs[:4], refs[4:8], refs[8:12]
    parts, (state, halves, increments) = refs[12:16], refs[16:]
    run, core, row, zh, y = where[0], where[1], where[2], where[3], where[4]
    turns = 2 * run + core
    closing = (row == 0) & (turns == 0)
    table(where, increments, mine, other)
    for k in range(3):
        for x in range(32):
            state[k, x] = early[k, x]

    @pl.when(closing | (row >= 2))
    def _():
        add_end(state, core, here_two, there_two)
        steps(8, state, halves, blocks, spin, strat)

    @pl.when(closing | (row >= 1))
    def _():
        add_end(state, core, here_one, there_one)

    block = 4 * zh + y

    def turn(i, carry):
        coarse_step(state, halves, blocks, spin[...], strat)
        add_block(state, increments, i, block)
        return carry

    lax.fori_loop(0, turns, turn, 0)

    for j in range(4):
        column = y ^ j
        for half in range(2):
            side = zh if half == 0 else 1 - zh
            for k in range(3):
                for cell in range(4):
                    parts[j][half, 4 * k + cell] = state[k, 4 * (4 * side + column) + cell]


def final_kernel(kept, sent, detail, mean, out, rows):
    for k in range(3):
        for cell in range(4):
            n = 4 * k + cell
            slot = n % 2
            value = kept[n] + sent[n] + mean[k, cell]
            for j in range(4):
                rows[slot, pl.ds(j, 8, stride=4), :] = value
            for j in range(4):
                out[k, 4 * cell + j] = detail[k, 4 * cell + j] + rows[slot]


def call(kernel, outs, scratch, cost=0):
    f32 = jnp.float32

    def run(*args):
        return pl.pallas_call(
            kernel,
            out_shape=[jax.ShapeDtypeStruct(shape, f32) for shape in outs],
            in_specs=[SMEM if arg.dtype == jnp.int32 else VMEM for arg in args],
            cost_estimate=pl.CostEstimate(flops=cost, bytes_accessed=cost // 256, transcendentals=0),
            out_specs=[VMEM] * len(outs),
            scratch_shapes=[pltpu.VMEM(shape, kind) for shape, kind in scratch],
            compiler_params=PARAMS,
        )(*args)

    return run


def swapped(by):
    return [(i, i ^ by) for i in range(4)]


def per_device(slice_starts, coriolis, stratification, inverse_blocks):
    f32, bf16 = jnp.float32, jnp.bfloat16
    start = slice_starts[0]
    halves, state = ((3, 256, 256), bf16), ((3, 32, 8, 128), f32)
    increments = ((8, 12, 8, 128), f32)

    even_edges = [(s, s ^ 1) for s in range(8)]
    odd_edges = [(s, (s + 1 if s % 2 else s - 1) % 8) for s in range(8)]
    odd = lax.ppermute(start, SPACE, odd_edges)
    even_strat = lax.ppermute(stratification, SPACE, even_edges)
    even_strat, later, strat_later = lax.optimization_barrier(
        (even_strat, start, stratification)
    )
    even = lax.ppermute(later, SPACE, even_edges)
    odd_strat = lax.ppermute(strat_later, SPACE, [(1, 2), (2, 1), (5, 6), (6, 5)])
    relayed = lax.ppermute(even_strat, SPACE, [(1, 5), (5, 1), (2, 6), (6, 2)])
    hopped_strat = lax.ppermute(relayed, SPACE, [(1, 3), (5, 7), (2, 0), (6, 4)])
    (mean,) = call(means_kernel, [(3, 4, 8, 128)], [((2, 32, 128), f32)], COST)(start)
    next_mean = lax.ppermute(mean, TM, ring(32, -1))

    spots = [lax.axis_index(name).astype(jnp.int32) for name in ("zl", "c", "x", "zh", "y")]
    where = jnp.stack(spots)
    (pair_means,) = call(strat_means_kernel, [(2, 4, 8, 128)], [((2, 32, 128), f32)])(
        even_strat, stratification
    )
    across = lax.ppermute(pair_means, "y", [(1, 2), (2, 1)])
    forwarded = lax.ppermute(across, "y", swapped(1))
    (near,) = call(columns_kernel, [(4, 4, 8, 128)], [])(
        where[3:], pair_means, across, forwarded
    )
    far = lax.ppermute(near, "zh", ring(2, 1))
    half_spin = jnp.broadcast_to(0.5 * coriolis[:, None], (32, 128))
    coarse_spin = jnp.broadcast_to(4.0 * coriolis.reshape(8, 4).mean(axis=1)[:, None], (8, 128))
    turned = jnp.swapaxes(inverse_blocks, 1, 2)
    top = lax.reduce_precision(turned, exponent_bits=8, mantissa_bits=7)
    wide = jnp.concatenate([top, turned - top], axis=2).astype(bf16)
    blocks = jnp.concatenate([wide, wide], axis=1)

    levels = ((3, 32, 32, 128), f32)
    (edges,) = call(
        even_side_kernel,
        [(STEPS, 3, 4, 32, 128)],
        [levels, levels, ((32, 32, 128), f32), ((3, 32, 128), f32)],
    )(half_spin, blocks, where[3:], stratification, even_strat, start, even)
    levels = ((3, 36, 32, 128), f32)
    (fine,) = call(
        odd_side_kernel,
        [(3, 16, 32, 128)],
        [levels, levels, ((32, 32, 128), f32), ((3, 32, 128), f32)],
        COST,
    )(half_spin, where[3:], stratification, odd_strat, hopped_strat, edges, odd)
    detail, increment, strat = call(
        split_kernel, [(3, 16, 32, 128), (12, 8, 128), (32, 8, 128)], [((4, 32, 128), f32)]
    )(where[3:], fine, next_mean, near, far)

    beside = lax.ppermute(increment, "zl", swapped(1))
    mine = [increment, beside]
    mine += [lax.ppermute(part, "zl", swapped(2)) for part in (increment, beside)]
    other = [lax.ppermute(part, "c", ring(2, 1)) for part in mine]
    detail = lax.ppermute(detail, TM, ring(32, 1))
    pair = [state[0], (3, 16, 8, 128)]
    common = (where, coarse_spin, blocks, strat)
    end, part = call(plane_kernel, pair, [halves, increments])(*common, *mine, *other)
    here = [lax.ppermute(part, "x", ring(4, by)) for by in (3, 2, 1)]
    there = [lax.ppermute(here[0], "c", ring(2, 1))]
    there[0], here[1], here[2] = lax.optimization_barrier((there[0], here[1], here[2]))
    (early,) = call(early_kernel, [state[0]], [halves])(*common, end, here[0], there[0])
    there += [lax.ppermute(part, "c", ring(2, 1)) for part in here[1:]]
    parts = call(chain_kernel, [(2, 12, 8, 128)] * 4, [state, halves, increments])(
        *common, early, *mine, *other, here[1], there[1], here[2], there[2]
    )
    total = parts[0]
    for by in (1, 2, 3):
        total = total + lax.ppermute(parts[by], "y", swapped(by))
    sent = lax.ppermute(total[1], "zh", ring(2, 1))
    (out,) = call(final_kernel, [(3, 16, 32, 128)], [((2, 32, 128), f32)])(
        total[0], sent, detail, mean
    )
    return out[None]


def solution(mesh):
    inner = Mesh(mesh.devices.reshape(SIZES), AXES)
    in_specs = (P(TM, None, SPACE, None, None), P(), P(SPACE, None, None), P())
    out_specs = P(TM, None, SPACE, None, None)
    return jax.shard_map(
        per_device, mesh=inner, in_specs=in_specs, out_specs=out_specs, check_vma=False
    )
```

```python
import jax
import jax.numpy as jnp
from jax import lax
from jax.experimental import pallas as pl
from jax.experimental.pallas import tpu as pltpu
from jax.sharding import Mesh
from jax.sharding import PartitionSpec as P

AXES = ("x", "zl", "c", "zh", "y")
SIZES = (4, 4, 2, 2, 4)
TM = ("x", "zl", "c")
SPACE = ("zh", "y")

VMEM = pl.BlockSpec(memory_space=pltpu.VMEM)
SMEM = pl.BlockSpec(memory_space=pltpu.SMEM)
PARAMS = pltpu.CompilerParams(vmem_limit_bytes=40 * 1024 * 1024)

STEPS = 8
COST = 10**10
EVEN_UNROLL = (14, 12, 20, 16, 12, 8, 4)


def ring(size, by):
    return [(i, (i + by) % size) for i in range(size)]


def y_next(q):
    return pltpu.roll(q, q.shape[0] - 1, 0)


def y_prev(q):
    return pltpu.roll(q, 1, 0)


def fine_step(src, dst, strat, half_spin, weights, sign, first, count, unroll, place=None):
    here_weight, up_weight, down_weight = weights
    quarter = 0.25 * sign
    place = place or (lambda x: x)

    def vertical(q):
        above, below = pltpu.roll(q, 127, 1), pltpu.roll(q, 1, 1)
        return here_weight[...] * q + (up_weight[...] * above + down_weight[...] * below)

    def zonal(x):
        u = src[0, x]
        sides = src[0, x + 1] + src[0, x - 1] + (y_next(u) + y_prev(u))
        push = src[2, x + 1] - src[2, x - 1]
        return vertical(u) + (half_spin[...] * src[1, x] - quarter * push) + 0.05 * sides

    def chunk(i, carry):
        before, here = carry
        for k in range(unroll):
            x = first + unroll * i + k
            after = zonal(x + 1)
            dst[0, place(x)] = here
            v = src[1, x]
            b = src[2, x]
            b_next, b_prev = y_next(b), y_prev(b)
            v_new = (
                vertical(v)
                - (half_spin[...] * here + 0.25 * (b_next - b_prev))
                + 0.05 * (src[1, x + 1] + src[1, x - 1] + (y_next(v) + y_prev(v)))
            )
            dst[1, place(x)] = v_new
            flow = sign * (after - before) + (y_next(v_new) - y_prev(v_new))
            dst[2, place(x)] = (
                vertical(b)
                - strat[x] * flow
                + 0.05 * (src[2, x + 1] + src[2, x - 1] + (b_next + b_prev))
            )
            before, here = here, after
        return before, here

    lax.fori_loop(0, count // unroll, chunk, (zonal(first - 1), zonal(first)))


def fill_weights(weights):
    lane = lax.broadcasted_iota(jnp.int32, (32, 128), 1)
    up = jnp.where(lane < 127, 0.15, 0.0).astype(jnp.float32)
    down = jnp.where(lane > 0, 0.15, 0.0).astype(jnp.float32)
    weights[0] = 0.8 - up - down
    weights[1] = up
    weights[2] = down
    return [weights.at[n] for n in range(3)]


def turned_round(place):
    reverse = place[1] % 2

    def cell(i):
        return i * (1 - 2 * reverse) + 15 * reverse

    return cell, (1 - 2 * reverse).astype(jnp.float32)


def even_side_kernel(
    spin, blocks, place, own_strat, even_strat, start, even, edges, one, two, strat, weights
):
    del blocks
    cell, sign = turned_round(place)
    for x in range(16):
        strat[cell(x)] = 0.25 * own_strat[x]
        strat[16 + cell(x)] = 0.25 * even_strat[x]
        for k in range(3):
            one[k, cell(x)] = start[k, x]
            one[k, 16 + cell(x)] = even[k, x]
    listed = fill_weights(weights)
    bufs = (one, two)
    for level in range(STEPS):
        src = bufs[level % 2]
        for k in range(3):
            for x in range(4):
                edges[level, k, x] = src[k, 2 * level + x]
        if level < STEPS - 1:
            fine_step(
                src, bufs[(level + 1) % 2], strat, spin, listed, sign,
                2 * level + 2, 28 - 4 * level, EVEN_UNROLL[level],
            )


def odd_side_kernel(
    spin, place, own_strat, odd_strat, hopped_strat, edges, odd, out, one, two, strat, weights
):
    cell, sign = turned_round(place)
    for x in range(16):
        strat[cell(x)] = 0.25 * (odd_strat[x] + hopped_strat[x])
        strat[16 + cell(x)] = 0.25 * own_strat[x]
        for k in range(3):
            one[k, cell(x)] = odd[k, x]
    listed = fill_weights(weights)
    bufs = (one, two)
    for level in range(STEPS):
        src, dst, where = bufs[level % 2], bufs[(level + 1) % 2], None
        if level == STEPS - 1:
            dst, where = out, lambda x: cell(x - 16)
        for k in range(3):
            for x in range(4):
                src[k, 16 + 2 * level + x] = edges[level, k, x]
        fine_step(src, dst, strat, spin, listed, sign, 2 * level + 2, 16, 16, where)


def block_means(rows, cells):
    rows[...] = (cells[0] + cells[1]) + (cells[2] + cells[3])
    parts = [rows[pl.ds(j, 8, stride=4), :] for j in range(4)]
    return ((parts[0] + parts[1]) + (parts[2] + parts[3])) * 0.0625


def means_kernel(start, mean, rows):
    for k in range(3):
        for cell in range(4):
            cells = [start[k, 4 * cell + j] for j in range(4)]
            mean[k, cell] = block_means(rows.at[cell % 2], cells)


def strat_means_kernel(even, own, means, rows):
    for n, block in enumerate((own, even)):
        for cell in range(4):
            cells = [block[4 * cell + j] for j in range(4)]
            means[n, cell] = block_means(rows.at[cell % 2], cells)


def columns_kernel(place, own, relayed, across, forwarded, columns, far_columns):
    y = place[1]
    beside = y + 1 - 2 * (y % 2)
    columns[y] = own[0]
    columns[beside] = own[1]
    inner = (y == 1) | (y == 2)
    near = jnp.where(y < 2, 2, 1)
    far = jnp.where(y < 2, 3, 0)

    @pl.when(inner)
    def _():
        columns[near] = across[0]
        columns[far] = across[1]
        far_columns[near] = across[2]
        far_columns[far] = across[3]
        far_columns[y] = relayed[0]
        far_columns[beside] = relayed[1]

    @pl.when(jnp.logical_not(inner))
    def _():
        columns[near] = forwarded[0]
        columns[far] = forwarded[1]
        far_columns[near] = forwarded[2]
        far_columns[far] = forwarded[3]
        far_columns[beside] = forwarded[4]
        far_columns[y] = forwarded[5]


def split_kernel(place, fine, next_mean, strat_near, strat_far, detail, increment, strat, rows):
    zh = place[0]
    for column in range(4):
        for cell in range(4):
            strat[16 * zh + 4 * column + cell] = 0.5 * strat_near[column, cell]
            strat[16 * (1 - zh) + 4 * column + cell] = 0.5 * strat_far[column, cell]
    for k in range(3):
        for cell in range(4):
            slot = (4 * k + cell) % 2
            mean = block_means(rows.at[slot], [fine[k, 4 * cell + j] for j in range(4)])
            increment[4 * k + cell] = mean - next_mean[k, cell]
            for j in range(4):
                rows[2 + slot, pl.ds(j, 8, stride=4), :] = mean
            for j in range(4):
                detail[k, 4 * cell + j] = fine[k, 4 * cell + j] - rows[2 + slot]


def coarse_step(state, halves, blocks, spin, strat):
    zonal, meridional = {}, {}

    def half_zonal(x):
        x = x % 32
        if x not in zonal:
            push = state[2, (x + 1) % 32] - state[2, (x - 1) % 32]
            zonal[x] = state[0, x] + spin * state[1, x] - 0.5 * push
        return zonal[x]

    def half_meridional(x):
        b = state[2, x]
        return state[1, x] - spin * half_zonal(x) - 0.5 * (y_next(b) - y_prev(b))

    def keep(k, pair, value):
        top = value.astype(jnp.bfloat16)
        rest = (value - top.astype(jnp.float32)).astype(jnp.bfloat16)
        halves[k, pl.ds(16 * pair, 16), pl.ds(0, 128)] = top
        halves[k, pl.ds(16 * pair, 16), pl.ds(128, 128)] = rest

    for pair in range(16):
        columns = [[], [], []]
        for x in (2 * pair, 2 * pair + 1):
            u = half_zonal(x)
            v = half_meridional(x)
            flow = (half_zonal(x + 1) - half_zonal(x - 1)) + (y_next(v) - y_prev(v))
            columns[0].append(u)
            columns[1].append(v)
            columns[2].append(state[2, x] - strat[x] * flow)
        for k in range(3):
            keep(k, pair, jnp.concatenate(columns[k], axis=0))
    for k in range(3):
        wide = jnp.dot(halves[k], blocks[k], preferred_element_type=jnp.float32)
        image = (wide[:, :128] + wide[:, 128:]).reshape(32, 8, 128)
        for x in range(32):
            state[k, x] = image[x]


def table(where, increments, mine, other):
    zl = where[0]
    low = zl % 2
    beside = zl + 1 - 2 * low
    for j, run in enumerate((zl, beside, (zl + 2) % 4, (beside + 2) % 4)):
        for n in range(12):
            increments[2 * run + where[1], n] = mine[j][n]
            increments[2 * run + 1 - where[1], n] = other[j][n]


def add_block(state, increments, turn, block):
    for k in range(3):
        for cell in range(4):
            place = 4 * block + cell
            state[k, place] = state[k, place] + increments[turn, 4 * k + cell]


def clear(state):
    for k in range(3):
        for x in range(32):
            state[k, x] = jnp.zeros((8, 128), jnp.float32)


def steps(count, state, halves, blocks, spin, strat):
    def step(i, carry):
        coarse_step(state, halves, blocks, spin[...], strat)
        return carry

    lax.fori_loop(0, count, step, 0)


def plane_kernel(where, spin, blocks, strat, *refs):
    mine, other, (state, part, halves, increments) = refs[:4], refs[4:8], refs[8:]
    core, zh, y = where[1], where[3], where[4]
    table(where, increments, mine, other)
    clear(state)
    block = 4 * zh + y
    add_block(state, increments, 0, block)

    def turn(i, carry):
        coarse_step(state, halves, blocks, spin[...], strat)
        add_block(state, increments, i, block)
        return carry

    lax.fori_loop(1, 8, turn, 0)
    for k in range(3):
        part[k] = state[k, pl.ds(16 * core, 16)]


def chain_kernel(where, spin, blocks, strat, end, *refs):
    mine, other, here, there = refs[:4], refs[4:8], refs[8:11], refs[11:14]
    parts, (ends, state, halves, increments) = refs[14:18], refs[18:]
    run, core, row, zh, y = where[0], where[1], where[2], where[3], where[4]
    turns = 2 * run + core
    groups = jnp.where((row == 0) & (turns == 0), 4, row)
    table(where, increments, mine, other)
    for k in range(3):
        for x in range(32):
            ends[row, k, x] = end[k, x]
    for j in range(3):
        plane = (row + 3 - j) % 4
        for k in range(3):
            ends[plane, k, pl.ds(16 * core, 16)] = here[j][k]
            ends[plane, k, pl.ds(16 * (1 - core), 16)] = there[j][k]
    clear(state)

    def group(g, carry):
        @pl.when(g > 0)
        def _():
            steps(8, state, halves, blocks, spin, strat)

        for k in range(3):
            for x in range(32):
                state[k, x] = state[k, x] + ends[g, k, x]
        return carry

    lax.fori_loop(0, groups, group, 0)
    block = 4 * zh + y

    def turn(i, carry):
        coarse_step(state, halves, blocks, spin[...], strat)
        add_block(state, increments, i, block)
        return carry

    lax.fori_loop(0, turns, turn, 0)

    for j in range(4):
        column = y ^ j
        for half in range(2):
            side = zh if half == 0 else 1 - zh
            for k in range(3):
                for cell in range(4):
                    parts[j][half, 4 * k + cell] = state[k, 4 * (4 * side + column) + cell]


def final_kernel(kept, sent, detail, mean, out, rows):
    for k in range(3):
        for cell in range(4):
            n = 4 * k + cell
            slot = n % 2
            value = kept[n] + sent[n] + mean[k, cell]
            for j in range(4):
                rows[slot, pl.ds(j, 8, stride=4), :] = value
            for j in range(4):
                out[k, 4 * cell + j] = detail[k, 4 * cell + j] + rows[slot]


def call(kernel, outs, scratch, cost=0):
    f32 = jnp.float32

    def run(*args):
        return pl.pallas_call(
            kernel,
            out_shape=[jax.ShapeDtypeStruct(shape, f32) for shape in outs],
            in_specs=[SMEM if arg.dtype == jnp.int32 else VMEM for arg in args],
            cost_estimate=pl.CostEstimate(flops=cost, bytes_accessed=cost // 256, transcendentals=0),
            out_specs=[VMEM] * len(outs),
            scratch_shapes=[pltpu.VMEM(shape, kind) for shape, kind in scratch],
            compiler_params=PARAMS,
        )(*args)

    return run


def swapped(by):
    return [(i, i ^ by) for i in range(4)]


def per_device(slice_starts, coriolis, stratification, inverse_blocks):
    f32, bf16 = jnp.float32, jnp.bfloat16
    start = slice_starts[0]
    halves, state = ((3, 256, 256), bf16), ((3, 32, 8, 128), f32)
    increments = ((8, 12, 8, 128), f32)

    even_edges = [(s, s ^ 1) for s in range(8)]
    odd_edges = [(s, (s + 1 if s % 2 else s - 1) % 8) for s in range(8)]
    odd = lax.ppermute(start, SPACE, odd_edges)
    even = lax.ppermute(start, SPACE, even_edges)
    even_strat = lax.ppermute(stratification, SPACE, even_edges)
    odd_strat = lax.ppermute(stratification, SPACE, [(1, 2), (2, 1), (5, 6), (6, 5)])
    (pair_means,) = call(strat_means_kernel, [(2, 4, 8, 128)], [((2, 32, 128), f32)])(
        even_strat, stratification
    )
    load = jnp.concatenate([even_strat, pair_means.reshape(2, 32, 128)])
    relayed = lax.ppermute(load, SPACE, [(1, 5), (5, 1), (2, 6), (6, 2)])
    hopped_strat = lax.ppermute(relayed[:16], SPACE, [(1, 3), (5, 7), (2, 0), (6, 4)])
    (mean,) = call(means_kernel, [(3, 4, 8, 128)], [((2, 32, 128), f32)])(start)
    next_mean = lax.ppermute(mean, TM, ring(32, -1))

    spots = [lax.axis_index(name).astype(jnp.int32) for name in ("zl", "c", "x", "zh", "y")]
    where = jnp.stack(spots)
    relayed_means = relayed[16:].reshape(2, 4, 8, 128)
    across = lax.ppermute(
        jnp.concatenate([pair_means, relayed_means]), "y", [(1, 2), (2, 1)]
    )
    forwarded = lax.ppermute(jnp.concatenate([across, relayed_means]), "y", swapped(1))
    near, far = call(columns_kernel, [(4, 4, 8, 128)] * 2, [])(
        where[3:], pair_means, relayed_means, across, forwarded
    )
    half_spin = jnp.broadcast_to(0.5 * coriolis[:, None], (32, 128))
    coarse_spin = jnp.broadcast_to(4.0 * coriolis.reshape(8, 4).mean(axis=1)[:, None], (8, 128))
    turned = jnp.swapaxes(inverse_blocks, 1, 2)
    top = lax.reduce_precision(turned, exponent_bits=8, mantissa_bits=7)
    wide = jnp.concatenate([top, turned - top], axis=2).astype(bf16)
    blocks = jnp.concatenate([wide, wide], axis=1)

    levels = ((3, 32, 32, 128), f32)
    (edges,) = call(
        even_side_kernel,
        [(STEPS, 3, 4, 32, 128)],
        [levels, levels, ((32, 32, 128), f32), ((3, 32, 128), f32)],

    )(half_spin, blocks, where[3:], stratification, even_strat, start, even)
    levels = ((3, 36, 32, 128), f32)
    (fine,) = call(
        odd_side_kernel,
        [(3, 16, 32, 128)],
        [levels, levels, ((32, 32, 128), f32), ((3, 32, 128), f32)],
        COST,
    )(half_spin, where[3:], stratification, odd_strat, hopped_strat, edges, odd)
    detail, increment, strat = call(
        split_kernel, [(3, 16, 32, 128), (12, 8, 128), (32, 8, 128)], [((4, 32, 128), f32)]
    )(where[3:], fine, next_mean, near, far)

    beside = lax.ppermute(increment, "zl", swapped(1))
    mine = [increment, beside]
    mine += [lax.ppermute(part, "zl", swapped(2)) for part in (increment, beside)]
    other = [lax.ppermute(part, "c", ring(2, 1)) for part in mine]
    detail = lax.ppermute(detail, TM, ring(32, 1))
    pair = [state[0], (3, 16, 8, 128)]
    common = (where, coarse_spin, blocks, strat)
    end, part = call(plane_kernel, pair, [halves, increments])(*common, *mine, *other)
    here = [lax.ppermute(part, "x", ring(4, by)) for by in (1, 2, 3)]
    there = [lax.ppermute(part, "c", ring(2, 1)) for part in here]
    parts = call(
        chain_kernel, [(2, 12, 8, 128)] * 4, [((4, 3, 32, 8, 128), f32), state, halves, increments]
    )(*common, end, *mine, *other, *here, *there)
    total = parts[0]
    for by in (1, 2, 3):
        total = total + lax.ppermute(parts[by], "y", swapped(by))
    sent = lax.ppermute(total[1], "zh", ring(2, 1))
    (out,) = call(final_kernel, [(3, 16, 32, 128)], [((2, 32, 128), f32)])(
        total[0], sent, detail, mean
    )
    return out[None]


def solution(mesh):
    inner = Mesh(mesh.devices.reshape(SIZES), AXES)
    in_specs = (P(TM, None, SPACE, None, None), P(), P(SPACE, None, None), P())
    out_specs = P(TM, None, SPACE, None, None)
    return jax.shard_map(
        per_device, mesh=inner, in_specs=in_specs, out_specs=out_specs, check_vma=False
    )
```
